128 devices in a mesh: gx: 8 (over z, core), gy: 16 (over y, x).
Axes of the slice: x: 4, y: 4, z: 4, core: 2. Of those that a mesh axis runs over, the one named last changes fastest.
Arguments:
- fields: bfloat16 [2, 16, 128, 2048], P(None, None, 'gx', 'gy'), may hold values from -6 to 6
- phase: int32 [128, 2048], P('gx', 'gy'), may hold values 0 or 1
- electrode: int32 [2, 128, 2048], P(None, 'gx', 'gy'), may hold values 0 or 1
- planes: float32 [2, 2, 16, 32, 2048], P(None, None, None, 'gx', 'gy'), may hold values from -6 to 6
Outputs:
- new_fields: float32 [2, 16, 128, 2048], P(None, None, 'gx', 'gy')
- new_planes: float32 [2, 2, 16, 32, 2048], P(None, None, None, 'gx', 'gy')
The draws below stay inside these ranges and needn't reach their ends.
All inputs are finite; a program needn't handle non-finite values. No bound on the sum of `phase` or of `electrode` on one device may be relied on, other than what follows from the above.
Results may differ from the reference program's by a relative error of at most 0.00035.
Values sent between devices are 32-bit elements; how exact they have to be, the bound alone decides.
A program may use at most 64 MiB of HBM per device.

```python
import jax
import jax.numpy as jnp
from jax import lax

Z = 16
CX = 16
STEPS = 2
NX = 128
NY = 2048
N_GX = 8


def set_ends(values, stream_key, low, high):
    index_at = [jax.random.randint(jax.random.fold_in(stream_key, axis), (), 0, length) for axis, length in enumerate(values.shape)]
    widest = values.shape.index(max(values.shape))
    next_to = index_at[:widest] + [(index_at[widest] + 1) % values.shape[widest]] + index_at[widest + 1:]
    return values.at[tuple(index_at)].set(low).at[tuple(next_to)].set(high)


def block_scale(key, shape, shards, least, top_value):
    def one(dim, shards_of):
        steps = jax.random.uniform(jax.random.fold_in(jax.random.fold_in(key, 6), dim), (shards_of,), jnp.float32, least / len(shards), top_value / len(shards))
        return jnp.repeat(jnp.exp(steps), shape[dim] // shards_of).reshape((-1,) + (1,) * (len(shape) - dim - 1))

    gain = one(*shards[0])
    for cut in shards[1:]:
        gain = gain * one(*cut)
    return gain


def bell_draw(key, extent, scale, most, pieces=(), held_as=jnp.bfloat16):
    factor_of = block_scale(key, extent, pieces, -0.22, 0.18) if pieces else 1.0
    values = jax.random.normal(key, extent, jnp.float32) * scale * factor_of
    return jnp.minimum(jnp.maximum(values, -most), most).astype(held_as)


def setup_inputs(seed: int = 0) -> dict:
    keys = jax.random.split(jax.random.key(seed), 5)
    fields = bell_draw(keys[0], (2, Z, NX, NY), 1.0, 6.0, ((2, 8), (3, 16)))
    phase = set_ends((jax.random.randint(keys[1], (NX, NY), 0, 2) < 1).astype(jnp.int32), jax.random.fold_in(keys[1], 1), 0, 1)
    electrode = set_ends((jax.random.randint(keys[2], (STEPS, NX, NY), 0, 3) < 1).astype(jnp.int32), jax.random.fold_in(keys[2], 1), 0, 1)
    planes = bell_draw(keys[3], (STEPS, 2, Z, 4 * N_GX, NY), 1.0, 6.0, ((3, 8), (4, 16)), jnp.float32)
    return dict(fields=fields, phase=phase, electrode=electrode, planes=planes)


cond_oil = 0.6
cond_drop = 2.0
diff_oil = 0.3
diff_drop = 1.0
thermal_slope = 0.3
joule_rate = 0.5
time_step = 2.0
robin_weight = 2.0
extrap_half = 0.5
cheb_centre = 1.0
cheb_radius = 0.95
cheb_ratio = cheb_centre / cheb_radius
rho_first = 1.0 / cheb_ratio
rho_second = 1.0 / (2.0 * cheb_ratio - rho_first)


def shift_pad(values, axis, before, after):
    widths = [(0, 0)] * values.ndim
    widths[axis] = (before, after)
    return jnp.pad(values, widths)


def couple(padded, conduct, faces):
    centre = padded[..., 1:-1]
    middle = conduct[..., 1:-1]
    vertical = 0.5 * (middle[:, 1:] + middle[:, :-1])
    vert_flux = vertical * (centre[:, 1:] - centre[:, :-1])
    leakage = shift_pad(-vert_flux, 1, 0, 1) + shift_pad(vert_flux, 1, 1, 0)
    spread = shift_pad(vertical, 1, 0, 1) + shift_pad(vertical, 1, 1, 0)
    along = 0.5 * (middle[:, :, 1:] + middle[:, :, :-1])
    along_flux = along * (centre[:, :, 1:] - centre[:, :, :-1])
    leakage = leakage + shift_pad(-along_flux, 2, 0, 1) + shift_pad(along_flux, 2, 1, 0)
    spread = spread + shift_pad(along, 2, 0, 1) + shift_pad(along, 2, 1, 0)
    across = 0.5 * (conduct[..., 1:] + conduct[..., :-1]) * faces
    across_flux = across * (padded[..., 1:] - padded[..., :-1])
    leakage = leakage - across_flux[..., 1:] + across_flux[..., :-1]
    spread = spread + across[..., 1:] + across[..., :-1]
    return leakage, spread


def coefficients(temper, droplet):
    heat = jnp.broadcast_to(cond_oil + (cond_drop - cond_oil) * droplet, temper.shape)
    ions = (diff_oil + (diff_drop - diff_oil) * droplet) * jnp.exp(thermal_slope * temper)
    return jnp.stack([heat, ions], axis=0)


def window(block, droplet, active_all, left_all, right_all, faces, edge, is_first, is_last, depth_decay):
    state = block
    droplet_pad = jnp.pad(droplet, ((0, 0), (1, 1)))
    outputs = []
    for step in range(STEPS):
        padded = jnp.pad(state, ((0, 0), (0, 0), (0, 0), (1, 1)))
        conduct = coefficients(padded[0], droplet_pad)
        centre = state
        robin = robin_weight * conduct[..., 1:-1] * edge
        leakage, spread = couple(padded, conduct, faces)
        diagonal = 1.0 + time_step * (spread + robin)
        heat_src = joule_rate * active_all[step] * droplet * (1.0 + 0.5 * centre[1] * centre[1]) * depth_decay
        source = jnp.stack([heat_src, jnp.zeros_like(heat_src)], axis=0)
        trace = left_all[step][:, :, None, :] * is_first + right_all[step][:, :, None, :] * is_last
        target = centre + time_step * (source + robin * trace)
        residual = target - (centre + time_step * (leakage + robin * centre))
        move = residual / diagonal / cheb_centre
        first = centre + move
        padded_first = jnp.pad(first, ((0, 0), (0, 0), (0, 0), (1, 1)))
        leak_first, spread_unused = couple(padded_first, conduct, faces)
        residual_first = target - (first + time_step * (leak_first + robin * first))
        state = first + rho_second * rho_first * move + (2.0 * rho_second / cheb_radius) * residual_first / diagonal
        outputs.append(jnp.stack([state[:, :, 0], state[:, :, 1], state[:, :, -2], state[:, :, -1]], axis=2))
    return state, jnp.stack(outputs, axis=0)


def reference(fields, phase, electrode, planes):
    rims = planes.reshape(STEPS, 2, Z, N_GX, 4, NY)
    from_left = rims[:, :, :, :, 3] + extrap_half * (rims[:, :, :, :, 3] - rims[:, :, :, :, 2])
    from_right = rims[:, :, :, :, 0] + extrap_half * (rims[:, :, :, :, 0] - rims[:, :, :, :, 1])
    blank = jnp.zeros_like(from_left[:, :, :, :1])
    left_in = jnp.concatenate([blank, from_left[:, :, :, :-1]], axis=3)
    right_in = jnp.concatenate([from_right[:, :, :, 1:], blank], axis=3)
    face_index = jnp.arange(NY + 1, dtype=jnp.int32)
    faces = ((face_index >= 1) & (face_index <= NY - 1)).astype(jnp.float32)
    plane_index = jnp.arange(CX, dtype=jnp.int32)[:, None]
    is_first = (plane_index == 0).astype(jnp.float32)
    is_last = (plane_index == CX - 1).astype(jnp.float32)
    edge = is_first + is_last
    depth_decay = jnp.exp(-4.0 * jnp.arange(Z, dtype=jnp.float32) / Z)[:, None, None]

    def visit(index, carry):
        out_fields, out_planes = carry
        begin = (index * CX).astype(jnp.int32)
        block = lax.dynamic_slice_in_dim(fields, begin, CX, 2).astype(jnp.float32)
        droplet = lax.dynamic_slice_in_dim(phase, begin, CX, 0).astype(jnp.float32)
        active_all = lax.dynamic_slice_in_dim(electrode, begin, CX, 1).astype(jnp.float32)
        left_all = lax.dynamic_index_in_dim(left_in, index, 3, keepdims=False)
        right_all = lax.dynamic_index_in_dim(right_in, index, 3, keepdims=False)
        state, fresh = window(block, droplet, active_all, left_all, right_all, faces, edge, is_first, is_last, depth_decay)
        out_fields = lax.dynamic_update_slice_in_dim(out_fields, state, begin, 2)
        out_planes = lax.dynamic_update_slice_in_dim(out_planes, fresh, (index * 4).astype(jnp.int32), 3)
        return out_fields, out_planes

    start_fields = jnp.zeros((2, Z, NX, NY), jnp.float32)
    start_planes = jnp.zeros((STEPS, 2, Z, 4 * N_GX, NY), jnp.float32)
    new_fields, new_planes = lax.fori_loop(0, N_GX, visit, (start_fields, start_planes))
    return (new_fields, new_planes)
```

```python
import functools

import jax
import jax.numpy as jnp
from jax import lax
from jax.experimental import pallas as pl
from jax.experimental.pallas import tpu as pltpu
from jax.sharding import PartitionSpec as P

MESH = pl.DeviceIdType.MESH
cond_oil = 0.6
cond_drop = 2.0
diff_oil = 0.3
diff_drop = 1.0
thermal_slope = 0.3
cheb_radius = 0.95
cheb_ratio = 1.0 / cheb_radius
rho_first = 1.0 / cheb_ratio
rho_second = 1.0 / (2.0 * cheb_ratio - rho_first)
keep_old = rho_second * rho_first
take_new = 2.0 * rho_second / cheb_radius

Z = 16
X = 16
C = 128
CORNERS = ((-1, -1), (-1, 1), (1, -1), (1, 1))
SIDES_Y = ((0, -1), (0, 1))
SIDES_X = ((-1, 0), (1, 0))
ALL = CORNERS + SIDES_Y + SIDES_X


def lanes(shape):
    return lax.broadcasted_iota(jnp.int32, shape, len(shape) - 1)


def roll_last(v, shift):
    return pltpu.roll(v, shift % C, v.ndim - 1)


def roll_rows(v, shift):
    return pltpu.roll(v, shift % X, v.ndim - 2)


def row_masks(ndim):
    shape = (1,) * (ndim - 2) + (X, C)
    rows = lax.broadcasted_iota(jnp.int32, shape, ndim - 2)
    return rows


def packed_columns(v):
    head = v.shape[:-3]
    v = v.reshape(head + (2, 8, X, C))
    lane = lanes(head + (2, X, C))
    out = None
    for j in range(8):
        moved = roll_last(v[..., j, :, :], 16 * j + 8)
        out = moved if out is None else jnp.where(lane >= 16 * j, moved, out)
    return out


def packed_map(v):
    base = jnp.where(lanes(v.shape) < 16, roll_last(v, 8), 0.0)
    base = base + roll_last(base, 16)
    base = base + roll_last(base, 32)
    return base + roll_last(base, 64)


def steps_of(droplet, active, old_t, old_n, trace, decay, shifts, masks):
    xp, xm, yp, ym, zp, zm = shifts
    mxp, mxm, myp, mym, mzp, mzm, edge4 = masks

    def coefficients(k):
        faces = (
            (k + xp(k)) * mxp,
            (k + xm(k)) * mxm,
            (k + yp(k)) * myp,
            (k + ym(k)) * mym,
            (k + zp(k)) * mzp,
            (k + zm(k)) * mzm,
        )
        robin = k * edge4
        diagonal = 1.0 + robin + sum(faces[1:], faces[0])
        return faces, robin, 1.0 / diagonal

    def sweep(v, target, faces):
        total = target
        for face, move in zip(faces, shifts):
            total = total + face * move(v)
        return total

    heat = jnp.broadcast_to(cond_oil + (cond_drop - cond_oil) * droplet, old_t.shape)
    ion_base = diff_oil + (diff_drop - diff_oil) * droplet
    heat_faces, heat_robin, heat_inv = coefficients(heat)
    states = []
    for step in range(2):
        ions = ion_base * jnp.exp(thermal_slope * old_t)
        source = (active[step] * droplet) * decay * (1.0 + 0.5 * old_n * old_n)
        target_t = old_t + source + heat_robin * trace(step, 0)
        first = sweep(old_t, target_t, heat_faces) * heat_inv
        new_t = sweep(first, target_t, heat_faces) * (take_new * heat_inv) - keep_old * old_t
        ion_faces, ion_robin, ion_inv = coefficients(ions)
        target_n = old_n + ion_robin * trace(step, 1)
        first = sweep(old_n, target_n, ion_faces) * ion_inv
        new_n = sweep(first, target_n, ion_faces) * (take_new * ion_inv) - keep_old * old_n
        old_t, old_n = new_t, new_n
        states.append((old_t, old_n))
    return states


def kernel(
    n_gx,
    n_gy,
    f_hbm,
    ph_hbm,
    el_hbm,
    pl_hbm,
    of_ref,
    op_ref,
    f_in,
    ph_in,
    el_in,
    pl_in,
    send_b,
    send_g,
    recv_b,
    recv_g,
    recv_c,
    in_sem,
    send_sem,
    recv_sem,
):
    gx = lax.axis_index("gx")
    gy = lax.axis_index("gy")

    def exists(offset):
        found = []
        for place, move, count in ((gx, offset[0], n_gx), (gy, offset[1], n_gy)):
            if move < 0:
                found.append(place > 0)
            if move > 0:
                found.append(place < count - 1)
        return functools.reduce(jnp.logical_and, found)

    def at(offset):
        return (gx + offset[0], gy + offset[1])

    barrier = pltpu.get_barrier_semaphore()
    expected = jnp.int32(0)
    for offset in ALL:

        @pl.when(exists(offset))
        def _(offset=offset):
            pl.semaphore_signal(barrier, inc=1, device_id=at(offset), device_id_type=MESH)

        expected = expected + exists(offset).astype(jnp.int32)

    loads = [
        pltpu.make_async_copy(src, dst, in_sem.at[i])
        for i, (src, dst) in enumerate(((ph_hbm, ph_in), (el_hbm, el_in), (f_hbm, f_in), (pl_hbm, pl_in)))
    ]
    for load in loads:
        load.start()

    for i, offset in enumerate(SIDES_Y):

        @pl.when(jnp.logical_not(exists(offset)))
        def _(i=i):
            recv_b[i] = jnp.zeros(recv_b.shape[1:], jnp.float32)

    for i, offset in enumerate(SIDES_X):

        @pl.when(jnp.logical_not(exists(offset)))
        def _(i=i):
            recv_g[i] = jnp.zeros(recv_g.shape[1:], jnp.float32)

    for i, offset in enumerate(CORNERS):

        @pl.when(jnp.logical_not(exists(offset)))
        def _(i=i):
            recv_c[i] = jnp.zeros(recv_c.shape[1:], jnp.float32)

    loads[0].wait()
    loads[1].wait()
    send_b[4] = packed_map(ph_in[...].astype(jnp.float32))
    send_b[5] = packed_map(el_in[0].astype(jnp.float32))
    send_b[6] = packed_map(el_in[1].astype(jnp.float32))
    loads[2].wait()
    send_b[0:4] = packed_columns(f_in[...].astype(jnp.float32)).reshape(4, X, C)
    loads[3].wait()
    own_row = lax.broadcasted_iota(jnp.int32, (Z, C), 0) % 8 == lanes((Z, C)) // 16
    for side in range(2):
        near, far = ((0, 1), (3, 2))[side]
        for s in range(2):
            for f in range(2):
                a = pl_in[s, f, :, near, :]
                b = pl_in[s, f, :, far, :]
                g = a + 0.5 * (a - b)
                row = (s * 2 + f) * Z
                send_g[side, row : row + Z, :] = g
                spread = pltpu.roll(g, 8, 1, stride=16, stride_axis=0)
                spread = jnp.where(own_row, spread, 0.0).reshape(2, 8, C)
                row = 64 + (s * 2 + f) * 2
                send_g[side, row : row + 2, :] = jnp.sum(spread, axis=1)

    pl.semaphore_wait(barrier, expected)

    def copy_of(i, offset):
        back = (-offset[0], -offset[1])
        if offset in CORNERS:
            src = send_g.at[(offset[0] + 1) // 2, pl.ds(64, 8)]
            dst = recv_c.at[CORNERS.index(back)]
        elif offset in SIDES_Y:
            src = send_b
            dst = recv_b.at[SIDES_Y.index(back)]
        else:
            src = send_g.at[(offset[0] + 1) // 2]
            dst = recv_g.at[SIDES_X.index(back)]
        return pltpu.make_async_remote_copy(
            src_ref=src,
            dst_ref=dst,
            send_sem=send_sem.at[i],
            recv_sem=recv_sem.at[ALL.index(back)],
            device_id=at(offset),
            device_id_type=MESH,
        )

    for i, offset in enumerate(ALL):

        @pl.when(exists(offset))
        def _(i=i, offset=offset):
            copy_of(i, offset).start()

    def wait_from(offset):
        back = (-offset[0], -offset[1])

        @pl.when(exists(offset))
        def _():
            copy_of(ALL.index(back), back).wait_recv()

    for offset in SIDES_X:
        wait_from(offset)

    rows = row_masks(3)
    layer = lax.broadcasted_iota(jnp.int32, (Z, 1, 1), 0)
    one = jnp.float32(1.0)
    masks = (
        (rows < X - 1).astype(jnp.float32),
        (rows > 0).astype(jnp.float32),
        one,
        one,
        (layer < Z - 1).astype(jnp.float32),
        (layer > 0).astype(jnp.float32),
        jnp.where((rows == 0) | (rows == X - 1), 4.0, 0.0),
    )
    shifts = (
        lambda v: roll_rows(v, -1),
        lambda v: roll_rows(v, 1),
        lambda v: roll_last(v, -1),
        lambda v: roll_last(v, 1),
        lambda v: jnp.concatenate([v[1:], v[:1]], axis=0),
        lambda v: jnp.concatenate([v[-1:], v[:-1]], axis=0),
    )

    def trace_own(step, field):
        row = (step * 2 + field) * Z
        lo = jnp.broadcast_to(recv_g[0, row : row + Z, :][:, None, :], (Z, 8, C))
        hi = jnp.broadcast_to(recv_g[1, row : row + Z, :][:, None, :], (Z, 8, C))
        return jnp.concatenate([lo, hi], axis=1)

    decay = jnp.exp(-4.0 * layer.astype(jnp.float32) / Z)
    active = [el_in[s].astype(jnp.float32)[None] for s in range(2)]
    states = steps_of(
        ph_in[...].astype(jnp.float32)[None],
        active,
        f_in[0].astype(jnp.float32),
        f_in[1].astype(jnp.float32),
        trace_own,
        decay,
        shifts,
        masks,
    )
    for f in range(2):
        op_ref[0, f, :, 0:2, :] = states[0][f][:, 0:2, :]
        op_ref[0, f, :, 2:4, :] = states[0][f][:, 14:16, :]
        of_ref[f] = states[1][f]

    for offset in SIDES_Y + CORNERS:
        wait_from(offset)

    lane = lanes((1, 1, 1, C))
    column = lane % 16
    inner = column < 8
    rows = row_masks(4)
    half = lax.broadcasted_iota(jnp.int32, (1, 2, 1, 1), 1)
    layer = half * 8 + lane // 16
    left_open = (gy > 0).astype(jnp.float32)
    right_open = (gy < n_gy - 1).astype(jnp.float32)
    side = lax.broadcasted_iota(jnp.int32, (2, 1, 1, 1), 0)
    opened = jnp.where(side == 0, left_open, right_open)
    masks = (
        (rows < X - 1).astype(jnp.float32),
        (rows > 0).astype(jnp.float32),
        jnp.where(column == 7, opened, 1.0),
        jnp.where(column == 8, opened, 1.0),
        (layer < Z - 1).astype(jnp.float32),
        (layer > 0).astype(jnp.float32),
        jnp.where((rows == 0) | (rows == X - 1), 4.0, 0.0),
    )

    def swap(v):
        return jnp.concatenate([v[:, 1:2], v[:, 0:1]], axis=1)

    def layer_up(v):
        moved = roll_last(v, -16)
        return jnp.where(lane < 112, moved, swap(moved))

    def layer_down(v):
        moved = roll_last(v, 16)
        return jnp.where(lane >= 16, moved, swap(moved))

    shifts = (
        lambda v: roll_rows(v, -1),
        lambda v: roll_rows(v, 1),
        lambda v: roll_last(v, -1),
        lambda v: roll_last(v, 1),
        layer_up,
        layer_down,
    )

    def strip(first, last):
        own = send_b[first:last]
        inside = inner[0]
        return jnp.stack(
            [jnp.where(inside, recv_b[0, first:last], own), jnp.where(inside, own, recv_b[1, first:last])], axis=0
        )

    def trace_strip(step, field):
        row = (step * 2 + field) * 2
        halves = []
        for i in range(2):
            mid = recv_g[i, 64 + row : 66 + row, :]
            low = jnp.where(inner[0, 0], recv_c[2 * i, row : row + 2, :], mid)
            high = jnp.where(inner[0, 0], mid, recv_c[2 * i + 1, row : row + 2, :])
            both = jnp.stack([low, high], axis=0)[:, :, None, :]
            halves.append(jnp.broadcast_to(both, (2, 2, 8, C)))
        return jnp.concatenate(halves, axis=2)

    maps = strip(4, 7)
    decay = jnp.exp(-4.0 * layer.astype(jnp.float32) / Z)
    strips = steps_of(
        maps[:, 0:1],
        [maps[:, 1:2], maps[:, 2:3]],
        strip(0, 2),
        strip(2, 4),
        trace_strip,
        decay,
        shifts,
        masks,
    )
    edge = (lanes((1, X, C)) < 4) | (lanes((1, X, C)) >= C - 4)
    edge4 = (lanes((1, 4, C)) < 4) | (lanes((1, 4, C)) >= C - 4)
    for f in range(2):
        merged = jnp.where(inner[0], strips[1][f][1], strips[1][f][0])
        early = jnp.where(inner[0], strips[0][f][1], strips[0][f][0])
        for j in range(8):
            back = roll_last(merged, -(16 * j + 8))
            back_early = roll_last(early, -(16 * j + 8))
            for h in range(2):
                z = 8 * h + j
                value = jnp.where(edge[0], back[h], of_ref[f, z])
                of_ref[f, z] = value
                op_ref[1, f, z, 0:2, :] = value[0:2]
                op_ref[1, f, z, 2:4, :] = value[14:16]
                op_ref[0, f, z, 0:2, :] = jnp.where(edge4[0, 0:2], back_early[h, 0:2], op_ref[0, f, z, 0:2, :])
                op_ref[0, f, z, 2:4, :] = jnp.where(edge4[0, 0:2], back_early[h, 14:16], op_ref[0, f, z, 2:4, :])

    for i, offset in enumerate(ALL):

        @pl.when(exists(offset))
        def _(i=i, offset=offset):
            copy_of(i, offset).wait_send()


def solution(mesh):
    n_gx = mesh.shape["gx"]
    n_gy = mesh.shape["gy"]

    def shards(fields, phase, electrode, planes):
        in_hbm = pl.BlockSpec(memory_space=pltpu.HBM)
        vmem = pl.BlockSpec(memory_space=pltpu.VMEM)
        return pl.pallas_call(
            functools.partial(kernel, n_gx, n_gy),
            out_shape=(
                jax.ShapeDtypeStruct((2, Z, X, C), jnp.float32),
                jax.ShapeDtypeStruct((2, 2, Z, 4, C), jnp.float32),
            ),
            in_specs=[in_hbm] * 4,
            out_specs=(vmem, vmem),
            scratch_shapes=[
                pltpu.VMEM((2, Z, X, C), jnp.bfloat16),
                pltpu.VMEM((X, C), jnp.int32),
                pltpu.VMEM((2, X, C), jnp.int32),
                pltpu.VMEM((2, 2, Z, 4, C), jnp.float32),
                pltpu.VMEM((7, X, C), jnp.float32),
                pltpu.VMEM((2, 72, C), jnp.float32),
                pltpu.VMEM((2, 7, X, C), jnp.float32),
                pltpu.VMEM((2, 72, C), jnp.float32),
                pltpu.VMEM((4, 8, C), jnp.float32),
                pltpu.SemaphoreType.DMA((4,)),
                pltpu.SemaphoreType.DMA((8,)),
                pltpu.SemaphoreType.DMA((8,)),
            ],
            compiler_params=pltpu.CompilerParams(
                collective_id=0, has_side_effects=True, vmem_limit_bytes=32 * 1024 * 1024
            ),
        )(*[pltpu.with_memory_space_constraint(v, pltpu.HBM) for v in (fields, phase, electrode, planes)])

    placed = (
        P(None, None, "gx", "gy"),
        P("gx", "gy"),
        P(None, "gx", "gy"),
        P(None, None, None, "gx", "gy"),
    )
    return jax.shard_map(
        shards,
        mesh=mesh,
        in_specs=placed,
        out_specs=(P(None, None, "gx", "gy"), P(None, None, None, "gx", "gy")),
        check_vma=False,
    )
```

```python
import functools

import jax
import jax.numpy as jnp
from jax import lax
from jax.experimental import pallas as pl
from jax.experimental.pallas import tpu as pltpu
from jax.sharding import PartitionSpec as P

MESH = pl.DeviceIdType.MESH
cond_oil = 0.6
cond_drop = 2.0
diff_oil = 0.3
diff_drop = 1.0
thermal_slope = 0.3
cheb_radius = 0.95
cheb_ratio = 1.0 / cheb_radius
rho_first = 1.0 / cheb_ratio
rho_second = 1.0 / (2.0 * cheb_ratio - rho_first)
keep_old = rho_second * rho_first
take_new = 2.0 * rho_second / cheb_radius

Z = 16
X = 16
C = 128
CORNERS = ((-1, -1), (-1, 1), (1, -1), (1, 1))
SIDES_Y = ((0, -1), (0, 1))
SIDES_X = ((-1, 0), (1, 0))
ALL = CORNERS + SIDES_Y + SIDES_X


def lanes(shape):
    return lax.broadcasted_iota(jnp.int32, shape, len(shape) - 1)


def roll_last(v, shift):
    return pltpu.roll(v, shift % C, v.ndim - 1)


def roll_rows(v, shift):
    return pltpu.roll(v, shift % X, v.ndim - 2)


def row_masks(ndim):
    shape = (1,) * (ndim - 2) + (X, C)
    rows = lax.broadcasted_iota(jnp.int32, shape, ndim - 2)
    return rows


def packed_columns(v):
    head = v.shape[:-3]
    v = v.reshape(head + (2, 8, X, C))
    lane = lanes(head + (2, X, C))
    out = None
    for j in range(8):
        moved = roll_last(v[..., j, :, :], 16 * j + 8)
        out = moved if out is None else jnp.where(lane >= 16 * j, moved, out)
    return out


def packed_map(v):
    base = jnp.where(lanes(v.shape) < 16, roll_last(v, 8), 0.0)
    base = base + roll_last(base, 16)
    base = base + roll_last(base, 32)
    return base + roll_last(base, 64)


def steps_of(droplet, active, old_t, old_n, decay, shifts, masks):
    xp, xm, yp, ym, zp, zm = shifts
    mxp, mxm, myp, mym, mzp, mzm, edge4 = masks

    def coefficients(k):
        faces = (
            (k + xp(k)) * mxp,
            (k + xm(k)) * mxm,
            (k + yp(k)) * myp,
            (k + ym(k)) * mym,
            (k + zp(k)) * mzp,
            (k + zm(k)) * mzm,
        )
        robin = k * edge4
        diagonal = 1.0 + robin + sum(faces[1:], faces[0])
        return faces, robin, 1.0 / diagonal

    def sweep(v, target, faces):
        total = target
        for face, move in zip(faces, shifts):
            total = total + face * move(v)
        return total

    heat = jnp.broadcast_to(cond_oil + (cond_drop - cond_oil) * droplet, old_t.shape)
    ion_base = diff_oil + (diff_drop - diff_oil) * droplet
    heat_faces, heat_robin, heat_inv = coefficients(heat)
    def open_step(step, old_t, old_n):
        ions = ion_base * jnp.exp(thermal_slope * old_t)
        target_t = old_t + (active[step] * droplet) * decay * (1.0 + 0.5 * old_n * old_n)
        ion_faces, ion_robin, ion_inv = coefficients(ions)
        return (
            (old_t, target_t, sweep(old_t, target_t, heat_faces), heat_faces, heat_robin, heat_inv),
            (old_n, old_n, sweep(old_n, old_n, ion_faces), ion_faces, ion_robin, ion_inv),
        )

    def close_step(parts, step, trace):
        out = []
        for field, (old, target, total, faces, robin, inv) in enumerate(parts):
            given = robin * trace(step, field)
            first = (total + given) * inv
            out.append(sweep(first, target + given, faces) * (take_new * inv) - keep_old * old)
        return out

    parts = open_step(0, old_t, old_n)
    trace = yield
    early = close_step(parts, 0, trace)
    yield early, close_step(open_step(1, *early), 1, trace)


def kernel(
    n_gx,
    n_gy,
    f_hbm,
    ph_hbm,
    el_hbm,
    pl_hbm,
    of_ref,
    op_ref,
    f_in,
    ph_in,
    el_in,
    pl_in,
    send_b,
    send_g,
    recv_b,
    recv_g,
    recv_c,
    in_sem,
    send_sem,
    recv_sem,
):
    gx = lax.axis_index("gx")
    gy = lax.axis_index("gy")

    def exists(offset):
        found = []
        for place, move, count in ((gx, offset[0], n_gx), (gy, offset[1], n_gy)):
            if move < 0:
                found.append(place > 0)
            if move > 0:
                found.append(place < count - 1)
        return functools.reduce(jnp.logical_and, found)

    def at(offset):
        return (gx + offset[0], gy + offset[1])

    barrier = pltpu.get_barrier_semaphore()
    expected = jnp.int32(0)
    for offset in ALL:

        @pl.when(exists(offset))
        def _(offset=offset):
            pl.semaphore_signal(barrier, inc=1, device_id=at(offset), device_id_type=MESH)

        expected = expected + exists(offset).astype(jnp.int32)

    loads = [
        pltpu.make_async_copy(src, dst, in_sem.at[i])
        for i, (src, dst) in enumerate(((ph_hbm, ph_in), (el_hbm, el_in), (f_hbm, f_in), (pl_hbm, pl_in)))
    ]
    for load in loads:
        load.start()

    for i, offset in enumerate(SIDES_Y):

        @pl.when(jnp.logical_not(exists(offset)))
        def _(i=i):
            recv_b[i] = jnp.zeros(recv_b.shape[1:], jnp.float32)

    for i, offset in enumerate(SIDES_X):

        @pl.when(jnp.logical_not(exists(offset)))
        def _(i=i):
            recv_g[i] = jnp.zeros(recv_g.shape[1:], jnp.float32)

    for i, offset in enumerate(CORNERS):

        @pl.when(jnp.logical_not(exists(offset)))
        def _(i=i):
            recv_c[i] = jnp.zeros(recv_c.shape[1:], jnp.float32)

    loads[0].wait()
    loads[1].wait()
    send_b[4] = packed_map(ph_in[...].astype(jnp.float32))
    send_b[5] = packed_map(el_in[0].astype(jnp.float32))
    send_b[6] = packed_map(el_in[1].astype(jnp.float32))
    loads[2].wait()
    send_b[0:4] = packed_columns(f_in[...].astype(jnp.float32)).reshape(4, X, C)
    loads[3].wait()
    own_row = lax.broadcasted_iota(jnp.int32, (Z, C), 0) % 8 == lanes((Z, C)) // 16
    for side in range(2):
        near, far = ((0, 1), (3, 2))[side]
        for s in range(2):
            for f in range(2):
                a = pl_in[s, f, :, near, :]
                b = pl_in[s, f, :, far, :]
                g = a + 0.5 * (a - b)
                row = (s * 2 + f) * Z
                send_g[side, row : row + Z, :] = g
                spread = pltpu.roll(g, 8, 1, stride=16, stride_axis=0)
                spread = jnp.where(own_row, spread, 0.0).reshape(2, 8, C)
                row = 64 + (s * 2 + f) * 2
                send_g[side, row : row + 2, :] = jnp.sum(spread, axis=1)

    pl.semaphore_wait(barrier, expected)

    def copy_of(i, offset):
        back = (-offset[0], -offset[1])
        if offset in CORNERS:
            src = send_g.at[(offset[0] + 1) // 2, pl.ds(64, 8)]
            dst = recv_c.at[CORNERS.index(back)]
        elif offset in SIDES_Y:
            src = send_b
            dst = recv_b.at[SIDES_Y.index(back)]
        else:
            src = send_g.at[(offset[0] + 1) // 2]
            dst = recv_g.at[SIDES_X.index(back)]
        return pltpu.make_async_remote_copy(
            src_ref=src,
            dst_ref=dst,
            send_sem=send_sem.at[i],
            recv_sem=recv_sem.at[ALL.index(back)],
            device_id=at(offset),
            device_id_type=MESH,
        )

    for i, offset in enumerate(ALL):

        @pl.when(exists(offset))
        def _(i=i, offset=offset):
            copy_of(i, offset).start()

    def wait_from(offset):
        back = (-offset[0], -offset[1])

        @pl.when(exists(offset))
        def _():
            copy_of(ALL.index(back), back).wait_recv()

    rows = row_masks(3)
    layer = lax.broadcasted_iota(jnp.int32, (Z, 1, 1), 0)
    one = jnp.float32(1.0)
    masks = (
        (rows < X - 1).astype(jnp.float32),
        (rows > 0).astype(jnp.float32),
        one,
        one,
        (layer < Z - 1).astype(jnp.float32),
        (layer > 0).astype(jnp.float32),
        jnp.where((rows == 0) | (rows == X - 1), 4.0, 0.0),
    )
    shifts = (
        lambda v: roll_rows(v, -1),
        lambda v: roll_rows(v, 1),
        lambda v: roll_last(v, -1),
        lambda v: roll_last(v, 1),
        lambda v: jnp.concatenate([v[1:], v[:1]], axis=0),
        lambda v: jnp.concatenate([v[-1:], v[:-1]], axis=0),
    )

    def trace_own(step, field):
        row = (step * 2 + field) * Z
        lo = jnp.broadcast_to(recv_g[0, row : row + Z, :][:, None, :], (Z, 8, C))
        hi = jnp.broadcast_to(recv_g[1, row : row + Z, :][:, None, :], (Z, 8, C))
        return jnp.concatenate([lo, hi], axis=1)

    decay = jnp.exp(-4.0 * layer.astype(jnp.float32) / Z)
    active = [el_in[s].astype(jnp.float32)[None] for s in range(2)]
    work = steps_of(
        ph_in[...].astype(jnp.float32)[None],
        active,
        f_in[0].astype(jnp.float32),
        f_in[1].astype(jnp.float32),
        decay,
        shifts,
        masks,
    )
    next(work)
    for offset in SIDES_X:
        wait_from(offset)
    states = work.send(trace_own)
    for f in range(2):
        op_ref[0, f, :, 0:2, :] = states[0][f][:, 0:2, :]
        op_ref[0, f, :, 2:4, :] = states[0][f][:, 14:16, :]
        of_ref[f] = states[1][f]

    for offset in SIDES_Y:
        wait_from(offset)

    lane = lanes((1, 1, 1, C))
    column = lane % 16
    inner = column < 8
    rows = row_masks(4)
    half = lax.broadcasted_iota(jnp.int32, (1, 2, 1, 1), 1)
    layer = half * 8 + lane // 16
    left_open = (gy > 0).astype(jnp.float32)
    right_open = (gy < n_gy - 1).astype(jnp.float32)
    side = lax.broadcasted_iota(jnp.int32, (2, 1, 1, 1), 0)
    opened = jnp.where(side == 0, left_open, right_open)
    masks = (
        (rows < X - 1).astype(jnp.float32),
        (rows > 0).astype(jnp.float32),
        jnp.where(column == 7, opened, 1.0),
        jnp.where(column == 8, opened, 1.0),
        (layer < Z - 1).astype(jnp.float32),
        (layer > 0).astype(jnp.float32),
        jnp.where((rows == 0) | (rows == X - 1), 4.0, 0.0),
    )

    def swap(v):
        return jnp.concatenate([v[:, 1:2], v[:, 0:1]], axis=1)

    def layer_up(v):
        moved = roll_last(v, -16)
        return jnp.where(lane < 112, moved, swap(moved))

    def layer_down(v):
        moved = roll_last(v, 16)
        return jnp.where(lane >= 16, moved, swap(moved))

    shifts = (
        lambda v: roll_rows(v, -1),
        lambda v: roll_rows(v, 1),
        lambda v: roll_last(v, -1),
        lambda v: roll_last(v, 1),
        layer_up,
        layer_down,
    )

    def strip(first, last):
        own = send_b[first:last]
        inside = inner[0]
        return jnp.stack(
            [jnp.where(inside, recv_b[0, first:last], own), jnp.where(inside, own, recv_b[1, first:last])], axis=0
        )

    def trace_strip(step, field):
        row = (step * 2 + field) * 2
        halves = []
        for i in range(2):
            mid = recv_g[i, 64 + row : 66 + row, :]
            low = jnp.where(inner[0, 0], recv_c[2 * i, row : row + 2, :], mid)
            high = jnp.where(inner[0, 0], mid, recv_c[2 * i + 1, row : row + 2, :])
            both = jnp.stack([low, high], axis=0)[:, :, None, :]
            halves.append(jnp.broadcast_to(both, (2, 2, 8, C)))
        return jnp.concatenate(halves, axis=2)

    maps = strip(4, 7)
    decay = jnp.exp(-4.0 * layer.astype(jnp.float32) / Z)
    work = steps_of(
        maps[:, 0:1],
        [maps[:, 1:2], maps[:, 2:3]],
        strip(0, 2),
        strip(2, 4),
        decay,
        shifts,
        masks,
    )
    next(work)
    for offset in CORNERS:
        wait_from(offset)
    strips = work.send(trace_strip)
    edge = (lanes((1, X, C)) < 4) | (lanes((1, X, C)) >= C - 4)
    edge4 = (lanes((1, 4, C)) < 4) | (lanes((1, 4, C)) >= C - 4)
    for f in range(2):
        merged = jnp.where(inner[0], strips[1][f][1], strips[1][f][0])
        early = jnp.where(inner[0], strips[0][f][1], strips[0][f][0])
        for j in range(8):
            back = roll_last(merged, -(16 * j + 8))
            back_early = roll_last(early, -(16 * j + 8))
            for h in range(2):
                z = 8 * h + j
                value = jnp.where(edge[0], back[h], of_ref[f, z])
                of_ref[f, z] = value
                op_ref[1, f, z, 0:2, :] = value[0:2]
                op_ref[1, f, z, 2:4, :] = value[14:16]
                op_ref[0, f, z, 0:2, :] = jnp.where(edge4[0, 0:2], back_early[h, 0:2], op_ref[0, f, z, 0:2, :])
                op_ref[0, f, z, 2:4, :] = jnp.where(edge4[0, 0:2], back_early[h, 14:16], op_ref[0, f, z, 2:4, :])

    for i, offset in enumerate(ALL):

        @pl.when(exists(offset))
        def _(i=i, offset=offset):
            copy_of(i, offset).wait_send()


def write_out(f_ref, p_ref, of_hbm, op_hbm, sem):
    copies = [
        pltpu.make_async_copy(f_ref, of_hbm, sem.at[0]),
        pltpu.make_async_copy(p_ref, op_hbm, sem.at[1]),
    ]
    for copy in copies:
        copy.start()
    for copy in copies:
        copy.wait()


def solution(mesh):
    n_gx = mesh.shape["gx"]
    n_gy = mesh.shape["gy"]

    def shards(fields, phase, electrode, planes):
        in_hbm = pl.BlockSpec(memory_space=pltpu.HBM)
        vmem = pl.BlockSpec(memory_space=pltpu.VMEM)
        made = pl.pallas_call(
            functools.partial(kernel, n_gx, n_gy),
            out_shape=(
                jax.ShapeDtypeStruct((2, Z, X, C), jnp.float32),
                jax.ShapeDtypeStruct((2, 2, Z, 4, C), jnp.float32),
            ),
            in_specs=[in_hbm] * 4,
            out_specs=(vmem, vmem),
            scratch_shapes=[
                pltpu.VMEM((2, Z, X, C), jnp.bfloat16),
                pltpu.VMEM((X, C), jnp.int32),
                pltpu.VMEM((2, X, C), jnp.int32),
                pltpu.VMEM((2, 2, Z, 4, C), jnp.float32),
                pltpu.VMEM((7, X, C), jnp.float32),
                pltpu.VMEM((2, 72, C), jnp.float32),
                pltpu.VMEM((2, 7, X, C), jnp.float32),
                pltpu.VMEM((2, 72, C), jnp.float32),
                pltpu.VMEM((4, 8, C), jnp.float32),
                pltpu.SemaphoreType.DMA((4,)),
                pltpu.SemaphoreType.DMA((8,)),
                pltpu.SemaphoreType.DMA((8,)),
            ],
            compiler_params=pltpu.CompilerParams(
                collective_id=0, has_side_effects=True, vmem_limit_bytes=32 * 1024 * 1024
            ),
        )(*[pltpu.with_memory_space_constraint(v, pltpu.HBM) for v in (fields, phase, electrode, planes)])
        return pl.pallas_call(
            write_out,
            out_shape=(
                pltpu.HBM((2, Z, X, C), jnp.float32),
                pltpu.HBM((2, 2, Z, 4, C), jnp.float32),
            ),
            in_specs=[vmem, vmem],
            out_specs=(in_hbm, in_hbm),
            scratch_shapes=[pltpu.SemaphoreType.DMA((2,))],
        )(*[pltpu.with_memory_space_constraint(v, pltpu.VMEM) for v in made])

    placed = (
        P(None, None, "gx", "gy"),
        P("gx", "gy"),
        P(None, "gx", "gy"),
        P(None, None, None, "gx", "gy"),
    )
    return jax.shard_map(
        shards,
        mesh=mesh,
        in_specs=placed,
        out_specs=(P(None, None, "gx", "gy"), P(None, None, None, "gx", "gy")),
        check_vma=False,
    )
```

```python
import functools

import jax
import jax.numpy as jnp
from jax import lax
from jax.experimental import pallas as pl
from jax.experimental.pallas import tpu as pltpu
from jax.sharding import PartitionSpec as P

MESH = pl.DeviceIdType.MESH
cond_oil = 0.6
cond_drop = 2.0
diff_oil = 0.3
diff_drop = 1.0
thermal_slope = 0.3
cheb_radius = 0.95
cheb_ratio = 1.0 / cheb_radius
rho_first = 1.0 / cheb_ratio
rho_second = 1.0 / (2.0 * cheb_ratio - rho_first)
log2_e = 1.4426950408889634
keep_old = rho_second * rho_first
take_new = 2.0 * rho_second / cheb_radius

Z = 16
X = 16
C = 128
CORNERS = ((-1, -1), (-1, 1), (1, -1), (1, 1))
SIDES_Y = ((0, -1), (0, 1))
SIDES_X = ((-1, 0), (1, 0))
ALL = CORNERS + SIDES_Y + SIDES_X


def lanes(shape):
    return lax.broadcasted_iota(jnp.int32, shape, len(shape) - 1)


def roll_last(v, shift):
    return pltpu.roll(v, shift % C, v.ndim - 1)


def roll_rows(v, shift):
    return pltpu.roll(v, shift % X, v.ndim - 2)


def row_masks(ndim):
    shape = (1,) * (ndim - 2) + (X, C)
    rows = lax.broadcasted_iota(jnp.int32, shape, ndim - 2)
    return rows


def packed_columns(v):
    head = v.shape[:-3]
    v = v.reshape(head + (2, 8, X, C))
    lane = lanes(head + (2, X, C))
    out = None
    for j in range(8):
        moved = roll_last(v[..., j, :, :], 16 * j + 8)
        out = moved if out is None else jnp.where(lane >= 16 * j, moved, out)
    return out


def packed_map(v):
    base = jnp.where(lanes(v.shape) < 16, roll_last(v, 8), 0.0)
    base = base + roll_last(base, 16)
    base = base + roll_last(base, 32)
    return base + roll_last(base, 64)


def periodic_columns(v):
    base = jnp.where(lanes(v.shape) < 8, roll_last(v, 4), 0.0)
    for shift in (8, 16, 32, 64):
        base = base + roll_last(base, shift)
    return base


def edge_columns(v):
    lane = lanes(v.shape[:-3] + (X, C))
    out = None
    for z in range(Z):
        moved = roll_last(v[..., z, :, :], 8 * z + 4)
        out = moved if out is None else jnp.where(lane >= 8 * z, moved, out)
    return out


def wider(v):
    v = jnp.stack([roll_last(v, 4), roll_last(v, -60)], axis=v.ndim - 2)
    lane = lanes(v.shape)
    v = jnp.where(lane >= 64, roll_last(v, 32), v)
    v = jnp.where(lane % 64 >= 32, roll_last(v, 16), v)
    return jnp.where(lane % 32 >= 16, roll_last(v, 8), v)


def inverse(v):
    guess = pl.reciprocal(v, approx=True)
    return guess * (2.0 - v * guess)


def steps_of(droplet, active, old_t, old_n, decay, grid):
    def sweep(v, target, faces):
        px, mx, py, my, z_part = faces
        along = px * grid.xp(v) + mx * grid.xm(v)
        across = py * grid.yp(v) + my * grid.ym(v)
        return (target + along) + (across + z_part(v))

    def sides(k):
        px = grid.x_closed(k + grid.xp(k))
        py = grid.y_closed(k + grid.yp(k))
        return px, grid.xm(px), py, grid.ym(py)

    def coefficients(k):
        px, mx, py, my = sides(k)
        z_part, z_total = grid.layers(k)
        robin = k * grid.edge4
        diagonal = (1.0 + robin) + (px + mx) + (py + my) + z_total
        return (px, mx, py, my, z_part), robin, inverse(diagonal)

    def heat_coefficients(k):
        px, mx, py, my = sides(k)
        robin = k * grid.edge4
        diagonal = (1.0 + robin) + (px + mx) + (py + my)
        z_part, inv = grid.even_layers(k, diagonal)
        return (px, mx, py, my, z_part), robin, inv

    ion_base = diff_oil + (diff_drop - diff_oil) * droplet
    heat_faces, heat_robin, heat_inv = heat_coefficients(cond_oil + (cond_drop - cond_oil) * droplet)
    heating = [(0.5 * (e * droplet)) * decay for e in active]

    def open_step(step, old_t, old_n):
        ions = ion_base * jnp.exp2((thermal_slope * log2_e) * old_t)
        target_t = old_t + heating[step] * (2.0 + old_n * old_n)
        ion_faces, ion_robin, ion_inv = coefficients(ions)
        return (
            (old_t, target_t, sweep(old_t, target_t, heat_faces), heat_faces, heat_robin, heat_inv),
            (old_n, old_n, sweep(old_n, old_n, ion_faces), ion_faces, ion_robin, ion_inv),
        )

    def close_step(parts, step, trace):
        out = []
        for field, (old, target, total, faces, robin, inv) in enumerate(parts):
            given = robin * trace(step, field)
            first = (total + given) * inv
            out.append(sweep(first, target + given, faces) * (take_new * inv) - keep_old * old)
        return out

    parts = open_step(0, old_t, old_n)
    trace = yield
    early = close_step(parts, 0, trace)
    yield early, close_step(open_step(1, *early), 1, trace)


class Rolled:
    def xp(self, v):
        return roll_rows(v, -1)

    def xm(self, v):
        return roll_rows(v, 1)

    def yp(self, v):
        return roll_last(v, -1)

    def ym(self, v):
        return roll_last(v, 1)

    def x_closed(self, face):
        half = face[..., 8:, :]
        rows = lax.broadcasted_iota(jnp.int32, (1,) * (face.ndim - 2) + (8, C), face.ndim - 2)
        return jnp.concatenate([face[..., :8, :], jnp.where(rows == 7, 0.0, half)], axis=face.ndim - 2)


class Span:
    def __init__(self, values, start):
        self.values, self.start = values, start

    def __call__(self, lo, hi):
        return self.values[lo - self.start : hi - self.start]


def gathered(function, lo, hi, size=4):
    return Span(jnp.concatenate([function(a, min(a + size, hi)) for a in range(lo, hi, size)], axis=0), lo)


def joined(*spans):
    return Span(jnp.concatenate([span.values for span in spans], axis=0), spans[0].start)


def x_sum(face, v, lo, hi):
    top, low = min(hi, X - 1), max(lo - 1, 0)
    up = face(lo, top)
    down = face(low, hi - 1)
    if v is not None:
        up = up * v(lo + 1, top + 1)
        down = down * v(low, hi - 1)
    first, last = max(lo, 1), top
    parts = [up[:1]] if lo == 0 else []
    if last > first:
        parts.append(up[first - lo : last - lo] + down[first - low - 1 : last - low - 1])
    if hi == X:
        parts.append(down[-1:])
    return jnp.concatenate(parts, axis=0)


class OwnColumns:
    def __init__(self, droplet, active, temper, ions, decay):
        self.olds = [[Span(temper, 0), Span(ions, 0)]]
        both = lambda v: jnp.concatenate([v, v], axis=1)
        heat = cond_oil + (cond_drop - cond_oil) * droplet
        self.ion_base = both(diff_oil + (diff_drop - diff_oil) * droplet)
        self.heating = [Span(both(0.5 * (e * droplet)) * decay, 0) for e in active]
        face = Span(heat[1:] + heat[:-1], 0)
        py = heat + roll_last(heat, -1)
        my = roll_last(py, 1)
        edge = jnp.concatenate([heat[:1], jnp.zeros_like(heat[1:-1]), heat[-1:]], axis=0)
        base = (1.0 + 4.0 * edge) + x_sum(face, None, 0, X) + (py + my)
        twice = both(2.0 * heat)
        row = lax.broadcasted_iota(jnp.int32, (1, Z, C), 1)
        pz = jnp.where(row == Z - 1, 0.0, twice)
        mz = jnp.where(row == 0, 0.0, twice)
        heat_faces = (Span(both(face.values), 0), Span(both(py), 0), Span(both(my), 0), Span(pz, 0), Span(mz, 0))
        self.heat = (heat_faces, Span(inverse(both(base) + (pz + mz)), 0), Span(both(heat), 0))
        self.states = []

    def ion_parts(self, temper, lo, hi):
        k = self.ion_base[lo:hi] * jnp.exp2((thermal_slope * log2_e) * temper(lo, hi))
        py = k + roll_last(k, -1)
        row = lax.broadcasted_iota(jnp.int32, (1, 8, C), 1)
        pz = k + roll_rows(k, -1)
        pz = jnp.concatenate([pz[:, :8], jnp.where(row == 7, 0.0, pz[:, 8:])], axis=1)
        return k, py, roll_last(py, 1), pz, roll_rows(pz, 1)

    def ion_spans(self, temper, lo, hi):
        parts = [self.ion_parts(temper, a, min(a + 4, hi)) for a in range(lo, hi, 4)]
        return [Span(jnp.concatenate(p, axis=0), lo) for p in zip(*parts)]

    def ion_inverse(self, spans, face, lo, hi):
        def part(a, b):
            k, py, my, pz, mz = [v(a, b) for v in spans]
            total = (1.0 + x_sum(face, None, a, b)) + (py + my) + (pz + mz)
            if a == 0:
                total = jnp.concatenate([total[:1] + 4.0 * k[:1], total[1:]], axis=0)
            if b == X:
                total = jnp.concatenate([total[:-1], total[-1:] + 4.0 * k[-1:]], axis=0)
            return inverse(total)

        return gathered(part, lo, hi)

    def sweep(self, v, target, faces, a, b):
        face, py, my, pz, mz = faces
        mid = v(a, b)
        across = py(a, b) * roll_last(mid, -1) + my(a, b) * roll_last(mid, 1)
        upright = pz(a, b) * roll_rows(mid, -1) + mz(a, b) * roll_rows(mid, 1)
        return (target(a, b) + x_sum(face, v, a, b)) + (across + upright)

    def targets(self, step, old, lo, hi):
        heated = lambda a, b: old[0](a, b) + self.heating[step](a, b) * (2.0 + old[1](a, b) * old[1](a, b))
        return [gathered(heated, lo, hi), Span(old[1](lo, hi), lo)]

    def last(self, old, target, first, faces, inv, lo, hi):
        def part(a, b):
            return self.sweep(first, target, faces, a, b) * (take_new * inv(a, b)) - keep_old * old(a, b)

        return gathered(part, lo, hi)

    def before(self):
        old = self.olds[0]
        spans = self.ion_spans(old[0], 0, X)
        face = Span(spans[0].values[1:] + spans[0].values[:-1], 0)
        ion = ((face, *spans[1:]), self.ion_inverse(spans, face, 0, X), spans[0])
        self.sets0 = (self.heat, ion)
        self.target0 = self.targets(0, old, 0, X)
        self.total0, self.first0, self.mid1 = [], [], []
        for f in range(2):
            faces, inv, k = self.sets0[f]
            total = gathered(lambda a, b: self.sweep(old[f], self.target0[f], faces, a, b), 0, X)
            first = gathered(lambda a, b: total(a, b) * inv(a, b), 1, X - 1)
            self.total0.append(total)
            self.first0.append(first)
            self.mid1.append(self.last(old[f], self.target0[f], first, faces, inv, 2, X - 2))
        new = self.mid1
        self.spans1 = self.ion_spans(new[0], 2, X - 2)
        k = self.spans1[0]
        self.face1 = Span(k.values[1:] + k.values[:-1], 2)
        self.inv1 = self.ion_inverse(self.spans1, self.face1, 3, X - 3)
        self.target1 = self.targets(1, new, 2, X - 2)
        sets = ((self.heat[0], self.heat[1]), ((self.face1, *self.spans1[1:]), self.inv1))
        self.first1, self.mid2 = [], []
        for f in range(2):
            faces, inv = sets[f]
            first = gathered(lambda a, b: self.sweep(new[f], self.target1[f], faces, a, b) * inv(a, b), 3, X - 3)
            self.first1.append(first)
            self.mid2.append(self.last(new[f], self.target1[f], first, faces, inv, 4, X - 4))

    def after(self, trace):
        old = self.olds[0]
        news = []
        for f in range(2):
            faces, inv, k = self.sets0[f]
            ends, target = [], self.target0[f].values
            for side, x in ((0, 0), (1, X - 1)):
                given = 4.0 * k(x, x + 1) * trace(0, f, side)
                ends.append((self.total0[f](x, x + 1) + given) * inv(x, x + 1))
                target = (
                    jnp.concatenate([target[:1] + given, target[1:]], axis=0)
                    if side == 0
                    else jnp.concatenate([target[:-1], target[-1:] + given], axis=0)
                )
            first = Span(jnp.concatenate([ends[0], self.first0[f].values, ends[1]], axis=0), 0)
            target = Span(target, 0)
            low = self.last(old[f], target, first, faces, inv, 0, 2)
            high = self.last(old[f], target, first, faces, inv, X - 2, X)
            news.append(joined(low, self.mid1[f], high))
        low, high = self.ion_spans(news[0], 0, 2), self.ion_spans(news[0], X - 2, X)
        spans = [joined(a, b, c) for a, b, c in zip(low, self.spans1, high)]
        k = spans[0].values
        face = Span(
            jnp.concatenate([k[1:3] + k[0:2], self.face1.values, k[X - 2 :] + k[X - 3 : X - 1]], axis=0), 0
        )
        inv = joined(self.ion_inverse(spans, face, 0, 3), self.inv1, self.ion_inverse(spans, face, X - 3, X))
        low, high = self.targets(1, news, 0, 2), self.targets(1, news, X - 2, X)
        ends = []
        for f, (faces, inv, k) in enumerate((self.heat, ((face, *spans[1:]), inv, spans[0]))):
            target = joined(low[f], self.target1[f], high[f]).values
            target = Span(
                jnp.concatenate(
                    [
                        target[:1] + 4.0 * k(0, 1) * trace(1, f, 0),
                        target[1:-1],
                        target[-1:] + 4.0 * k(X - 1, X) * trace(1, f, 1),
                    ],
                    axis=0,
                ),
                0,
            )
            part = lambda a, b: self.sweep(news[f], target, faces, a, b) * inv(a, b)
            first = joined(gathered(part, 0, 3), self.first1[f], gathered(part, X - 3, X))
            ends.append(
                joined(
                    self.last(news[f], target, first, faces, inv, 0, 4),
                    self.mid2[f],
                    self.last(news[f], target, first, faces, inv, X - 4, X),
                )
            )
        return news, ends


class Strips(Rolled):
    def __init__(self, left_open, right_open):
        rows = row_masks(4)
        self.lane = lanes((1, 1, 1, C))
        self.column = self.lane % 16
        layer = 8 * lax.broadcasted_iota(jnp.int32, (1, 2, 1, 1), 1) + self.lane // 16
        side = lax.broadcasted_iota(jnp.int32, (2, 1, 1, 1), 0)
        self.edge4 = jnp.where((rows == 0) | (rows == X - 1), 4.0, 0.0)
        self.between = jnp.where(self.column == 7, jnp.where(side == 0, left_open, right_open), 1.0)
        self.below_top = (layer < Z - 1).astype(jnp.float32)
        self.decay = jnp.exp(-4.0 * layer.astype(jnp.float32) / Z)

    def y_closed(self, face):
        return face * self.between

    def zp(self, v):
        moved = roll_last(v, -16)
        return jnp.where(self.lane < 112, moved, jnp.concatenate([moved[:, 1:2], moved[:, 0:1]], axis=1))

    def zm(self, v):
        moved = roll_last(v, 16)
        return jnp.where(self.lane >= 16, moved, jnp.concatenate([moved[:, 1:2], moved[:, 0:1]], axis=1))

    def layers(self, k):
        up = (k + self.zp(k)) * self.below_top
        down = self.zm(up)
        return lambda v: up * self.zp(v) + down * self.zm(v), up + down

    def even_layers(self, k, diagonal):
        up = jnp.broadcast_to(2.0 * k, k.shape[:1] + (2,) + k.shape[2:]) * self.below_top
        down = self.zm(up)
        return lambda v: up * self.zp(v) + down * self.zm(v), inverse(diagonal + (up + down))


def kernel(
    n_gx,
    n_gy,
    f_hbm,
    ph_hbm,
    el_hbm,
    pl_hbm,
    of_ref,
    op_ref,
    f_in,
    f_32,
    ph_in,
    el_in,
    pl_in,
    own_b,
    send_b,
    send_g,
    recv_b,
    recv_g,
    recv_c,
    in_sem,
    send_sem,
    recv_sem,
):
    gx = lax.axis_index("gx")
    gy = lax.axis_index("gy")

    def exists(offset):
        found = []
        for place, move, count in ((gx, offset[0], n_gx), (gy, offset[1], n_gy)):
            if move < 0:
                found.append(place > 0)
            if move > 0:
                found.append(place < count - 1)
        return functools.reduce(jnp.logical_and, found)

    def at(offset):
        return (gx + offset[0], gy + offset[1])

    barrier = pltpu.get_barrier_semaphore()
    expected = jnp.int32(0)
    for offset in ALL:

        @pl.when(exists(offset))
        def _(offset=offset):
            pl.semaphore_signal(barrier, inc=1, device_id=at(offset), device_id_type=MESH)

        expected = expected + exists(offset).astype(jnp.int32)

    loads = [
        pltpu.make_async_copy(src, dst, in_sem.at[i])
        for i, (src, dst) in enumerate(((ph_hbm, ph_in), (el_hbm, el_in), (f_hbm, f_in), (pl_hbm, pl_in)))
    ]
    for load in loads:
        load.start()

    for i, offset in enumerate(SIDES_Y):

        @pl.when(jnp.logical_not(exists(offset)))
        def _(i=i):
            recv_b[i] = jnp.zeros(recv_b.shape[1:], jnp.float32)

    for i, offset in enumerate(SIDES_X):

        @pl.when(jnp.logical_not(exists(offset)))
        def _(i=i):
            recv_g[i] = jnp.zeros(recv_g.shape[1:], jnp.float32)

    for i, offset in enumerate(CORNERS):

        @pl.when(jnp.logical_not(exists(offset)))
        def _(i=i):
            recv_c[i] = jnp.zeros(recv_c.shape[1:], jnp.float32)

    for load in loads:
        load.wait()
    maps = [ph_in[...].astype(jnp.float32), el_in[0].astype(jnp.float32), el_in[1].astype(jnp.float32)]
    drop, on0, on1 = [periodic_columns(m) for m in maps]
    near = edge_columns(f_in[...].astype(jnp.float32))
    place = lanes((X, C)) % 8
    send_b[0, 0] = jnp.where(place >= 4, near[0], roll_last(drop, -4))
    send_b[0, 1] = jnp.where(place >= 4, near[1], jnp.where(place == 0, roll_last(on1, -4), roll_last(on0, -3)))
    send_b[1, 0] = jnp.where(place < 4, near[0], roll_last(drop, 4))
    send_b[1, 1] = jnp.where(place < 4, near[1], jnp.where(place == 7, roll_last(on1, 4), roll_last(on0, 3)))
    own_row = lax.broadcasted_iota(jnp.int32, (Z, C), 0) % 8 == lanes((Z, C)) // 16
    for side in range(2):
        near, far = ((0, 1), (3, 2))[side]
        for s in range(2):
            for f in range(2):
                a = pl_in[s, f, :, near, :]
                b = pl_in[s, f, :, far, :]
                g = a + 0.5 * (a - b)
                row = (s * 2 + f) * Z
                send_g[side, row : row + Z, :] = g
                spread = pltpu.roll(g, 8, 1, stride=16, stride_axis=0)
                spread = jnp.where(own_row, spread, 0.0).reshape(2, 8, C)
                row = 64 + (s * 2 + f) * 2
                send_g[side, row : row + 2, :] = jnp.sum(spread, axis=1)

    pl.semaphore_wait(barrier, expected)

    def copy_of(i, offset):
        back = (-offset[0], -offset[1])
        if offset in CORNERS:
            src = send_g.at[(offset[0] + 1) // 2, pl.ds(64, 8)]
            dst = recv_c.at[CORNERS.index(back)]
        elif offset in SIDES_Y:
            src = send_b.at[(offset[1] + 1) // 2]
            dst = recv_b.at[SIDES_Y.index(back)]
        else:
            src = send_g.at[(offset[0] + 1) // 2]
            dst = recv_g.at[SIDES_X.index(back)]
        return pltpu.make_async_remote_copy(
            src_ref=src,
            dst_ref=dst,
            send_sem=send_sem.at[i],
            recv_sem=recv_sem.at[ALL.index(back)],
            device_id=at(offset),
            device_id_type=MESH,
        )

    for i, offset in enumerate(ALL):

        @pl.when(exists(offset))
        def _(i=i, offset=offset):
            copy_of(i, offset).start()

    for i in range(3):
        own_b[4 + i] = packed_map(maps[i])
    own_b[0:4] = packed_columns(f_in[...].astype(jnp.float32)).reshape(4, X, C)

    def wait_from(offset):
        back = (-offset[0], -offset[1])

        @pl.when(exists(offset))
        def _():
            copy_of(ALL.index(back), back).wait_recv()

    for f in range(2):
        f_32[f] = f_in[f].astype(jnp.float32).reshape(Z * X, C)
    planes_x = lambda f: jnp.stack([f_32[f, pl.ds(x, Z, stride=X), :] for x in range(X)], axis=0)
    rows = lambda v: jnp.broadcast_to(v[:, None, :], (X, 8, C))
    height = lax.broadcasted_iota(jnp.int32, (1, Z, C), 1)
    decay = jnp.exp(-4.0 * height.astype(jnp.float32) / Z)
    columns = OwnColumns(rows(maps[0]), [rows(maps[1]), rows(maps[2])], planes_x(0), planes_x(1), decay)
    columns.before()
    for offset in SIDES_X + SIDES_Y:
        wait_from(offset)

    def trace_own(step, field, side):
        row = (step * 2 + field) * Z
        return recv_g[side, row : row + Z, :][None]

    early, late = columns.after(trace_own)
    for f in range(2):
        for x in range(X):
            of_ref[f, pl.ds(x, Z, stride=X), :] = late[f].values[x]
        for p, x in enumerate((0, 1, X - 2, X - 1)):
            op_ref[0, f, pl.ds(p, Z, stride=4), :] = early[f].values[x]

    grid = Strips((gy > 0).astype(jnp.float32), (gy < n_gy - 1).astype(jnp.float32))
    inner = grid.column < 8

    def strip(outer, own):
        inside = inner[0, 0]
        return jnp.stack([jnp.where(inside, outer[0], own), jnp.where(inside, own, outer[1])], axis=0)

    def trace_strip(step, field):
        row = (step * 2 + field) * 2
        halves = []
        for i in range(2):
            mid = recv_g[i, 64 + row : 66 + row, :]
            low = jnp.where(inner[0, 0], recv_c[2 * i, row : row + 2, :], mid)
            high = jnp.where(inner[0, 0], mid, recv_c[2 * i + 1, row : row + 2, :])
            both = jnp.stack([low, high], axis=0)[:, :, None, :]
            halves.append(jnp.broadcast_to(both, (2, 2, 8, C)))
        return jnp.concatenate(halves, axis=2)

    fields = [strip([wider(recv_b[i, f]) for i in range(2)], own_b[2 * f : 2 * f + 2]) for f in range(2)]
    drop = strip([recv_b[0, 0], recv_b[1, 0]], own_b[4])
    on0 = strip([roll_last(recv_b[0, 1], 1), roll_last(recv_b[1, 1], -1)], own_b[5])
    on1 = strip([recv_b[0, 1], recv_b[1, 1]], own_b[6])
    work = steps_of(
        drop[:, None],
        [on0[:, None], on1[:, None]],
        fields[0],
        fields[1],
        grid.decay,
        grid,
    )
    next(work)
    for offset in CORNERS:
        wait_from(offset)
    strips = work.send(trace_strip)
    lane = lanes((X, C))
    edge = (lane < 4) | (lane >= C - 4)

    def four(v):
        return [v[..., 0:2, :], v[..., X - 2 : X, :]]

    def both_sides(state):
        return jnp.where(inner[0], state[1], state[0])

    early = jnp.concatenate(four(both_sides(strips[0][0])) + four(both_sides(strips[0][1])), axis=1)
    for j in range(8):
        back = roll_last(early, -(16 * j + 8))
        for h in range(2):
            z = 8 * h + j
            for f in range(2):
                rows = slice(4 * z, 4 * z + 4)
                op_ref[0, f, rows, :] = jnp.where(edge[:4], back[h, 4 * f : 4 * f + 4], op_ref[0, f, rows, :])
    for f in range(2):
        merged = both_sides(strips[1][f])
        for j in range(8):
            back = roll_last(merged, -(16 * j + 8))
            for h in range(2):
                z = 8 * h + j
                rows = slice(X * z, X * z + X)
                value = jnp.where(edge, back[h], of_ref[f, rows, :])
                of_ref[f, rows, :] = value
                op_ref[1, f, 4 * z : 4 * z + 4, :] = jnp.concatenate(four(value), axis=0)

    for i, offset in enumerate(ALL):

        @pl.when(exists(offset))
        def _(i=i, offset=offset):
            copy_of(i, offset).wait_send()


def write_out(f_ref, p_ref, of_hbm, op_hbm, sem):
    copies = [
        pltpu.make_async_copy(f_ref, of_hbm, sem.at[0]),
        pltpu.make_async_copy(p_ref, op_hbm, sem.at[1]),
    ]
    for copy in copies:
        copy.start()
    for copy in copies:
        copy.wait()


def solution(mesh):
    n_gx = mesh.shape["gx"]
    n_gy = mesh.shape["gy"]

    def shards(fields, phase, electrode, planes):
        in_hbm = pl.BlockSpec(memory_space=pltpu.HBM)
        vmem = pl.BlockSpec(memory_space=pltpu.VMEM)
        made = pl.pallas_call(
            functools.partial(kernel, n_gx, n_gy),
            out_shape=(
                jax.ShapeDtypeStruct((2, Z * X, C), jnp.float32),
                jax.ShapeDtypeStruct((2, 2, Z * 4, C), jnp.float32),
            ),
            in_specs=[in_hbm] * 4,
            out_specs=(vmem, vmem),
            scratch_shapes=[
                pltpu.VMEM((2, Z, X, C), jnp.bfloat16),
                pltpu.VMEM((2, Z * X, C), jnp.float32),
                pltpu.VMEM((X, C), jnp.int32),
                pltpu.VMEM((2, X, C), jnp.int32),
                pltpu.VMEM((2, 2, Z, 4, C), jnp.float32),
                pltpu.VMEM((7, X, C), jnp.float32),
                pltpu.VMEM((2, 2, X, C), jnp.float32),
                pltpu.VMEM((2, 72, C), jnp.float32),
                pltpu.VMEM((2, 2, X, C), jnp.float32),
                pltpu.VMEM((2, 72, C), jnp.float32),
                pltpu.VMEM((4, 8, C), jnp.float32),
                pltpu.SemaphoreType.DMA((4,)),
                pltpu.SemaphoreType.DMA((8,)),
                pltpu.SemaphoreType.DMA((8,)),
            ],
            compiler_params=pltpu.CompilerParams(
                collective_id=0, has_side_effects=True, vmem_limit_bytes=32 * 1024 * 1024
            ),
        )(*[pltpu.with_memory_space_constraint(v, pltpu.HBM) for v in (fields, phase, electrode, planes)])
        new_fields, new_planes = pl.pallas_call(
            write_out,
            out_shape=(
                pltpu.HBM((2, Z * X, C), jnp.float32),
                pltpu.HBM((2, 2, Z * 4, C), jnp.float32),
            ),
            in_specs=[vmem, vmem],
            out_specs=(in_hbm, in_hbm),
            scratch_shapes=[pltpu.SemaphoreType.DMA((2,))],
        )(*[pltpu.with_memory_space_constraint(v, pltpu.VMEM) for v in made])
        return new_fields.reshape(2, Z, X, C), new_planes.reshape(2, 2, Z, 4, C)

    placed = (
        P(None, None, "gx", "gy"),
        P("gx", "gy"),
        P(None, "gx", "gy"),
        P(None, None, None, "gx", "gy"),
    )
    return jax.shard_map(
        shards,
        mesh=mesh,
        in_specs=placed,
        out_specs=(P(None, None, "gx", "gy"), P(None, None, None, "gx", "gy")),
        check_vma=False,
    )
```

```python
import functools

import jax
import jax.numpy as jnp
from jax import lax
from jax.experimental import pallas as pl
from jax.experimental.pallas import tpu as pltpu
from jax.sharding import PartitionSpec as P

MESH = pl.DeviceIdType.MESH
cond_oil = 0.6
cond_drop = 2.0
diff_oil = 0.3
diff_drop = 1.0
thermal_slope = 0.3
cheb_radius = 0.95
cheb_ratio = 1.0 / cheb_radius
rho_first = 1.0 / cheb_ratio
rho_second = 1.0 / (2.0 * cheb_ratio - rho_first)
log2_e = 1.4426950408889634
keep_old = rho_second * rho_first
take_new = 2.0 * rho_second / cheb_radius

Z = 16
X = 16
C = 128
CORNERS = ((-1, -1), (-1, 1), (1, -1), (1, 1))
SIDES_Y = ((0, -1), (0, 1))
SIDES_X = ((-1, 0), (1, 0))
ALL = CORNERS + SIDES_Y + SIDES_X


def lanes(shape):
    return lax.broadcasted_iota(jnp.int32, shape, len(shape) - 1)


def roll_last(v, shift):
    return pltpu.roll(v, shift % C, v.ndim - 1)


def roll_rows(v, shift):
    return pltpu.roll(v, shift % X, v.ndim - 2)


def row_masks(ndim):
    shape = (1,) * (ndim - 2) + (X, C)
    rows = lax.broadcasted_iota(jnp.int32, shape, ndim - 2)
    return rows


def packed_columns(v):
    head = v.shape[:-3]
    v = v.reshape(head + (2, 8, X, C))
    lane = lanes(head + (2, X, C))
    out = None
    for j in range(8):
        moved = roll_last(v[..., j, :, :], 16 * j + 8)
        out = moved if out is None else jnp.where(lane >= 16 * j, moved, out)
    return out


def packed_map(v):
    base = jnp.where(lanes(v.shape) < 16, roll_last(v, 8), 0.0)
    base = base + roll_last(base, 16)
    base = base + roll_last(base, 32)
    return base + roll_last(base, 64)


def periodic_columns(v):
    base = jnp.where(lanes(v.shape) < 8, roll_last(v, 4), 0.0)
    for shift in (8, 16, 32, 64):
        base = base + roll_last(base, shift)
    return base


def edge_columns(v):
    lane = lanes(v.shape[:-3] + (X, C))
    out = None
    for z in range(Z):
        moved = roll_last(v[..., z, :, :], 8 * z + 4)
        out = moved if out is None else jnp.where(lane >= 8 * z, moved, out)
    return out


def wider(v):
    v = jnp.stack([roll_last(v, 4), roll_last(v, -60)], axis=v.ndim - 2)
    lane = lanes(v.shape)
    v = jnp.where(lane >= 64, roll_last(v, 32), v)
    v = jnp.where(lane % 64 >= 32, roll_last(v, 16), v)
    return jnp.where(lane % 32 >= 16, roll_last(v, 8), v)


def inverse(v):
    guess = pl.reciprocal(v, approx=True)
    return guess * (2.0 - v * guess)


def steps_of(droplet, active, old_t, old_n, decay, grid):
    def sweep(v, target, faces):
        px, mx, py, my, z_part = faces
        along = px * grid.xp(v) + mx * grid.xm(v)
        across = py * grid.yp(v) + my * grid.ym(v)
        return (target + along) + (across + z_part(v))

    def sides(k):
        px, mx = grid.x_faces(k)
        py, my = grid.y_faces(k)
        return px, mx, py, my

    def coefficients(k):
        px, mx, py, my = sides(k)
        z_part, z_total = grid.layers(k)
        robin = k * grid.edge4
        diagonal = (1.0 + robin) + (px + mx) + (py + my) + z_total
        return (px, mx, py, my, z_part), robin, inverse(diagonal)

    def heat_coefficients(k):
        px, mx, py, my = sides(k)
        robin = k * grid.edge4
        diagonal = (1.0 + robin) + (px + mx) + (py + my)
        z_part, inv = grid.even_layers(k, diagonal)
        return (px, mx, py, my, z_part), robin, inv

    ion_base = diff_oil + (diff_drop - diff_oil) * droplet
    heat_faces, heat_robin, heat_inv = heat_coefficients(cond_oil + (cond_drop - cond_oil) * droplet)
    heating = [(0.5 * (e * droplet)) * decay for e in active]

    def open_step(step, old_t, old_n):
        ions = ion_base * jnp.exp2((thermal_slope * log2_e) * old_t)
        target_t = old_t + heating[step] * (2.0 + old_n * old_n)
        ion_faces, ion_robin, ion_inv = coefficients(ions)
        if step == 0:
            yield
        return (
            (old_t, target_t, sweep(old_t, target_t, heat_faces), heat_faces, heat_robin, heat_inv),
            (old_n, old_n, sweep(old_n, old_n, ion_faces), ion_faces, ion_robin, ion_inv),
        )

    def close_step(parts, step, trace):
        out = []
        for field, (old, target, total, faces, robin, inv) in enumerate(parts):
            given = robin * trace(step, field)
            first = (total + given) * inv
            out.append(sweep(first, target + given, faces) * (take_new * inv) - keep_old * old)
        return out

    yield
    parts = yield from open_step(0, old_t, old_n)
    trace = yield
    early = close_step(parts, 0, trace)
    parts = yield from open_step(1, *early)
    yield early, close_step(parts, 1, trace)


class Rolled:
    def xp(self, v):
        return roll_rows(v, -1)

    def xm(self, v):
        return roll_rows(v, 1)

    def yp(self, v):
        return roll_last(v, -1)

    def ym(self, v):
        return roll_last(v, 1)

    def x_faces(self, k):
        rows = lax.broadcasted_iota(jnp.int32, (1,) * (k.ndim - 2) + (8, C), k.ndim - 2)
        up, down = k + self.xp(k), k + self.xm(k)
        axis = k.ndim - 2
        return (
            jnp.concatenate([up[..., :8, :], jnp.where(rows == 7, 0.0, up[..., 8:, :])], axis=axis),
            jnp.concatenate([jnp.where(rows == 0, 0.0, down[..., :8, :]), down[..., 8:, :]], axis=axis),
        )


class Span:
    def __init__(self, values, start):
        self.values, self.start = values, start

    def __call__(self, lo, hi):
        return self.values[lo - self.start : hi - self.start]


def gathered(function, lo, hi, size=4):
    return Span(jnp.concatenate([function(a, min(a + size, hi)) for a in range(lo, hi, size)], axis=0), lo)


def joined(*spans):
    return Span(jnp.concatenate([span.values for span in spans], axis=0), spans[0].start)


def x_sum(face, v, lo, hi):
    top, low = min(hi, X - 1), max(lo - 1, 0)
    up = face(lo, top)
    down = face(low, hi - 1)
    if v is not None:
        up = up * v(lo + 1, top + 1)
        down = down * v(low, hi - 1)
    first, last = max(lo, 1), top
    parts = [up[:1]] if lo == 0 else []
    if last > first:
        parts.append(up[first - lo : last - lo] + down[first - low - 1 : last - low - 1])
    if hi == X:
        parts.append(down[-1:])
    return jnp.concatenate(parts, axis=0)


class OwnColumns:
    def __init__(self, droplet, active, temper, ions, decay):
        self.olds = [[Span(temper, 0), Span(ions, 0)]]
        both = lambda v: jnp.concatenate([v, v], axis=1)
        heat = cond_oil + (cond_drop - cond_oil) * droplet
        self.ion_base = both(diff_oil + (diff_drop - diff_oil) * droplet)
        self.heating = [Span(both(0.5 * (e * droplet)) * decay, 0) for e in active]
        face = Span(heat[1:] + heat[:-1], 0)
        py = heat + roll_last(heat, -1)
        my = roll_last(py, 1)
        edge = jnp.concatenate([heat[:1], jnp.zeros_like(heat[1:-1]), heat[-1:]], axis=0)
        base = (1.0 + 4.0 * edge) + x_sum(face, None, 0, X) + (py + my)
        twice = both(2.0 * heat)
        row = lax.broadcasted_iota(jnp.int32, (1, Z, C), 1)
        pz = jnp.where(row == Z - 1, 0.0, twice)
        mz = jnp.where(row == 0, 0.0, twice)
        heat_faces = (Span(both(face.values), 0), Span(both(py), 0), Span(both(my), 0), Span(pz, 0), Span(mz, 0))
        self.heat = (heat_faces, Span(inverse(both(base) + (pz + mz)), 0), Span(both(heat), 0))
        self.states = []

    def ion_parts(self, temper, lo, hi):
        k = self.ion_base[lo:hi] * jnp.exp2((thermal_slope * log2_e) * temper(lo, hi))
        row = lax.broadcasted_iota(jnp.int32, (1, 8, C), 1)
        pz, mz = k + roll_rows(k, -1), k + roll_rows(k, 1)
        pz = jnp.concatenate([pz[:, :8], jnp.where(row == 7, 0.0, pz[:, 8:])], axis=1)
        mz = jnp.concatenate([jnp.where(row == 0, 0.0, mz[:, :8]), mz[:, 8:]], axis=1)
        return k, k + roll_last(k, -1), k + roll_last(k, 1), pz, mz

    def ion_spans(self, temper, lo, hi):
        parts = [self.ion_parts(temper, a, min(a + 4, hi)) for a in range(lo, hi, 4)]
        return [Span(jnp.concatenate(p, axis=0), lo) for p in zip(*parts)]

    def ion_inverse(self, spans, face, lo, hi):
        def part(a, b):
            k, py, my, pz, mz = [v(a, b) for v in spans]
            total = (1.0 + x_sum(face, None, a, b)) + (py + my) + (pz + mz)
            if a == 0:
                total = jnp.concatenate([total[:1] + 4.0 * k[:1], total[1:]], axis=0)
            if b == X:
                total = jnp.concatenate([total[:-1], total[-1:] + 4.0 * k[-1:]], axis=0)
            return inverse(total)

        return gathered(part, lo, hi)

    def sweep(self, v, target, faces, a, b):
        face, py, my, pz, mz = faces
        mid = v(a, b)
        across = py(a, b) * roll_last(mid, -1) + my(a, b) * roll_last(mid, 1)
        upright = pz(a, b) * roll_rows(mid, -1) + mz(a, b) * roll_rows(mid, 1)
        return (target(a, b) + x_sum(face, v, a, b)) + (across + upright)

    def targets(self, step, old, lo, hi):
        heated = lambda a, b: old[0](a, b) + self.heating[step](a, b) * (2.0 + old[1](a, b) * old[1](a, b))
        return [gathered(heated, lo, hi), Span(old[1](lo, hi), lo)]

    def last(self, old, target, first, faces, inv, lo, hi):
        def part(a, b):
            return self.sweep(first, target, faces, a, b) * (take_new * inv(a, b)) - keep_old * old(a, b)

        return gathered(part, lo, hi)

    def before(self):
        old = self.olds[0]
        spans = self.ion_spans(old[0], 0, X)
        face = Span(spans[0].values[1:] + spans[0].values[:-1], 0)
        ion = ((face, *spans[1:]), self.ion_inverse(spans, face, 0, X), spans[0])
        self.sets0 = (self.heat, ion)
        self.target0 = self.targets(0, old, 0, X)
        self.total0, self.first0, self.mid1 = [], [], []
        for f in range(2):
            faces, inv, k = self.sets0[f]
            total = gathered(lambda a, b: self.sweep(old[f], self.target0[f], faces, a, b), 0, X)
            first = gathered(lambda a, b: total(a, b) * inv(a, b), 1, X - 1)
            self.total0.append(total)
            self.first0.append(first)
            self.mid1.append(self.last(old[f], self.target0[f], first, faces, inv, 2, X - 2))
        new = self.mid1
        self.spans1 = self.ion_spans(new[0], 2, X - 2)
        k = self.spans1[0]
        self.face1 = Span(k.values[1:] + k.values[:-1], 2)
        self.inv1 = self.ion_inverse(self.spans1, self.face1, 3, X - 3)
        self.target1 = self.targets(1, new, 2, X - 2)
        sets = ((self.heat[0], self.heat[1]), ((self.face1, *self.spans1[1:]), self.inv1))
        self.first1, self.mid2 = [], []
        for f in range(2):
            faces, inv = sets[f]
            first = gathered(lambda a, b: self.sweep(new[f], self.target1[f], faces, a, b) * inv(a, b), 3, X - 3)
            self.first1.append(first)
            self.mid2.append(self.last(new[f], self.target1[f], first, faces, inv, 4, X - 4))

    def after(self, trace):
        old = self.olds[0]
        news = []
        for f in range(2):
            faces, inv, k = self.sets0[f]
            ends, target = [], self.target0[f].values
            for side, x in ((0, 0), (1, X - 1)):
                given = 4.0 * k(x, x + 1) * trace(0, f, side)
                ends.append((self.total0[f](x, x + 1) + given) * inv(x, x + 1))
                target = (
                    jnp.concatenate([target[:1] + given, target[1:]], axis=0)
                    if side == 0
                    else jnp.concatenate([target[:-1], target[-1:] + given], axis=0)
                )
            first = Span(jnp.concatenate([ends[0], self.first0[f].values, ends[1]], axis=0), 0)
            target = Span(target, 0)
            low = self.last(old[f], target, first, faces, inv, 0, 2)
            high = self.last(old[f], target, first, faces, inv, X - 2, X)
            news.append(joined(low, self.mid1[f], high))
            yield
        low, high = self.ion_spans(news[0], 0, 2), self.ion_spans(news[0], X - 2, X)
        spans = [joined(a, b, c) for a, b, c in zip(low, self.spans1, high)]
        k = spans[0].values
        face = Span(
            jnp.concatenate([k[1:3] + k[0:2], self.face1.values, k[X - 2 :] + k[X - 3 : X - 1]], axis=0), 0
        )
        inv = joined(self.ion_inverse(spans, face, 0, 3), self.inv1, self.ion_inverse(spans, face, X - 3, X))
        yield
        low, high = self.targets(1, news, 0, 2), self.targets(1, news, X - 2, X)
        ends = []
        for f, (faces, inv, k) in enumerate((self.heat, ((face, *spans[1:]), inv, spans[0]))):
            target = joined(low[f], self.target1[f], high[f]).values
            target = Span(
                jnp.concatenate(
                    [
                        target[:1] + 4.0 * k(0, 1) * trace(1, f, 0),
                        target[1:-1],
                        target[-1:] + 4.0 * k(X - 1, X) * trace(1, f, 1),
                    ],
                    axis=0,
                ),
                0,
            )
            part = lambda a, b: self.sweep(news[f], target, faces, a, b) * inv(a, b)
            first = joined(gathered(part, 0, 3), self.first1[f], gathered(part, X - 3, X))
            ends.append(
                joined(
                    self.last(news[f], target, first, faces, inv, 0, 4),
                    self.mid2[f],
                    self.last(news[f], target, first, faces, inv, X - 4, X),
                )
            )
            yield
        self.states = news, ends


class Strips(Rolled):
    def __init__(self, left_open, right_open):
        rows = row_masks(4)
        self.lane = lanes((1, 1, 1, C))
        self.column = self.lane % 16
        layer = 8 * lax.broadcasted_iota(jnp.int32, (1, 2, 1, 1), 1) + self.lane // 16
        side = lax.broadcasted_iota(jnp.int32, (2, 1, 1, 1), 0)
        self.edge4 = jnp.where((rows == 0) | (rows == X - 1), 4.0, 0.0)
        opened = jnp.where(side == 0, left_open, right_open)
        self.between_up = jnp.where(self.column == 7, opened, 1.0)
        self.between_down = jnp.where(self.column == 8, opened, 1.0)
        self.below_top = (layer < Z - 1).astype(jnp.float32)
        self.above_floor = (layer > 0).astype(jnp.float32)
        self.decay = jnp.exp(-4.0 * layer.astype(jnp.float32) / Z)

    def y_faces(self, k):
        return (k + self.yp(k)) * self.between_up, (k + self.ym(k)) * self.between_down

    def zp(self, v):
        moved = roll_last(v, -16)
        return jnp.where(self.lane < 112, moved, jnp.concatenate([moved[:, 1:2], moved[:, 0:1]], axis=1))

    def zm(self, v):
        moved = roll_last(v, 16)
        return jnp.where(self.lane >= 16, moved, jnp.concatenate([moved[:, 1:2], moved[:, 0:1]], axis=1))

    def layers(self, k):
        up = (k + self.zp(k)) * self.below_top
        down = (k + self.zm(k)) * self.above_floor
        return lambda v: up * self.zp(v) + down * self.zm(v), up + down

    def even_layers(self, k, diagonal):
        twice = jnp.broadcast_to(2.0 * k, k.shape[:1] + (2,) + k.shape[2:])
        up, down = twice * self.below_top, twice * self.above_floor
        return lambda v: up * self.zp(v) + down * self.zm(v), inverse(diagonal + (up + down))


def kernel(
    n_gx,
    n_gy,
    f_hbm,
    ph_hbm,
    el_hbm,
    pl_hbm,
    of_ref,
    op_ref,
    f_in,
    f_32,
    ph_in,
    el_in,
    pl_in,
    own_b,
    send_b,
    send_g,
    recv_b,
    recv_g,
    recv_c,
    in_sem,
    send_sem,
    recv_sem,
):
    gx = lax.axis_index("gx")
    gy = lax.axis_index("gy")

    def exists(offset):
        found = []
        for place, move, count in ((gx, offset[0], n_gx), (gy, offset[1], n_gy)):
            if move < 0:
                found.append(place > 0)
            if move > 0:
                found.append(place < count - 1)
        return functools.reduce(jnp.logical_and, found)

    def at(offset):
        return (gx + offset[0], gy + offset[1])

    barrier = pltpu.get_barrier_semaphore()
    expected = jnp.int32(0)
    for offset in ALL:

        @pl.when(exists(offset))
        def _(offset=offset):
            pl.semaphore_signal(barrier, inc=1, device_id=at(offset), device_id_type=MESH)

        expected = expected + exists(offset).astype(jnp.int32)

    loads = [
        pltpu.make_async_copy(src, dst, in_sem.at[i])
        for i, (src, dst) in enumerate(((ph_hbm, ph_in), (el_hbm, el_in), (f_hbm, f_in), (pl_hbm, pl_in)))
    ]
    for load in loads:
        load.start()

    for i, offset in enumerate(SIDES_Y):

        @pl.when(jnp.logical_not(exists(offset)))
        def _(i=i):
            recv_b[i] = jnp.zeros(recv_b.shape[1:], jnp.float32)

    for i, offset in enumerate(SIDES_X):

        @pl.when(jnp.logical_not(exists(offset)))
        def _(i=i):
            recv_g[i] = jnp.zeros(recv_g.shape[1:], jnp.float32)

    for i, offset in enumerate(CORNERS):

        @pl.when(jnp.logical_not(exists(offset)))
        def _(i=i):
            recv_c[i] = jnp.zeros(recv_c.shape[1:], jnp.float32)

    for load in loads:
        load.wait()
    maps = [ph_in[...].astype(jnp.float32), el_in[0].astype(jnp.float32), el_in[1].astype(jnp.float32)]
    drop, on0, on1 = [periodic_columns(m) for m in maps]
    near = edge_columns(f_in[...].astype(jnp.float32))
    place = lanes((X, C)) % 8
    send_b[0, 0] = jnp.where(place >= 4, near[0], roll_last(drop, -4))
    send_b[0, 1] = jnp.where(place >= 4, near[1], jnp.where(place == 0, roll_last(on1, -4), roll_last(on0, -3)))
    send_b[1, 0] = jnp.where(place < 4, near[0], roll_last(drop, 4))
    send_b[1, 1] = jnp.where(place < 4, near[1], jnp.where(place == 7, roll_last(on1, 4), roll_last(on0, 3)))
    own_row = lax.broadcasted_iota(jnp.int32, (Z, C), 0) % 8 == lanes((Z, C)) // 16
    for side in range(2):
        near, far = ((0, 1), (3, 2))[side]
        for s in range(2):
            for f in range(2):
                a = pl_in[s, f, :, near, :]
                b = pl_in[s, f, :, far, :]
                g = a + 0.5 * (a - b)
                row = (s * 2 + f) * Z
                send_g[side, row : row + Z, :] = g
                spread = pltpu.roll(g, 8, 1, stride=16, stride_axis=0)
                spread = jnp.where(own_row, spread, 0.0).reshape(2, 8, C)
                row = 64 + (s * 2 + f) * 2
                send_g[side, row : row + 2, :] = jnp.sum(spread, axis=1)

    pl.semaphore_wait(barrier, expected)

    def copy_of(i, offset):
        back = (-offset[0], -offset[1])
        if offset in CORNERS:
            src = send_g.at[(offset[0] + 1) // 2, pl.ds(64, 8)]
            dst = recv_c.at[CORNERS.index(back)]
        elif offset in SIDES_Y:
            src = send_b.at[(offset[1] + 1) // 2]
            dst = recv_b.at[SIDES_Y.index(back)]
        else:
            src = send_g.at[(offset[0] + 1) // 2]
            dst = recv_g.at[SIDES_X.index(back)]
        return pltpu.make_async_remote_copy(
            src_ref=src,
            dst_ref=dst,
            send_sem=send_sem.at[i],
            recv_sem=recv_sem.at[ALL.index(back)],
            device_id=at(offset),
            device_id_type=MESH,
        )

    for i, offset in enumerate(ALL):

        @pl.when(exists(offset))
        def _(i=i, offset=offset):
            copy_of(i, offset).start()

    for i in range(3):
        own_b[4 + i] = packed_map(maps[i])
    own_b[0:4] = packed_columns(f_in[...].astype(jnp.float32)).reshape(4, X, C)

    def wait_from(offset):
        back = (-offset[0], -offset[1])

        @pl.when(exists(offset))
        def _():
            copy_of(ALL.index(back), back).wait_recv()

    for f in range(2):
        f_32[f] = f_in[f].astype(jnp.float32).reshape(Z * X, C)
    planes_x = lambda f: jnp.stack([f_32[f, pl.ds(x, Z, stride=X), :] for x in range(X)], axis=0)
    rows = lambda v: jnp.broadcast_to(v[:, None, :], (X, 8, C))
    height = lax.broadcasted_iota(jnp.int32, (1, Z, C), 1)
    decay = jnp.exp(-4.0 * height.astype(jnp.float32) / Z)
    columns = OwnColumns(rows(maps[0]), [rows(maps[1]), rows(maps[2])], planes_x(0), planes_x(1), decay)
    columns.before()
    for offset in SIDES_X + SIDES_Y:
        wait_from(offset)

    def trace_own(step, field, side):
        row = (step * 2 + field) * Z
        return recv_g[side, row : row + Z, :][None]

    rest = columns.after(trace_own)
    next(rest)
    grid = Strips((gy > 0).astype(jnp.float32), (gy < n_gy - 1).astype(jnp.float32))
    inner = grid.column < 8

    def strip(outer, own):
        inside = inner[0, 0]
        return jnp.stack([jnp.where(inside, outer[0], own), jnp.where(inside, own, outer[1])], axis=0)

    def trace_strip(step, field):
        row = (step * 2 + field) * 2
        halves = []
        for i in range(2):
            mid = recv_g[i, 64 + row : 66 + row, :]
            low = jnp.where(inner[0, 0], recv_c[2 * i, row : row + 2, :], mid)
            high = jnp.where(inner[0, 0], mid, recv_c[2 * i + 1, row : row + 2, :])
            both = jnp.stack([low, high], axis=0)[:, :, None, :]
            halves.append(jnp.broadcast_to(both, (2, 2, 8, C)))
        return jnp.concatenate(halves, axis=2)

    next(rest)
    fields = [strip([wider(recv_b[i, f]) for i in range(2)], own_b[2 * f : 2 * f + 2]) for f in range(2)]
    drop = strip([recv_b[0, 0], recv_b[1, 0]], own_b[4])
    on0 = strip([roll_last(recv_b[0, 1], 1), roll_last(recv_b[1, 1], -1)], own_b[5])
    on1 = strip([recv_b[0, 1], recv_b[1, 1]], own_b[6])
    work = steps_of(
        drop[:, None],
        [on0[:, None], on1[:, None]],
        fields[0],
        fields[1],
        grid.decay,
        grid,
    )
    for _ in rest:
        next(work)
    early, late = columns.states
    for f in range(2):
        for x in range(X):
            of_ref[f, pl.ds(x, Z, stride=X), :] = late[f].values[x]
        for p, x in enumerate((0, 1, X - 2, X - 1)):
            op_ref[0, f, pl.ds(p, Z, stride=4), :] = early[f].values[x]
    for offset in CORNERS:
        wait_from(offset)
    strips = work.send(trace_strip)
    lane = lanes((X, C))
    edge = (lane < 4) | (lane >= C - 4)

    def four(v):
        return [v[..., 0:2, :], v[..., X - 2 : X, :]]

    def both_sides(state):
        return jnp.where(inner[0], state[1], state[0])

    early = jnp.concatenate(four(both_sides(strips[0][0])) + four(both_sides(strips[0][1])), axis=1)
    for j in range(8):
        back = roll_last(early, -(16 * j + 8))
        for h in range(2):
            z = 8 * h + j
            for f in range(2):
                rows = slice(4 * z, 4 * z + 4)
                op_ref[0, f, rows, :] = jnp.where(edge[:4], back[h, 4 * f : 4 * f + 4], op_ref[0, f, rows, :])
    for f in range(2):
        merged = both_sides(strips[1][f])
        for j in range(8):
            back = roll_last(merged, -(16 * j + 8))
            for h in range(2):
                z = 8 * h + j
                rows = slice(X * z, X * z + X)
                value = jnp.where(edge, back[h], of_ref[f, rows, :])
                of_ref[f, rows, :] = value
                op_ref[1, f, 4 * z : 4 * z + 4, :] = jnp.concatenate(four(value), axis=0)

    for i, offset in enumerate(ALL):

        @pl.when(exists(offset))
        def _(i=i, offset=offset):
            copy_of(i, offset).wait_send()


def write_out(f_ref, p_ref, of_hbm, op_hbm, sem):
    copies = [
        pltpu.make_async_copy(f_ref, of_hbm, sem.at[0]),
        pltpu.make_async_copy(p_ref, op_hbm, sem.at[1]),
    ]
    for copy in copies:
        copy.start()
    for copy in copies:
        copy.wait()


def solution(mesh):
    n_gx = mesh.shape["gx"]
    n_gy = mesh.shape["gy"]

    def shards(fields, phase, electrode, planes):
        in_hbm = pl.BlockSpec(memory_space=pltpu.HBM)
        vmem = pl.BlockSpec(memory_space=pltpu.VMEM)
        made = pl.pallas_call(
            functools.partial(kernel, n_gx, n_gy),
            out_shape=(
                jax.ShapeDtypeStruct((2, Z * X, C), jnp.float32),
                jax.ShapeDtypeStruct((2, 2, Z * 4, C), jnp.float32),
            ),
            in_specs=[in_hbm] * 4,
            out_specs=(vmem, vmem),
            scratch_shapes=[
                pltpu.VMEM((2, Z, X, C), jnp.bfloat16),
                pltpu.VMEM((2, Z * X, C), jnp.float32),
                pltpu.VMEM((X, C), jnp.int32),
                pltpu.VMEM((2, X, C), jnp.int32),
                pltpu.VMEM((2, 2, Z, 4, C), jnp.float32),
                pltpu.VMEM((7, X, C), jnp.float32),
                pltpu.VMEM((2, 2, X, C), jnp.float32),
                pltpu.VMEM((2, 72, C), jnp.float32),
                pltpu.VMEM((2, 2, X, C), jnp.float32),
                pltpu.VMEM((2, 72, C), jnp.float32),
                pltpu.VMEM((4, 8, C), jnp.float32),
                pltpu.SemaphoreType.DMA((4,)),
                pltpu.SemaphoreType.DMA((8,)),
                pltpu.SemaphoreType.DMA((8,)),
            ],
            compiler_params=pltpu.CompilerParams(
                collective_id=0, has_side_effects=True, vmem_limit_bytes=32 * 1024 * 1024
            ),
        )(*[pltpu.with_memory_space_constraint(v, pltpu.HBM) for v in (fields, phase, electrode, planes)])
        new_fields, new_planes = pl.pallas_call(
            write_out,
            out_shape=(
                pltpu.HBM((2, Z * X, C), jnp.float32),
                pltpu.HBM((2, 2, Z * 4, C), jnp.float32),
            ),
            in_specs=[vmem, vmem],
            out_specs=(in_hbm, in_hbm),
            scratch_shapes=[pltpu.SemaphoreType.DMA((2,))],
        )(*[pltpu.with_memory_space_constraint(v, pltpu.VMEM) for v in made])
        return new_fields.reshape(2, Z, X, C), new_planes.reshape(2, 2, Z, 4, C)

    placed = (
        P(None, None, "gx", "gy"),
        P("gx", "gy"),
        P(None, "gx", "gy"),
        P(None, None, None, "gx", "gy"),
    )
    return jax.shard_map(
        shards,
        mesh=mesh,
        in_specs=placed,
        out_specs=(P(None, None, "gx", "gy"), P(None, None, None, "gx", "gy")),
        check_vma=False,
    )
```

```python
import functools

import jax
import jax.numpy as jnp
from jax import lax
from jax.experimental import pallas as pl
from jax.experimental.pallas import tpu as pltpu
from jax.sharding import PartitionSpec as P

MESH = pl.DeviceIdType.MESH
cond_oil = 0.6
cond_drop = 2.0
diff_oil = 0.3
diff_drop = 1.0
thermal_slope = 0.3
cheb_radius = 0.95
cheb_ratio = 1.0 / cheb_radius
rho_first = 1.0 / cheb_ratio
rho_second = 1.0 / (2.0 * cheb_ratio - rho_first)
log2_e = 1.4426950408889634
keep_old = rho_second * rho_first
take_new = 2.0 * rho_second / cheb_radius

Z = 16
X = 16
C = 128
PITCH = 17
CORNERS = ((-1, -1), (-1, 1), (1, -1), (1, 1))
SIDES_Y = ((0, -1), (0, 1))
SIDES_X = ((-1, 0), (1, 0))
ALL = CORNERS + SIDES_Y + SIDES_X


def lanes(shape):
    return lax.broadcasted_iota(jnp.int32, shape, len(shape) - 1)


def roll_last(v, shift):
    return pltpu.roll(v, shift % C, v.ndim - 1)


def roll_rows(v, shift):
    return pltpu.roll(v, shift % 8, v.ndim - 2)


def rows_of(ref, index, start, step):
    at = lambda first: ref[(*index, pl.ds(first, 8, stride=step), slice(None))]
    return jnp.stack([at(start), at(start + step // 2)], axis=0)


def next_of(v, axis, turn):
    even, odd = lax.slice_in_dim(v, 0, 1, axis=axis), lax.slice_in_dim(v, 1, 2, axis=axis)
    return jnp.concatenate([odd, turn(even)], axis=axis)


def previous_of(v, axis, turn):
    even, odd = lax.slice_in_dim(v, 0, 1, axis=axis), lax.slice_in_dim(v, 1, 2, axis=axis)
    return jnp.concatenate([turn(odd), even], axis=axis)


def faces_of(k, axis, forth, back, last, first):
    even, odd = lax.slice_in_dim(k, 0, 1, axis=axis), lax.slice_in_dim(k, 1, 2, axis=axis)
    inner = even + odd
    up = jnp.where(last, 0.0, odd + forth(even))
    down = jnp.where(first, 0.0, even + back(odd))
    return jnp.concatenate([inner, up], axis=axis), jnp.concatenate([down, inner], axis=axis)


def packed_columns(v):
    head = v.shape[:-3]
    v = v.reshape(head + (8, 2, X, C))
    lane = lanes(head + (2, X, C))
    out = None
    for j in range(8):
        moved = roll_last(v[..., j, :, :, :], 16 * j + 8)
        out = moved if out is None else jnp.where(lane >= 16 * j, moved, out)
    return out


def packed_map(v):
    base = jnp.where(lanes(v.shape) < 16, roll_last(v, 8), 0.0)
    base = base + roll_last(base, 16)
    base = base + roll_last(base, 32)
    return base + roll_last(base, 64)


def periodic_columns(v):
    base = jnp.where(lanes(v.shape) < 8, roll_last(v, 4), 0.0)
    for shift in (8, 16, 32, 64):
        base = base + roll_last(base, shift)
    return base


def edge_columns(v):
    lane = lanes(v.shape[:-3] + (X, C))
    out = None
    for z in range(Z):
        moved = roll_last(v[..., z, :, :], 8 * z + 4)
        out = moved if out is None else jnp.where(lane >= 8 * z, moved, out)
    return out


def inverse(v):
    guess = pl.reciprocal(v, approx=True)
    return guess * (2.0 - v * guess)


def steps_of(droplet, active, old_t, old_n, decay, grid):
    def sweep(v, target, faces):
        px, mx, py, my, z_part = faces
        along = px * grid.xp(v) + mx * grid.xm(v)
        across = py * grid.yp(v) + my * grid.ym(v)
        return (target + along) + (across + z_part(v))

    def sides(k):
        return (*grid.x_faces(k), *grid.y_faces(k))

    def coefficients(k):
        px, mx, py, my = sides(k)
        z_part, z_total = grid.layers(k)
        robin = k * grid.edge4
        diagonal = (1.0 + robin) + (px + mx) + (py + my) + z_total
        return (px, mx, py, my, z_part), robin, inverse(diagonal)

    def heat_coefficients(k):
        px, mx, py, my = sides(k)
        robin = k * grid.edge4
        diagonal = (1.0 + robin) + (px + mx) + (py + my)
        z_part, inv = grid.even_layers(k, diagonal)
        return (px, mx, py, my, z_part), robin, inv

    ion_base = diff_oil + (diff_drop - diff_oil) * droplet
    heat_faces, heat_robin, heat_inv = heat_coefficients(cond_oil + (cond_drop - cond_oil) * droplet)
    heating = [(0.5 * (e * droplet)) * decay for e in active]

    def open_step(step, old_t, old_n):
        ions = ion_base * jnp.exp2((thermal_slope * log2_e) * old_t)
        target_t = old_t + heating[step] * (2.0 + old_n * old_n)
        ion_faces, ion_robin, ion_inv = coefficients(ions)
        if step == 0:
            yield
        return (
            (old_t, target_t, sweep(old_t, target_t, heat_faces), heat_faces, heat_robin, heat_inv),
            (old_n, old_n, sweep(old_n, old_n, ion_faces), ion_faces, ion_robin, ion_inv),
        )

    def close_step(parts, step, trace):
        out = []
        for field, (old, target, total, faces, robin, inv) in enumerate(parts):
            given = robin * trace(step, field)
            first = (total + given) * inv
            out.append(sweep(first, target + given, faces) * (take_new * inv) - keep_old * old)
        return out

    yield
    parts = yield from open_step(0, old_t, old_n)
    trace = yield
    early = close_step(parts, 0, trace)
    parts = yield from open_step(1, *early)
    yield early, close_step(parts, 1, trace)


class Span:
    def __init__(self, values, start):
        self.values, self.start = values, start

    def __call__(self, lo, hi):
        return self.values[lo - self.start : hi - self.start]


def gathered(function, lo, hi, size=4):
    return Span(jnp.concatenate([function(a, min(a + size, hi)) for a in range(lo, hi, size)], axis=0), lo)


def joined(*spans):
    return Span(jnp.concatenate([span.values for span in spans], axis=0), spans[0].start)


def x_sum(face, v, lo, hi):
    top, low = min(hi, X - 1), max(lo - 1, 0)
    up = face(lo, top)
    down = face(low, hi - 1)
    if v is not None:
        up = up * v(lo + 1, top + 1)
        down = down * v(low, hi - 1)
    first, last = max(lo, 1), top
    parts = [up[:1]] if lo == 0 else []
    if last > first:
        parts.append(up[first - lo : last - lo] + down[first - low - 1 : last - low - 1])
    if hi == X:
        parts.append(down[-1:])
    return jnp.concatenate(parts, axis=0)


class OwnColumns:
    def __init__(self, droplet, active, temper, ions, decay):
        self.olds = [[Span(temper, 0), Span(ions, 0)]]
        both = lambda v: jnp.concatenate([v, v], axis=1)
        heat = cond_oil + (cond_drop - cond_oil) * droplet
        self.ion_base = both(diff_oil + (diff_drop - diff_oil) * droplet)
        self.heating = [Span(both(0.5 * (e * droplet)) * decay, 0) for e in active]
        face = Span(heat[1:] + heat[:-1], 0)
        py = heat + roll_last(heat, -1)
        my = roll_last(py, 1)
        edge = jnp.concatenate([heat[:1], jnp.zeros_like(heat[1:-1]), heat[-1:]], axis=0)
        base = (1.0 + 4.0 * edge) + x_sum(face, None, 0, X) + (py + my)
        row = lax.broadcasted_iota(jnp.int32, (1, 1, 8, 1), 2)
        self.high, self.low = row == 7, row == 0
        pz = jnp.concatenate([2.0 * heat, jnp.where(self.high, 0.0, 2.0 * heat)], axis=1)
        mz = jnp.concatenate([jnp.where(self.low, 0.0, 2.0 * heat), 2.0 * heat], axis=1)
        heat_faces = (Span(both(face.values), 0), Span(both(py), 0), Span(both(my), 0), Span(pz, 0), Span(mz, 0))
        self.heat = (heat_faces, Span(inverse(both(base) + (pz + mz)), 0), Span(both(heat), 0))
        self.states = []

    def ion_parts(self, temper, lo, hi):
        k = self.ion_base[lo:hi] * jnp.exp2((thermal_slope * log2_e) * temper(lo, hi))
        pz, mz = faces_of(k, 1, lambda u: roll_rows(u, -1), lambda u: roll_rows(u, 1), self.high, self.low)
        return k, k + roll_last(k, -1), k + roll_last(k, 1), pz, mz

    def ion_spans(self, temper, lo, hi):
        parts = [self.ion_parts(temper, a, min(a + 4, hi)) for a in range(lo, hi, 4)]
        return [Span(jnp.concatenate(p, axis=0), lo) for p in zip(*parts)]

    def ion_inverse(self, spans, face, lo, hi):
        def part(a, b):
            k, py, my, pz, mz = [v(a, b) for v in spans]
            total = (1.0 + x_sum(face, None, a, b)) + (py + my) + (pz + mz)
            if a == 0:
                total = jnp.concatenate([total[:1] + 4.0 * k[:1], total[1:]], axis=0)
            if b == X:
                total = jnp.concatenate([total[:-1], total[-1:] + 4.0 * k[-1:]], axis=0)
            return inverse(total)

        return gathered(part, lo, hi)

    def sweep(self, v, target, faces, a, b):
        face, py, my, pz, mz = faces
        mid = v(a, b)
        across = py(a, b) * roll_last(mid, -1) + my(a, b) * roll_last(mid, 1)
        above = next_of(mid, 1, lambda u: roll_rows(u, -1))
        below = previous_of(mid, 1, lambda u: roll_rows(u, 1))
        upright = pz(a, b) * above + mz(a, b) * below
        return (target(a, b) + x_sum(face, v, a, b)) + (across + upright)

    def targets(self, step, old, lo, hi):
        heated = lambda a, b: old[0](a, b) + self.heating[step](a, b) * (2.0 + old[1](a, b) * old[1](a, b))
        return [gathered(heated, lo, hi), Span(old[1](lo, hi), lo)]

    def last(self, old, target, first, faces, inv, lo, hi):
        def part(a, b):
            return self.sweep(first, target, faces, a, b) * (take_new * inv(a, b)) - keep_old * old(a, b)

        return gathered(part, lo, hi)

    def before(self):
        old = self.olds[0]
        spans = self.ion_spans(old[0], 0, X)
        face = Span(spans[0].values[1:] + spans[0].values[:-1], 0)
        ion = ((face, *spans[1:]), self.ion_inverse(spans, face, 0, X), spans[0])
        self.sets0 = (self.heat, ion)
        self.target0 = self.targets(0, old, 0, X)
        self.total0, self.first0, self.mid1 = [], [], []
        for f in range(2):
            faces, inv, k = self.sets0[f]
            total = gathered(lambda a, b: self.sweep(old[f], self.target0[f], faces, a, b), 0, X)
            first = gathered(lambda a, b: total(a, b) * inv(a, b), 1, X - 1)
            self.total0.append(total)
            self.first0.append(first)
            self.mid1.append(self.last(old[f], self.target0[f], first, faces, inv, 2, X - 2))
        new = self.mid1
        self.spans1 = self.ion_spans(new[0], 2, X - 2)
        k = self.spans1[0]
        self.face1 = Span(k.values[1:] + k.values[:-1], 2)
        self.inv1 = self.ion_inverse(self.spans1, self.face1, 3, X - 3)
        self.target1 = self.targets(1, new, 2, X - 2)
        sets = ((self.heat[0], self.heat[1]), ((self.face1, *self.spans1[1:]), self.inv1))
        self.first1, self.mid2 = [], []
        for f in range(2):
            faces, inv = sets[f]
            first = gathered(lambda a, b: self.sweep(new[f], self.target1[f], faces, a, b) * inv(a, b), 3, X - 3)
            self.first1.append(first)
            self.mid2.append(self.last(new[f], self.target1[f], first, faces, inv, 4, X - 4))

    def after(self, trace):
        old = self.olds[0]
        news = []
        for f in range(2):
            faces, inv, k = self.sets0[f]
            ends, target = [], self.target0[f].values
            for side, x in ((0, 0), (1, X - 1)):
                given = 4.0 * k(x, x + 1) * trace(0, f, side)
                ends.append((self.total0[f](x, x + 1) + given) * inv(x, x + 1))
                target = (
                    jnp.concatenate([target[:1] + given, target[1:]], axis=0)
                    if side == 0
                    else jnp.concatenate([target[:-1], target[-1:] + given], axis=0)
                )
            first = Span(jnp.concatenate([ends[0], self.first0[f].values, ends[1]], axis=0), 0)
            target = Span(target, 0)
            low = self.last(old[f], target, first, faces, inv, 0, 2)
            high = self.last(old[f], target, first, faces, inv, X - 2, X)
            news.append(joined(low, self.mid1[f], high))
            yield
        low, high = self.ion_spans(news[0], 0, 2), self.ion_spans(news[0], X - 2, X)
        spans = [joined(a, b, c) for a, b, c in zip(low, self.spans1, high)]
        k = spans[0].values
        face = Span(
            jnp.concatenate([k[1:3] + k[0:2], self.face1.values, k[X - 2 :] + k[X - 3 : X - 1]], axis=0), 0
        )
        inv = joined(self.ion_inverse(spans, face, 0, 3), self.inv1, self.ion_inverse(spans, face, X - 3, X))
        yield
        low, high = self.targets(1, news, 0, 2), self.targets(1, news, X - 2, X)
        ends = []
        for f, (faces, inv, k) in enumerate((self.heat, ((face, *spans[1:]), inv, spans[0]))):
            target = joined(low[f], self.target1[f], high[f]).values
            target = Span(
                jnp.concatenate(
                    [
                        target[:1] + 4.0 * k(0, 1) * trace(1, f, 0),
                        target[1:-1],
                        target[-1:] + 4.0 * k(X - 1, X) * trace(1, f, 1),
                    ],
                    axis=0,
                ),
                0,
            )
            part = lambda a, b: self.sweep(news[f], target, faces, a, b) * inv(a, b)
            first = joined(gathered(part, 0, 3), self.first1[f], gathered(part, X - 3, X))
            ends.append(
                joined(
                    self.last(news[f], target, first, faces, inv, 0, 4),
                    self.mid2[f],
                    self.last(news[f], target, first, faces, inv, X - 4, X),
                )
            )
            yield
        self.states = news, ends


class Strips:
    def __init__(self, left_open, right_open):
        self.lane = lanes((1, 1, 1, 1, C))
        self.column = self.lane % 16
        row = lax.broadcasted_iota(jnp.int32, (1, 1, 1, 8, 1), 3)
        half_x = lax.broadcasted_iota(jnp.int32, (1, 1, 2, 1, 1), 2)
        half_z = lax.broadcasted_iota(jnp.int32, (1, 2, 1, 1, 1), 1)
        side = lax.broadcasted_iota(jnp.int32, (2, 1, 1, 1, 1), 0)
        self.low, self.high = row == 0, row == 7
        self.floor, self.top = self.lane < 16, self.lane >= 112
        self.edge4 = jnp.where(2 * row + half_x == 0, 4.0, 0.0) + jnp.where(2 * row + half_x == X - 1, 4.0, 0.0)
        opened = jnp.where(side == 0, left_open, right_open)
        self.between_up = jnp.where(self.column == 7, opened, 1.0)
        self.between_down = jnp.where(self.column == 8, opened, 1.0)
        self.decay = jnp.exp(-4.0 * (2 * (self.lane // 16) + half_z).astype(jnp.float32) / Z)

    def xp(self, v):
        return next_of(v, 2, lambda u: roll_rows(u, -1))

    def xm(self, v):
        return previous_of(v, 2, lambda u: roll_rows(u, 1))

    def yp(self, v):
        return roll_last(v, -1)

    def ym(self, v):
        return roll_last(v, 1)

    def zp(self, v):
        return next_of(v, 1, lambda u: roll_last(u, -16))

    def zm(self, v):
        return previous_of(v, 1, lambda u: roll_last(u, 16))

    def x_faces(self, k):
        return faces_of(k, 2, lambda u: roll_rows(u, -1), lambda u: roll_rows(u, 1), self.high, self.low)

    def y_faces(self, k):
        return (k + self.yp(k)) * self.between_up, (k + self.ym(k)) * self.between_down

    def layers(self, k):
        up, down = faces_of(k, 1, lambda u: roll_last(u, -16), lambda u: roll_last(u, 16), self.top, self.floor)
        return lambda v: up * self.zp(v) + down * self.zm(v), up + down

    def even_layers(self, k, diagonal):
        twice = 2.0 * k
        up = jnp.concatenate([twice, jnp.where(self.top, 0.0, twice)], axis=1)
        down = jnp.concatenate([jnp.where(self.floor, 0.0, twice), twice], axis=1)
        return lambda v: up * self.zp(v) + down * self.zm(v), inverse(diagonal + (up + down))


def kernel(
    n_gx,
    n_gy,
    f_hbm,
    ph_hbm,
    el_hbm,
    pl_hbm,
    of_ref,
    op_ref,
    f_in,
    f_32,
    ph_in,
    el_in,
    pl_in,
    own_b,
    send_b,
    send_g,
    recv_b,
    recv_g,
    recv_c,
    merge_ref,
    late_ref,
    in_sem,
    send_sem,
    recv_sem,
):
    gx = lax.axis_index("gx")
    gy = lax.axis_index("gy")

    def exists(offset):
        found = []
        for place, move, count in ((gx, offset[0], n_gx), (gy, offset[1], n_gy)):
            if move < 0:
                found.append(place > 0)
            if move > 0:
                found.append(place < count - 1)
        return functools.reduce(jnp.logical_and, found)

    def at(offset):
        return (gx + offset[0], gy + offset[1])

    barrier = pltpu.get_barrier_semaphore()
    expected = jnp.int32(0)
    for offset in ALL:

        @pl.when(exists(offset))
        def _(offset=offset):
            pl.semaphore_signal(barrier, inc=1, device_id=at(offset), device_id_type=MESH)

        expected = expected + exists(offset).astype(jnp.int32)

    loads = [
        pltpu.make_async_copy(src, dst, in_sem.at[i])
        for i, (src, dst) in enumerate(((ph_hbm, ph_in), (el_hbm, el_in), (f_hbm, f_in), (pl_hbm, pl_in)))
    ]
    for load in loads:
        load.start()

    for i, offset in enumerate(SIDES_Y):

        @pl.when(jnp.logical_not(exists(offset)))
        def _(i=i):
            recv_b[i] = jnp.zeros(recv_b.shape[1:], jnp.float32)

    for i, offset in enumerate(SIDES_X):

        @pl.when(jnp.logical_not(exists(offset)))
        def _(i=i):
            recv_g[i] = jnp.zeros(recv_g.shape[1:], jnp.float32)

    for i, offset in enumerate(CORNERS):

        @pl.when(jnp.logical_not(exists(offset)))
        def _(i=i):
            recv_c[i] = jnp.zeros(recv_c.shape[1:], jnp.float32)

    for load in loads:
        load.wait()
    maps = [ph_in[...].astype(jnp.float32), el_in[0].astype(jnp.float32), el_in[1].astype(jnp.float32)]
    drop, on0, on1 = [periodic_columns(m) for m in maps]
    near = edge_columns(f_in[...].astype(jnp.float32))
    place = lanes((X, C)) % 8
    send_b[0, 0] = jnp.where(place >= 4, near[0], roll_last(drop, -4))
    send_b[0, 1] = jnp.where(place >= 4, near[1], jnp.where(place == 0, roll_last(on1, -4), roll_last(on0, -3)))
    send_b[1, 0] = jnp.where(place < 4, near[0], roll_last(drop, 4))
    send_b[1, 1] = jnp.where(place < 4, near[1], jnp.where(place == 7, roll_last(on1, 4), roll_last(on0, 3)))
    own_row = lax.broadcasted_iota(jnp.int32, (8, C), 0) == lanes((8, C)) // 16
    for side in range(2):
        near, far = ((0, 1), (3, 2))[side]
        for s in range(2):
            for f in range(2):
                first = (s * 2 + f) * Z
                a = pl_in[pl.ds(4 * first + near, Z, stride=4), :]
                b = pl_in[pl.ds(4 * first + far, Z, stride=4), :]
                send_g[side, first : first + Z, :] = a + 0.5 * (a - b)
    for side in range(2):
        for row in range(4):
            halves = rows_of(send_g, (side,), row * Z, 2)
            for h in range(2):
                spread = pltpu.roll(halves[h], 8, 1, stride=16, stride_axis=0)
                spread = jnp.sum(jnp.where(own_row, spread, 0.0), axis=0, keepdims=True)
                send_g[side, 64 + 2 * row + h : 65 + 2 * row + h, :] = spread

    pl.semaphore_wait(barrier, expected)

    def copy_of(i, offset):
        back = (-offset[0], -offset[1])
        if offset in CORNERS:
            src = send_g.at[(offset[0] + 1) // 2, pl.ds(64, 8)]
            dst = recv_c.at[CORNERS.index(back)]
        elif offset in SIDES_Y:
            src = send_b.at[(offset[1] + 1) // 2]
            dst = recv_b.at[SIDES_Y.index(back)]
        else:
            src = send_g.at[(offset[0] + 1) // 2]
            dst = recv_g.at[SIDES_X.index(back)]
        return pltpu.make_async_remote_copy(
            src_ref=src,
            dst_ref=dst,
            send_sem=send_sem.at[i],
            recv_sem=recv_sem.at[ALL.index(back)],
            device_id=at(offset),
            device_id_type=MESH,
        )

    for i, offset in enumerate(ALL):

        @pl.when(exists(offset))
        def _(i=i, offset=offset):
            copy_of(i, offset).start()

    for i in range(3):
        own_b[4 + i] = packed_map(maps[i])
    own_b[0:4] = packed_columns(f_in[...].astype(jnp.float32)).reshape(4, X, C)

    def wait_from(offset):
        back = (-offset[0], -offset[1])

        @pl.when(exists(offset))
        def _():
            copy_of(ALL.index(back), back).wait_recv()

    for f in range(2):
        layers = f_in[f].astype(jnp.float32)
        for z in range(Z):
            f_32[f, PITCH * z : PITCH * z + X, :] = layers[z]
    planes_x = lambda f: jnp.stack([rows_of(f_32, (f,), x, 2 * PITCH) for x in range(X)], axis=0)
    rows = lambda v: jnp.broadcast_to(v[:, None, None, :], (X, 1, 8, C))
    half = lax.broadcasted_iota(jnp.int32, (1, 2, 1, 1), 1)
    height = 2 * lax.broadcasted_iota(jnp.int32, (1, 1, 8, C), 2) + half
    decay = jnp.exp(-4.0 * height.astype(jnp.float32) / Z)
    columns = OwnColumns(rows(maps[0]), [rows(maps[1]), rows(maps[2])], planes_x(0), planes_x(1), decay)
    columns.before()
    for offset in SIDES_X + SIDES_Y:
        wait_from(offset)

    def trace_own(step, field, side):
        return rows_of(recv_g, (side,), (step * 2 + field) * Z, 2)[None]

    rest = columns.after(trace_own)
    next(rest)
    grid = Strips((gy > 0).astype(jnp.float32), (gy < n_gy - 1).astype(jnp.float32))
    inner = grid.column[0] < 8

    def strip(outer, own):
        return jnp.stack([jnp.where(inner, outer[0], own), jnp.where(inner, own, outer[1])], axis=0)

    def halo(side, field):
        v = rows_of(recv_b, (side, field), 0, 2)
        return jnp.stack([roll_last(v, 4), roll_last(v, -4)], axis=0)

    def own_strip(i):
        return rows_of(own_b, (i,), 0, 2)

    def map_strip(field, own, turns):
        outer = [roll_last(rows_of(recv_b, (side, field), 0, 2), turns[side])[None] for side in range(2)]
        return strip(outer, own_strip(own)[None])

    def trace_strip(step, field):
        row = (step * 2 + field) * 2
        halves = []
        for i in range(2):
            mid = recv_g[i, 64 + row : 66 + row, :]
            low = jnp.where(inner[0, 0], recv_c[2 * i, row : row + 2, :], mid)
            high = jnp.where(inner[0, 0], mid, recv_c[2 * i + 1, row : row + 2, :])
            halves.append(jnp.broadcast_to(jnp.stack([low, high], axis=0)[:, :, None, :], (2, 2, 8, C)))
        return jnp.stack(halves, axis=2)

    next(rest)
    fields = [
        strip([halo(side, f) for side in range(2)], jnp.stack([own_strip(2 * f), own_strip(2 * f + 1)], axis=0))
        for f in range(2)
    ]
    drop = map_strip(0, 4, (0, 0))
    on0 = map_strip(1, 5, (1, -1))
    on1 = map_strip(1, 6, (0, 0))
    work = steps_of(
        drop,
        [on0, on1],
        fields[0],
        fields[1],
        grid.decay,
        grid,
    )
    for _ in rest:
        next(work)
    early, late = columns.states
    for f in range(2):
        for h in range(2):
            for x in range(X):
                late_ref[f, pl.ds(PITCH * x + h, 8, stride=2), :] = late[f].values[x, h]
            for p, x in enumerate((0, 1, X - 2, X - 1)):
                op_ref[0, f, pl.ds(p + 4 * h, 8, stride=8), :] = early[f].values[x, h]
    for offset in CORNERS:
        wait_from(offset)
    strips = work.send(trace_strip)
    lane = lanes((X, C))
    edge = (lane < 4) | (lane >= C - 4)

    def both_sides(state):
        return jnp.where(inner, state[1], state[0])

    four = []
    for f in range(2):
        state = both_sides(strips[0][f])
        four += [state[:, 0, 0:1], state[:, 1, 0:1], state[:, 0, 7:8], state[:, 1, 7:8]]
    four = jnp.concatenate(four, axis=1)
    for j in range(8):
        back = roll_last(four, -(16 * j + 8))
        for h in range(2):
            for f in range(2):
                rows = slice(4 * (2 * j + h), 4 * (2 * j + h) + 4)
                op_ref[0, f, rows, :] = jnp.where(edge[:4], back[h, 4 * f : 4 * f + 4], op_ref[0, f, rows, :])
    for f in range(2):
        state = both_sides(strips[1][f])
        for h in range(2):
            for i in range(2):
                merge_ref[f, h, pl.ds(i, 8, stride=2), :] = state[h, i]
    for f in range(2):
        for h in range(2):
            state = merge_ref[f, h]
            for j in range(8):
                z = 2 * j + h
                rows = slice(X * z, X * z + X)
                value = jnp.where(edge, roll_last(state, -(16 * j + 8)), late_ref[f, pl.ds(z, X, stride=PITCH), :])
                of_ref[f, rows, :] = value
                op_ref[1, f, 4 * z : 4 * z + 4, :] = jnp.concatenate([value[0:2], value[X - 2 :]], axis=0)

    for i, offset in enumerate(ALL):

        @pl.when(exists(offset))
        def _(i=i, offset=offset):
            copy_of(i, offset).wait_send()


def write_out(f_ref, p_ref, of_hbm, op_hbm, sem):
    copies = [
        pltpu.make_async_copy(f_ref, of_hbm, sem.at[0]),
        pltpu.make_async_copy(p_ref, op_hbm, sem.at[1]),
    ]
    for copy in copies:
        copy.start()
    for copy in copies:
        copy.wait()


def solution(mesh):
    n_gx = mesh.shape["gx"]
    n_gy = mesh.shape["gy"]

    def shards(fields, phase, electrode, planes):
        in_hbm = pl.BlockSpec(memory_space=pltpu.HBM)
        vmem = pl.BlockSpec(memory_space=pltpu.VMEM)
        made = pl.pallas_call(
            functools.partial(kernel, n_gx, n_gy),
            out_shape=(
                jax.ShapeDtypeStruct((2, Z * X, C), jnp.float32),
                jax.ShapeDtypeStruct((2, 2, Z * 4, C), jnp.float32),
            ),
            in_specs=[in_hbm] * 4,
            out_specs=(vmem, vmem),
            scratch_shapes=[
                pltpu.VMEM((2, Z, X, C), jnp.bfloat16),
                pltpu.VMEM((2, Z * PITCH, C), jnp.float32),
                pltpu.VMEM((X, C), jnp.int32),
                pltpu.VMEM((2, X, C), jnp.int32),
                pltpu.VMEM((2 * 2 * Z * 4, C), jnp.float32),
                pltpu.VMEM((7, X, C), jnp.float32),
                pltpu.VMEM((2, 2, X, C), jnp.float32),
                pltpu.VMEM((2, 72, C), jnp.float32),
                pltpu.VMEM((2, 2, X, C), jnp.float32),
                pltpu.VMEM((2, 72, C), jnp.float32),
                pltpu.VMEM((4, 8, C), jnp.float32),
                pltpu.VMEM((2, 2, X, C), jnp.float32),
                pltpu.VMEM((2, PITCH * X, C), jnp.float32),
                pltpu.SemaphoreType.DMA((4,)),
                pltpu.SemaphoreType.DMA((8,)),
                pltpu.SemaphoreType.DMA((8,)),
            ],
            compiler_params=pltpu.CompilerParams(
                collective_id=0, has_side_effects=True, vmem_limit_bytes=32 * 1024 * 1024
            ),
        )(*[pltpu.with_memory_space_constraint(v, pltpu.HBM) for v in (fields, phase, electrode, planes.reshape(2 * 2 * Z * 4, C))])
        new_fields, new_planes = pl.pallas_call(
            write_out,
            out_shape=(
                pltpu.HBM((2, Z * X, C), jnp.float32),
                pltpu.HBM((2, 2, Z * 4, C), jnp.float32),
            ),
            in_specs=[vmem, vmem],
            out_specs=(in_hbm, in_hbm),
            scratch_shapes=[pltpu.SemaphoreType.DMA((2,))],
        )(*[pltpu.with_memory_space_constraint(v, pltpu.VMEM) for v in made])
        return new_fields.reshape(2, Z, X, C), new_planes.reshape(2, 2, Z, 4, C)

    placed = (
        P(None, None, "gx", "gy"),
        P("gx", "gy"),
        P(None, "gx", "gy"),
        P(None, None, None, "gx", "gy"),
    )
    return jax.shard_map(
        shards,
        mesh=mesh,
        in_specs=placed,
        out_specs=(P(None, None, "gx", "gy"), P(None, None, None, "gx", "gy")),
        check_vma=False,
    )
```

```python
import functools

import jax
import jax.numpy as jnp
from jax import lax
from jax.experimental import pallas as pl
from jax.experimental.pallas import tpu as pltpu
from jax.sharding import PartitionSpec as P

MESH = pl.DeviceIdType.MESH
cond_oil = 0.6
cond_drop = 2.0
diff_oil = 0.3
diff_drop = 1.0
thermal_slope = 0.3
cheb_radius = 0.95
cheb_ratio = 1.0 / cheb_radius
rho_first = 1.0 / cheb_ratio
rho_second = 1.0 / (2.0 * cheb_ratio - rho_first)
log2_e = 1.4426950408889634
keep_old = rho_second * rho_first
take_new = 2.0 * rho_second / cheb_radius

Z = 16
X = 16
C = 128
PITCH = 17
CORNERS = ((-1, -1), (-1, 1), (1, -1), (1, 1))
SIDES_Y = ((0, -1), (0, 1))
SIDES_X = ((-1, 0), (1, 0))
ALL = CORNERS + SIDES_Y + SIDES_X


def lanes(shape):
    return lax.broadcasted_iota(jnp.int32, shape, len(shape) - 1)


def roll_last(v, shift):
    return pltpu.roll(v, shift % C, v.ndim - 1)


def roll_rows(v, shift):
    return pltpu.roll(v, shift % 8, v.ndim - 2)


def rows_of(ref, index, start, step):
    at = lambda first: ref[(*index, pl.ds(first, 8, stride=step), slice(None))]
    return jnp.stack([at(start), at(start + step // 2)], axis=0)


def next_of(v, axis, turn):
    even, odd = lax.slice_in_dim(v, 0, 1, axis=axis), lax.slice_in_dim(v, 1, 2, axis=axis)
    return jnp.concatenate([odd, turn(even)], axis=axis)


def previous_of(v, axis, turn):
    even, odd = lax.slice_in_dim(v, 0, 1, axis=axis), lax.slice_in_dim(v, 1, 2, axis=axis)
    return jnp.concatenate([turn(odd), even], axis=axis)


def faces_of(k, axis, forth, back, last, first):
    even, odd = lax.slice_in_dim(k, 0, 1, axis=axis), lax.slice_in_dim(k, 1, 2, axis=axis)
    inner = even + odd
    up = jnp.where(last, 0.0, odd + forth(even))
    down = jnp.where(first, 0.0, even + back(odd))
    return jnp.concatenate([inner, up], axis=axis), jnp.concatenate([down, inner], axis=axis)


def packed_columns(v):
    head = v.shape[:-3]
    v = v.reshape(head + (8, 2, X, C))
    lane = lanes(head + (2, X, C))
    out = None
    for j in range(8):
        moved = roll_last(v[..., j, :, :, :], 16 * j + 8)
        out = moved if out is None else jnp.where(lane >= 16 * j, moved, out)
    return out


def packed_map(v):
    base = jnp.where(lanes(v.shape) < 16, roll_last(v, 8), 0.0)
    base = base + roll_last(base, 16)
    base = base + roll_last(base, 32)
    return base + roll_last(base, 64)


def periodic_columns(v):
    base = jnp.where(lanes(v.shape) < 8, roll_last(v, 4), 0.0)
    for shift in (8, 16, 32, 64):
        base = base + roll_last(base, shift)
    return base


def edge_columns(v):
    lane = lanes(v.shape[:-3] + (X, C))
    out = None
    for z in range(Z):
        moved = roll_last(v[..., z, :, :], 8 * z + 4)
        out = moved if out is None else jnp.where(lane >= 8 * z, moved, out)
    return out


def inverse(v):
    guess = pl.reciprocal(v, approx=True)
    return guess * (2.0 - v * guess)


def steps_of(droplet, active, old_t, old_n, decay, grid):
    def sweep(v, target, faces):
        px, mx, py, my, z_part = faces
        along = px * grid.xp(v) + mx * grid.xm(v)
        across = py * grid.yp(v) + my * grid.ym(v)
        return (target + along) + (across + z_part(v))

    def sides(k):
        return (*grid.x_faces(k), *grid.y_faces(k))

    def coefficients(k):
        px, mx, py, my = sides(k)
        z_part, z_total = grid.layers(k)
        robin = k * grid.edge4
        diagonal = (1.0 + robin) + (px + mx) + (py + my) + z_total
        return (px, mx, py, my, z_part), robin, inverse(diagonal)

    def heat_coefficients(k):
        px, mx, py, my = sides(k)
        robin = k * grid.edge4
        diagonal = (1.0 + robin) + (px + mx) + (py + my)
        z_part, inv = grid.even_layers(k, diagonal)
        return (px, mx, py, my, z_part), robin, inv

    ion_base = diff_oil + (diff_drop - diff_oil) * droplet
    heat_faces, heat_robin, heat_inv = heat_coefficients(cond_oil + (cond_drop - cond_oil) * droplet)
    heating = [(0.5 * (e * droplet)) * decay for e in active]

    def open_step(step, old_t, old_n):
        ions = ion_base * jnp.exp2((thermal_slope * log2_e) * old_t)
        target_t = old_t + heating[step] * (2.0 + old_n * old_n)
        ion_faces, ion_robin, ion_inv = coefficients(ions)
        if step == 0:
            yield
        return (
            (old_t, target_t, sweep(old_t, target_t, heat_faces), heat_faces, heat_robin, heat_inv),
            (old_n, old_n, sweep(old_n, old_n, ion_faces), ion_faces, ion_robin, ion_inv),
        )

    def close_field(parts, step, field, trace):
        old, target, total, faces, robin, inv = parts[field]
        given = robin * trace(step, field)
        first = (total + given) * inv
        return sweep(first, target + given, faces) * (take_new * inv) - keep_old * old

    yield
    parts = yield from open_step(0, old_t, old_n)
    trace = yield
    early = [close_field(parts, 0, field, trace) for field in range(2)]
    yield early
    parts = yield from open_step(1, *early)
    for field in range(2):
        yield close_field(parts, 1, field, trace)


class Span:
    def __init__(self, values, start):
        self.values, self.start = values, start

    def __call__(self, lo, hi):
        return self.values[lo - self.start : hi - self.start]


def gathered(function, lo, hi, size=4):
    return Span(jnp.concatenate([function(a, min(a + size, hi)) for a in range(lo, hi, size)], axis=0), lo)


def joined(*spans):
    return Span(jnp.concatenate([span.values for span in spans], axis=0), spans[0].start)


def x_sum(face, v, lo, hi):
    top, low = min(hi, X - 1), max(lo - 1, 0)
    up = face(lo, top)
    down = face(low, hi - 1)
    if v is not None:
        up = up * v(lo + 1, top + 1)
        down = down * v(low, hi - 1)
    first, last = max(lo, 1), top
    parts = [up[:1]] if lo == 0 else []
    if last > first:
        parts.append(up[first - lo : last - lo] + down[first - low - 1 : last - low - 1])
    if hi == X:
        parts.append(down[-1:])
    return jnp.concatenate(parts, axis=0)


class OwnColumns:
    def __init__(self, droplet, active, temper, ions, decay):
        self.olds = [[Span(temper, 0), Span(ions, 0)]]
        both = lambda v: jnp.concatenate([v, v], axis=1)
        heat = cond_oil + (cond_drop - cond_oil) * droplet
        self.ion_base = both(diff_oil + (diff_drop - diff_oil) * droplet)
        self.heating = [Span(both(0.5 * (e * droplet)) * decay, 0) for e in active]
        face = Span(heat[1:] + heat[:-1], 0)
        py = heat + roll_last(heat, -1)
        my = roll_last(py, 1)
        edge = jnp.concatenate([heat[:1], jnp.zeros_like(heat[1:-1]), heat[-1:]], axis=0)
        base = (1.0 + 4.0 * edge) + x_sum(face, None, 0, X) + (py + my)
        row = lax.broadcasted_iota(jnp.int32, (1, 1, 8, 1), 2)
        self.high, self.low = row == 7, row == 0
        pz = jnp.concatenate([2.0 * heat, jnp.where(self.high, 0.0, 2.0 * heat)], axis=1)
        mz = jnp.concatenate([jnp.where(self.low, 0.0, 2.0 * heat), 2.0 * heat], axis=1)
        heat_faces = (Span(both(face.values), 0), Span(both(py), 0), Span(both(my), 0), Span(pz, 0), Span(mz, 0))
        self.heat = (heat_faces, Span(inverse(both(base) + (pz + mz)), 0), Span(both(heat), 0))
        self.states = []

    def ion_parts(self, temper, lo, hi):
        k = self.ion_base[lo:hi] * jnp.exp2((thermal_slope * log2_e) * temper(lo, hi))
        pz, mz = faces_of(k, 1, lambda u: roll_rows(u, -1), lambda u: roll_rows(u, 1), self.high, self.low)
        return k, k + roll_last(k, -1), k + roll_last(k, 1), pz, mz

    def ion_spans(self, temper, lo, hi):
        parts = [self.ion_parts(temper, a, min(a + 4, hi)) for a in range(lo, hi, 4)]
        return [Span(jnp.concatenate(p, axis=0), lo) for p in zip(*parts)]

    def ion_inverse(self, spans, face, lo, hi):
        def part(a, b):
            k, py, my, pz, mz = [v(a, b) for v in spans]
            total = (1.0 + x_sum(face, None, a, b)) + (py + my) + (pz + mz)
            if a == 0:
                total = jnp.concatenate([total[:1] + 4.0 * k[:1], total[1:]], axis=0)
            if b == X:
                total = jnp.concatenate([total[:-1], total[-1:] + 4.0 * k[-1:]], axis=0)
            return inverse(total)

        return gathered(part, lo, hi)

    def sweep(self, v, target, faces, a, b):
        face, py, my, pz, mz = faces
        mid = v(a, b)
        across = py(a, b) * roll_last(mid, -1) + my(a, b) * roll_last(mid, 1)
        above = next_of(mid, 1, lambda u: roll_rows(u, -1))
        below = previous_of(mid, 1, lambda u: roll_rows(u, 1))
        upright = pz(a, b) * above + mz(a, b) * below
        return (target(a, b) + x_sum(face, v, a, b)) + (across + upright)

    def targets(self, step, old, lo, hi):
        heated = lambda a, b: old[0](a, b) + self.heating[step](a, b) * (2.0 + old[1](a, b) * old[1](a, b))
        return [gathered(heated, lo, hi), Span(old[1](lo, hi), lo)]

    def last(self, old, target, first, faces, inv, lo, hi):
        def part(a, b):
            return self.sweep(first, target, faces, a, b) * (take_new * inv(a, b)) - keep_old * old(a, b)

        return gathered(part, lo, hi)

    def before(self):
        old = self.olds[0]
        spans = self.ion_spans(old[0], 0, X)
        face = Span(spans[0].values[1:] + spans[0].values[:-1], 0)
        ion = ((face, *spans[1:]), self.ion_inverse(spans, face, 0, X), spans[0])
        self.sets0 = (self.heat, ion)
        self.target0 = self.targets(0, old, 0, X)
        self.total0, self.first0, self.mid1 = [], [], []
        for f in range(2):
            faces, inv, k = self.sets0[f]
            total = gathered(lambda a, b: self.sweep(old[f], self.target0[f], faces, a, b), 0, X)
            first = gathered(lambda a, b: total(a, b) * inv(a, b), 1, X - 1)
            self.total0.append(total)
            self.first0.append(first)
            self.mid1.append(self.last(old[f], self.target0[f], first, faces, inv, 2, X - 2))
        new = self.mid1
        self.spans1 = self.ion_spans(new[0], 2, X - 2)
        k = self.spans1[0]
        self.face1 = Span(k.values[1:] + k.values[:-1], 2)
        self.inv1 = self.ion_inverse(self.spans1, self.face1, 3, X - 3)
        self.target1 = self.targets(1, new, 2, X - 2)
        sets = ((self.heat[0], self.heat[1]), ((self.face1, *self.spans1[1:]), self.inv1))
        self.first1, self.mid2 = [], []
        for f in range(2):
            faces, inv = sets[f]
            first = gathered(lambda a, b: self.sweep(new[f], self.target1[f], faces, a, b) * inv(a, b), 3, X - 3)
            self.first1.append(first)
            self.mid2.append(self.last(new[f], self.target1[f], first, faces, inv, 4, X - 4))

    def after(self, trace):
        old = self.olds[0]
        news = []
        for f in range(2):
            faces, inv, k = self.sets0[f]
            ends, target = [], self.target0[f].values
            for side, x in ((0, 0), (1, X - 1)):
                given = 4.0 * k(x, x + 1) * trace(0, f, side)
                ends.append((self.total0[f](x, x + 1) + given) * inv(x, x + 1))
                target = (
                    jnp.concatenate([target[:1] + given, target[1:]], axis=0)
                    if side == 0
                    else jnp.concatenate([target[:-1], target[-1:] + given], axis=0)
                )
            first = Span(jnp.concatenate([ends[0], self.first0[f].values, ends[1]], axis=0), 0)
            target = Span(target, 0)
            low = self.last(old[f], target, first, faces, inv, 0, 2)
            high = self.last(old[f], target, first, faces, inv, X - 2, X)
            news.append(joined(low, self.mid1[f], high))
            yield
        low, high = self.ion_spans(news[0], 0, 2), self.ion_spans(news[0], X - 2, X)
        spans = [joined(a, b, c) for a, b, c in zip(low, self.spans1, high)]
        k = spans[0].values
        face = Span(
            jnp.concatenate([k[1:3] + k[0:2], self.face1.values, k[X - 2 :] + k[X - 3 : X - 1]], axis=0), 0
        )
        inv = joined(self.ion_inverse(spans, face, 0, 3), self.inv1, self.ion_inverse(spans, face, X - 3, X))
        yield
        low, high = self.targets(1, news, 0, 2), self.targets(1, news, X - 2, X)
        ends = []
        for f, (faces, inv, k) in enumerate((self.heat, ((face, *spans[1:]), inv, spans[0]))):
            target = joined(low[f], self.target1[f], high[f]).values
            target = Span(
                jnp.concatenate(
                    [
                        target[:1] + 4.0 * k(0, 1) * trace(1, f, 0),
                        target[1:-1],
                        target[-1:] + 4.0 * k(X - 1, X) * trace(1, f, 1),
                    ],
                    axis=0,
                ),
                0,
            )
            part = lambda a, b: self.sweep(news[f], target, faces, a, b) * inv(a, b)
            first = joined(gathered(part, 0, 3), self.first1[f], gathered(part, X - 3, X))
            ends.append(
                joined(
                    self.last(news[f], target, first, faces, inv, 0, 4),
                    self.mid2[f],
                    self.last(news[f], target, first, faces, inv, X - 4, X),
                )
            )
            yield
        self.states = news, ends


class Strips:
    def __init__(self, left_open, right_open):
        self.lane = lanes((1, 1, 1, 1, C))
        self.column = self.lane % 16
        row = lax.broadcasted_iota(jnp.int32, (1, 1, 1, 8, 1), 3)
        half_x = lax.broadcasted_iota(jnp.int32, (1, 1, 2, 1, 1), 2)
        half_z = lax.broadcasted_iota(jnp.int32, (1, 2, 1, 1, 1), 1)
        side = lax.broadcasted_iota(jnp.int32, (2, 1, 1, 1, 1), 0)
        self.low, self.high = row == 0, row == 7
        self.floor, self.top = self.lane < 16, self.lane >= 112
        self.edge4 = jnp.where(2 * row + half_x == 0, 4.0, 0.0) + jnp.where(2 * row + half_x == X - 1, 4.0, 0.0)
        opened = jnp.where(side == 0, left_open, right_open)
        self.between_up = jnp.where(self.column == 7, opened, 1.0)
        self.between_down = jnp.where(self.column == 8, opened, 1.0)
        self.decay = jnp.exp(-4.0 * (2 * (self.lane // 16) + half_z).astype(jnp.float32) / Z)

    def xp(self, v):
        return next_of(v, 2, lambda u: roll_rows(u, -1))

    def xm(self, v):
        return previous_of(v, 2, lambda u: roll_rows(u, 1))

    def yp(self, v):
        return roll_last(v, -1)

    def ym(self, v):
        return roll_last(v, 1)

    def zp(self, v):
        return next_of(v, 1, lambda u: roll_last(u, -16))

    def zm(self, v):
        return previous_of(v, 1, lambda u: roll_last(u, 16))

    def x_faces(self, k):
        return faces_of(k, 2, lambda u: roll_rows(u, -1), lambda u: roll_rows(u, 1), self.high, self.low)

    def y_faces(self, k):
        return (k + self.yp(k)) * self.between_up, (k + self.ym(k)) * self.between_down

    def layers(self, k):
        up, down = faces_of(k, 1, lambda u: roll_last(u, -16), lambda u: roll_last(u, 16), self.top, self.floor)
        return lambda v: up * self.zp(v) + down * self.zm(v), up + down

    def even_layers(self, k, diagonal):
        twice = 2.0 * k
        up = jnp.concatenate([twice, jnp.where(self.top, 0.0, twice)], axis=1)
        down = jnp.concatenate([jnp.where(self.floor, 0.0, twice), twice], axis=1)
        return lambda v: up * self.zp(v) + down * self.zm(v), inverse(diagonal + (up + down))


def kernel(
    n_gx,
    n_gy,
    f_hbm,
    ph_hbm,
    el_hbm,
    pl_hbm,
    of_ref,
    op_ref,
    f_in,
    f_32,
    ph_in,
    el_in,
    pl_in,
    own_b,
    send_b,
    send_g,
    recv_b,
    recv_g,
    recv_c,
    merge_ref,
    late_ref,
    send_sem,
    recv_sem,
):
    gx = lax.axis_index("gx")
    gy = lax.axis_index("gy")

    def exists(offset):
        found = []
        for place, move, count in ((gx, offset[0], n_gx), (gy, offset[1], n_gy)):
            if move < 0:
                found.append(place > 0)
            if move > 0:
                found.append(place < count - 1)
        return functools.reduce(jnp.logical_and, found)

    def at(offset):
        return (gx + offset[0], gy + offset[1])

    barrier = pltpu.get_barrier_semaphore()
    expected = jnp.int32(0)
    for offset in ALL:

        @pl.when(exists(offset))
        def _(offset=offset):
            pl.semaphore_signal(barrier, inc=1, device_id=at(offset), device_id_type=MESH)

        expected = expected + exists(offset).astype(jnp.int32)

    loads = [
        pltpu.make_async_copy(src, dst, send_sem.at[i])
        for i, (src, dst) in enumerate(((ph_hbm, ph_in), (el_hbm, el_in), (f_hbm, f_in), (pl_hbm, pl_in)))
    ]
    for load in loads:
        load.start()

    for i, offset in enumerate(SIDES_Y):

        @pl.when(jnp.logical_not(exists(offset)))
        def _(i=i):
            recv_b[i] = jnp.zeros(recv_b.shape[1:], jnp.float32)

    for i, offset in enumerate(SIDES_X):

        @pl.when(jnp.logical_not(exists(offset)))
        def _(i=i):
            recv_g[i] = jnp.zeros(recv_g.shape[1:], jnp.float32)

    for i, offset in enumerate(CORNERS):

        @pl.when(jnp.logical_not(exists(offset)))
        def _(i=i):
            recv_c[i] = jnp.zeros(recv_c.shape[1:], jnp.float32)

    for load in loads:
        load.wait()
    maps = [ph_in[...].astype(jnp.float32), el_in[0].astype(jnp.float32), el_in[1].astype(jnp.float32)]
    drop, on0, on1 = [periodic_columns(m) for m in maps]
    near = edge_columns(f_in[...].astype(jnp.float32))
    place = lanes((X, C)) % 8
    send_b[0, 0] = jnp.where(place >= 4, near[0], roll_last(drop, -4))
    send_b[0, 1] = jnp.where(place >= 4, near[1], jnp.where(place == 0, roll_last(on1, -4), roll_last(on0, -3)))
    send_b[1, 0] = jnp.where(place < 4, near[0], roll_last(drop, 4))
    send_b[1, 1] = jnp.where(place < 4, near[1], jnp.where(place == 7, roll_last(on1, 4), roll_last(on0, 3)))
    own_row = lax.broadcasted_iota(jnp.int32, (8, C), 0) == lanes((8, C)) // 16
    for side in range(2):
        near, far = ((0, 1), (3, 2))[side]
        for s in range(2):
            for f in range(2):
                first = (s * 2 + f) * Z
                a = pl_in[pl.ds(4 * first + near, Z, stride=4), :]
                b = pl_in[pl.ds(4 * first + far, Z, stride=4), :]
                send_g[side, first : first + Z, :] = a + 0.5 * (a - b)
    for side in range(2):
        for row in range(4):
            halves = rows_of(send_g, (side,), row * Z, 2)
            for h in range(2):
                spread = pltpu.roll(halves[h], 8, 1, stride=16, stride_axis=0)
                spread = jnp.sum(jnp.where(own_row, spread, 0.0), axis=0, keepdims=True)
                send_g[side, 64 + 2 * row + h : 65 + 2 * row + h, :] = spread

    pl.semaphore_wait(barrier, expected)

    def copy_of(i, offset):
        back = (-offset[0], -offset[1])
        if offset in CORNERS:
            src = send_g.at[(offset[0] + 1) // 2, pl.ds(64, 8)]
            dst = recv_c.at[CORNERS.index(back)]
        elif offset in SIDES_Y:
            src = send_b.at[(offset[1] + 1) // 2]
            dst = recv_b.at[SIDES_Y.index(back)]
        else:
            src = send_g.at[(offset[0] + 1) // 2]
            dst = recv_g.at[SIDES_X.index(back)]
        return pltpu.make_async_remote_copy(
            src_ref=src,
            dst_ref=dst,
            send_sem=send_sem.at[i],
            recv_sem=recv_sem.at[ALL.index(back)],
            device_id=at(offset),
            device_id_type=MESH,
        )

    for i, offset in enumerate(ALL):

        @pl.when(exists(offset))
        def _(i=i, offset=offset):
            copy_of(i, offset).start()

    for i in range(3):
        own_b[4 + i] = packed_map(maps[i])
    own_b[0:4] = packed_columns(f_in[...].astype(jnp.float32)).reshape(4, X, C)

    def wait_from(offset):
        back = (-offset[0], -offset[1])

        @pl.when(exists(offset))
        def _():
            copy_of(ALL.index(back), back).wait_recv()

    for f in range(2):
        layers = f_in[f].astype(jnp.float32)
        for z in range(Z):
            f_32[f, PITCH * z : PITCH * z + X, :] = layers[z]
    planes_x = lambda f: jnp.stack([rows_of(f_32, (f,), x, 2 * PITCH) for x in range(X)], axis=0)
    rows = lambda v: jnp.broadcast_to(v[:, None, None, :], (X, 1, 8, C))
    half = lax.broadcasted_iota(jnp.int32, (1, 2, 1, 1), 1)
    height = 2 * lax.broadcasted_iota(jnp.int32, (1, 1, 8, C), 2) + half
    decay = jnp.exp(-4.0 * height.astype(jnp.float32) / Z)
    columns = OwnColumns(rows(maps[0]), [rows(maps[1]), rows(maps[2])], planes_x(0), planes_x(1), decay)
    columns.before()
    for offset in SIDES_X + SIDES_Y:
        wait_from(offset)

    def trace_own(step, field, side):
        return rows_of(recv_g, (side,), (step * 2 + field) * Z, 2)[None]

    rest = columns.after(trace_own)
    next(rest)
    grid = Strips((gy > 0).astype(jnp.float32), (gy < n_gy - 1).astype(jnp.float32))
    inner = grid.column[0] < 8

    def strip(outer, own):
        return jnp.stack([jnp.where(inner, outer[0], own), jnp.where(inner, own, outer[1])], axis=0)

    def halo(side, field):
        v = rows_of(recv_b, (side, field), 0, 2)
        return jnp.stack([roll_last(v, 4), roll_last(v, -4)], axis=0)

    def own_strip(i):
        return rows_of(own_b, (i,), 0, 2)

    def map_strip(field, own, turns):
        outer = [roll_last(rows_of(recv_b, (side, field), 0, 2), turns[side])[None] for side in range(2)]
        return strip(outer, own_strip(own)[None])

    def trace_strip(step, field):
        row = (step * 2 + field) * 2
        halves = []
        for i in range(2):
            mid = recv_g[i, 64 + row : 66 + row, :]
            low = jnp.where(inner[0, 0], recv_c[2 * i, row : row + 2, :], mid)
            high = jnp.where(inner[0, 0], mid, recv_c[2 * i + 1, row : row + 2, :])
            halves.append(jnp.broadcast_to(jnp.stack([low, high], axis=0)[:, :, None, :], (2, 2, 8, C)))
        return jnp.stack(halves, axis=2)

    next(rest)
    fields = [
        strip([halo(side, f) for side in range(2)], jnp.stack([own_strip(2 * f), own_strip(2 * f + 1)], axis=0))
        for f in range(2)
    ]
    drop = map_strip(0, 4, (0, 0))
    on0 = map_strip(1, 5, (1, -1))
    on1 = map_strip(1, 6, (0, 0))
    work = steps_of(
        drop,
        [on0, on1],
        fields[0],
        fields[1],
        grid.decay,
        grid,
    )
    for _ in rest:
        next(work)
    early, late = columns.states
    for f in range(2):
        for h in range(2):
            for x in range(X):
                late_ref[f, pl.ds(PITCH * x + h, 8, stride=2), :] = late[f].values[x, h]
            for p, x in enumerate((0, 1, X - 2, X - 1)):
                op_ref[0, f, pl.ds(p + 4 * h, 8, stride=8), :] = early[f].values[x, h]
    for i, offset in enumerate(ALL):

        @pl.when(exists(offset))
        def _(i=i, offset=offset):
            copy_of(i, offset).wait_send()

    for offset in CORNERS:
        wait_from(offset)
    lane = lanes((X, C))
    edge = (lane < 4) | (lane >= C - 4)

    def both_sides(state):
        return jnp.where(inner, state[1], state[0])

    def merge(field, state):
        state = both_sides(state)
        for h in range(2):
            for i in range(2):
                merge_ref[field, h, pl.ds(i, 8, stride=2), :] = state[h, i]
        for h in range(2):
            state = merge_ref[field, h]
            for j in range(8):
                z = 2 * j + h
                rows = slice(X * z, X * z + X)
                own = late_ref[field, pl.ds(z, X, stride=PITCH), :]
                value = jnp.where(edge, roll_last(state, -(16 * j + 8)), own)
                of_ref[field, rows, :] = value
                op_ref[1, field, 4 * z : 4 * z + 4, :] = jnp.concatenate([value[0:2], value[X - 2 :]], axis=0)

    four = []
    for state in work.send(trace_strip):
        state = both_sides(state)
        four += [state[:, 0, 0:1], state[:, 1, 0:1], state[:, 0, 7:8], state[:, 1, 7:8]]
    four = jnp.concatenate(four, axis=1)
    temper = next(work)
    for j in range(8):
        back = roll_last(four, -(16 * j + 8))
        for h in range(2):
            for f in range(2):
                rows = slice(4 * (2 * j + h), 4 * (2 * j + h) + 4)
                op_ref[0, f, rows, :] = jnp.where(edge[:4], back[h, 4 * f : 4 * f + 4], op_ref[0, f, rows, :])
    merge(0, temper)
    merge(1, next(work))


def write_out(f_ref, p_ref, of_hbm, op_hbm, sem):
    copies = [
        pltpu.make_async_copy(f_ref, of_hbm, sem.at[0]),
        pltpu.make_async_copy(p_ref, op_hbm, sem.at[1]),
    ]
    for copy in copies:
        copy.start()
    for copy in copies:
        copy.wait()


def solution(mesh):
    n_gx = mesh.shape["gx"]
    n_gy = mesh.shape["gy"]

    def shards(fields, phase, electrode, planes):
        in_hbm = pl.BlockSpec(memory_space=pltpu.HBM)
        vmem = pl.BlockSpec(memory_space=pltpu.VMEM)
        made = pl.pallas_call(
            functools.partial(kernel, n_gx, n_gy),
            out_shape=(
                jax.ShapeDtypeStruct((2, Z * X, C), jnp.float32),
                jax.ShapeDtypeStruct((2, 2, Z * 4, C), jnp.float32),
            ),
            in_specs=[in_hbm] * 4,
            out_specs=(vmem, vmem),
            scratch_shapes=[
                pltpu.VMEM((2, Z, X, C), jnp.bfloat16),
                pltpu.VMEM((2, Z * PITCH, C), jnp.float32),
                pltpu.VMEM((X, C), jnp.int32),
                pltpu.VMEM((2, X, C), jnp.int32),
                pltpu.VMEM((2 * 2 * Z * 4, C), jnp.float32),
                pltpu.VMEM((7, X, C), jnp.float32),
                pltpu.VMEM((2, 2, X, C), jnp.float32),
                pltpu.VMEM((2, 72, C), jnp.float32),
                pltpu.VMEM((2, 2, X, C), jnp.float32),
                pltpu.VMEM((2, 72, C), jnp.float32),
                pltpu.VMEM((4, 8, C), jnp.float32),
                pltpu.VMEM((2, 2, X, C), jnp.float32),
                pltpu.VMEM((2, PITCH * X, C), jnp.float32),
                pltpu.SemaphoreType.DMA((8,)),
                pltpu.SemaphoreType.DMA((8,)),
            ],
            compiler_params=pltpu.CompilerParams(
                collective_id=0, has_side_effects=True, vmem_limit_bytes=32 * 1024 * 1024
            ),
        )(*[pltpu.with_memory_space_constraint(v, pltpu.HBM) for v in (fields, phase, electrode, planes.reshape(2 * 2 * Z * 4, C))])
        new_fields, new_planes = pl.pallas_call(
            write_out,
            out_shape=(
                pltpu.HBM((2, Z * X, C), jnp.float32),
                pltpu.HBM((2, 2, Z * 4, C), jnp.float32),
            ),
            in_specs=[vmem, vmem],
            out_specs=(in_hbm, in_hbm),
            scratch_shapes=[pltpu.SemaphoreType.DMA((2,))],
        )(*[pltpu.with_memory_space_constraint(v, pltpu.VMEM) for v in made])
        return new_fields.reshape(2, Z, X, C), new_planes.reshape(2, 2, Z, 4, C)

    placed = (
        P(None, None, "gx", "gy"),
        P("gx", "gy"),
        P(None, "gx", "gy"),
        P(None, None, None, "gx", "gy"),
    )
    return jax.shard_map(
        shards,
        mesh=mesh,
        in_specs=placed,
        out_specs=(P(None, None, "gx", "gy"), P(None, None, None, "gx", "gy")),
        check_vma=False,
    )
```

```python
import functools

import jax
import jax.numpy as jnp
from jax import lax
from jax.experimental import pallas as pl
from jax.experimental.pallas import tpu as pltpu
from jax.sharding import PartitionSpec as P

MESH = pl.DeviceIdType.MESH
cond_oil = 0.6
cond_drop = 2.0
diff_oil = 0.3
diff_drop = 1.0
thermal_slope = 0.3
cheb_radius = 0.95
cheb_ratio = 1.0 / cheb_radius
rho_first = 1.0 / cheb_ratio
rho_second = 1.0 / (2.0 * cheb_ratio - rho_first)
log2_e = 1.4426950408889634
keep_old = rho_second * rho_first
take_new = 2.0 * rho_second / cheb_radius

Z = 16
X = 16
C = 128
PITCH = 17
CORNERS = ((-1, -1), (-1, 1), (1, -1), (1, 1))
SIDES_Y = ((0, -1), (0, 1))
SIDES_X = ((-1, 0), (1, 0))
ALL = CORNERS + SIDES_Y + SIDES_X


def lanes(shape):
    return lax.broadcasted_iota(jnp.int32, shape, len(shape) - 1)


def roll_last(v, shift):
    return pltpu.roll(v, shift % C, v.ndim - 1)


def roll_rows(v, shift):
    return pltpu.roll(v, shift % 8, v.ndim - 2)


def rows_of(ref, index, start, step):
    at = lambda first: ref[(*index, pl.ds(first, 8, stride=step), slice(None))]
    return jnp.stack([at(start), at(start + step // 2)], axis=0)


def next_of(v, axis, turn):
    even, odd = lax.slice_in_dim(v, 0, 1, axis=axis), lax.slice_in_dim(v, 1, 2, axis=axis)
    return jnp.concatenate([odd, turn(even)], axis=axis)


def previous_of(v, axis, turn):
    even, odd = lax.slice_in_dim(v, 0, 1, axis=axis), lax.slice_in_dim(v, 1, 2, axis=axis)
    return jnp.concatenate([turn(odd), even], axis=axis)


def faces_of(k, axis, forth, back, last, first):
    even, odd = lax.slice_in_dim(k, 0, 1, axis=axis), lax.slice_in_dim(k, 1, 2, axis=axis)
    inner = even + odd
    up = jnp.where(last, 0.0, odd + forth(even))
    down = jnp.where(first, 0.0, even + back(odd))
    return jnp.concatenate([inner, up], axis=axis), jnp.concatenate([down, inner], axis=axis)


def packed_columns(v):
    head = v.shape[:-3]
    v = v.reshape(head + (8, 2, X, C))
    lane = lanes(head + (2, X, C))
    out = None
    for j in range(8):
        moved = roll_last(v[..., j, :, :, :], 16 * j + 8)
        out = moved if out is None else jnp.where(lane >= 16 * j, moved, out)
    return out


def packed_map(v):
    base = jnp.where(lanes(v.shape) < 16, roll_last(v, 8), 0.0)
    base = base + roll_last(base, 16)
    base = base + roll_last(base, 32)
    return base + roll_last(base, 64)


def periodic_columns(v):
    base = jnp.where(lanes(v.shape) < 8, roll_last(v, 4), 0.0)
    for shift in (8, 16, 32, 64):
        base = base + roll_last(base, shift)
    return base


def edge_columns(v):
    lane = lanes(v.shape[:-3] + (X, C))
    out = None
    for z in range(Z):
        moved = roll_last(v[..., z, :, :], 8 * z + 4)
        out = moved if out is None else jnp.where(lane >= 8 * z, moved, out)
    return out


def inverse(v):
    guess = pl.reciprocal(v, approx=True)
    return guess * (2.0 - v * guess)


def steps_of(droplet, active, old_t, old_n, decay, grid):
    def sweep(v, target, faces):
        px, mx, py, my, z_part = faces
        along = px * grid.xp(v) + mx * grid.xm(v)
        across = py * grid.yp(v) + my * grid.ym(v)
        return (target + along) + (across + z_part(v))

    def sides(k):
        return (*grid.x_faces(k), *grid.y_faces(k))

    def coefficients(k):
        px, mx, py, my = sides(k)
        z_part, z_total = grid.layers(k)
        robin = k * grid.edge4
        diagonal = (1.0 + robin) + (px + mx) + (py + my) + z_total
        return (px, mx, py, my, z_part), robin, inverse(diagonal)

    def heat_coefficients(k):
        px, mx, py, my = sides(k)
        robin = k * grid.edge4
        diagonal = (1.0 + robin) + (px + mx) + (py + my)
        z_part, inv = grid.even_layers(k, diagonal)
        return (px, mx, py, my, z_part), robin, inv

    ion_base = diff_oil + (diff_drop - diff_oil) * droplet
    heat_faces, heat_robin, heat_inv = heat_coefficients(cond_oil + (cond_drop - cond_oil) * droplet)
    heating = [(0.5 * (e * droplet)) * decay for e in active]

    def open_step(step, old_t, old_n):
        ions = ion_base * jnp.exp2((thermal_slope * log2_e) * old_t)
        target_t = old_t + heating[step] * (2.0 + old_n * old_n)
        ion_faces, ion_robin, ion_inv = coefficients(ions)
        if step == 0:
            yield
        return (
            (old_t, target_t, sweep(old_t, target_t, heat_faces), heat_faces, heat_robin, heat_inv),
            (old_n, old_n, sweep(old_n, old_n, ion_faces), ion_faces, ion_robin, ion_inv),
        )

    def close_field(parts, step, field, trace):
        old, target, total, faces, robin, inv = parts[field]
        given = robin * trace(step, field)
        first = (total + given) * inv
        return sweep(first, target + given, faces) * (take_new * inv) - keep_old * old

    yield
    parts = yield from open_step(0, old_t, old_n)
    trace = yield
    early = [close_field(parts, 0, field, trace) for field in range(2)]
    yield early
    parts = yield from open_step(1, *early)
    for field in range(2):
        yield close_field(parts, 1, field, trace)


class Span:
    def __init__(self, values, start):
        self.values, self.start = values, start

    def __call__(self, lo, hi):
        return self.values[lo - self.start : hi - self.start]


def gathered(function, lo, hi, size=4):
    return Span(jnp.concatenate([function(a, min(a + size, hi)) for a in range(lo, hi, size)], axis=0), lo)


def joined(*spans):
    return Span(jnp.concatenate([span.values for span in spans], axis=0), spans[0].start)


def x_sum(face, v, lo, hi):
    top, low = min(hi, X - 1), max(lo - 1, 0)
    up = face(lo, top)
    down = face(low, hi - 1)
    if v is not None:
        up = up * v(lo + 1, top + 1)
        down = down * v(low, hi - 1)
    first, last = max(lo, 1), top
    parts = [up[:1]] if lo == 0 else []
    if last > first:
        parts.append(up[first - lo : last - lo] + down[first - low - 1 : last - low - 1])
    if hi == X:
        parts.append(down[-1:])
    return jnp.concatenate(parts, axis=0)


class OwnColumns:
    def __init__(self, droplet, active, temper, ions, decay):
        self.olds = [[Span(temper, 0), Span(ions, 0)]]
        both = lambda v: jnp.concatenate([v, v], axis=1)
        heat = cond_oil + (cond_drop - cond_oil) * droplet
        self.ion_base = both(diff_oil + (diff_drop - diff_oil) * droplet)
        self.heating = [Span(both(0.5 * (e * droplet)) * decay, 0) for e in active]
        face = Span(heat[1:] + heat[:-1], 0)
        py = heat + roll_last(heat, -1)
        my = roll_last(py, 1)
        edge = jnp.concatenate([heat[:1], jnp.zeros_like(heat[1:-1]), heat[-1:]], axis=0)
        base = (1.0 + 4.0 * edge) + x_sum(face, None, 0, X) + (py + my)
        row = lax.broadcasted_iota(jnp.int32, (1, 1, 8, 1), 2)
        self.high, self.low = row == 7, row == 0
        pz = jnp.concatenate([2.0 * heat, jnp.where(self.high, 0.0, 2.0 * heat)], axis=1)
        mz = jnp.concatenate([jnp.where(self.low, 0.0, 2.0 * heat), 2.0 * heat], axis=1)
        heat_faces = (Span(both(face.values), 0), Span(both(py), 0), Span(both(my), 0), Span(pz, 0), Span(mz, 0))
        self.heat = (heat_faces, Span(inverse(both(base) + (pz + mz)), 0), Span(both(heat), 0))
        self.states = []

    def ion_parts(self, temper, lo, hi):
        k = self.ion_base[lo:hi] * jnp.exp2((thermal_slope * log2_e) * temper(lo, hi))
        pz, mz = faces_of(k, 1, lambda u: roll_rows(u, -1), lambda u: roll_rows(u, 1), self.high, self.low)
        return k, k + roll_last(k, -1), k + roll_last(k, 1), pz, mz

    def ion_spans(self, temper, lo, hi):
        parts = [self.ion_parts(temper, a, min(a + 4, hi)) for a in range(lo, hi, 4)]
        return [Span(jnp.concatenate(p, axis=0), lo) for p in zip(*parts)]

    def ion_inverse(self, spans, face, lo, hi):
        def part(a, b):
            k, py, my, pz, mz = [v(a, b) for v in spans]
            total = (1.0 + x_sum(face, None, a, b)) + (py + my) + (pz + mz)
            if a == 0:
                total = jnp.concatenate([total[:1] + 4.0 * k[:1], total[1:]], axis=0)
            if b == X:
                total = jnp.concatenate([total[:-1], total[-1:] + 4.0 * k[-1:]], axis=0)
            return inverse(total)

        return gathered(part, lo, hi)

    def sweep(self, v, target, faces, a, b):
        face, py, my, pz, mz = faces
        mid = v(a, b)
        across = py(a, b) * roll_last(mid, -1) + my(a, b) * roll_last(mid, 1)
        above = next_of(mid, 1, lambda u: roll_rows(u, -1))
        below = previous_of(mid, 1, lambda u: roll_rows(u, 1))
        upright = pz(a, b) * above + mz(a, b) * below
        return (target(a, b) + x_sum(face, v, a, b)) + (across + upright)

    def targets(self, step, old, lo, hi):
        heated = lambda a, b: old[0](a, b) + self.heating[step](a, b) * (2.0 + old[1](a, b) * old[1](a, b))
        return [gathered(heated, lo, hi), Span(old[1](lo, hi), lo)]

    def last(self, old, target, first, faces, inv, lo, hi):
        def part(a, b):
            return self.sweep(first, target, faces, a, b) * (take_new * inv(a, b)) - keep_old * old(a, b)

        return gathered(part, lo, hi)

    def partial(self, v, target, faces, x, inner, between):
        face, py, my, pz, mz = faces
        mid = v(x, x + 1)
        across = py(x, x + 1) * roll_last(mid, -1) + my(x, x + 1) * roll_last(mid, 1)
        above = next_of(mid, 1, lambda u: roll_rows(u, -1))
        below = previous_of(mid, 1, lambda u: roll_rows(u, 1))
        upright = pz(x, x + 1) * above + mz(x, x + 1) * below
        return (target(x, x + 1) + face(between, between + 1) * v(inner, inner + 1)) + (across + upright)

    def before(self):
        old = self.olds[0]
        self.near1, self.near2, self.near3 = [], [], []
        spans = self.ion_spans(old[0], 0, X)
        face = Span(spans[0].values[1:] + spans[0].values[:-1], 0)
        ion = ((face, *spans[1:]), self.ion_inverse(spans, face, 0, X), spans[0])
        self.sets0 = (self.heat, ion)
        self.target0 = self.targets(0, old, 0, X)
        self.total0, self.first0, self.mid1 = [], [], []
        for f in range(2):
            faces, inv, k = self.sets0[f]
            total = gathered(lambda a, b: self.sweep(old[f], self.target0[f], faces, a, b), 0, X)
            first = gathered(lambda a, b: total(a, b) * inv(a, b), 1, X - 1)
            self.total0.append(total)
            self.first0.append(first)
            self.mid1.append(self.last(old[f], self.target0[f], first, faces, inv, 2, X - 2))
            near = []
            for x, inner, between, opened in ((1, 2, 1, 0), (X - 2, X - 3, X - 3, X - 2)):
                scale = take_new * inv(x, x + 1)
                base = self.partial(first, self.target0[f], faces, x, inner, between)
                near.append((base * scale - keep_old * old[f](x, x + 1), faces[0](opened, opened + 1) * scale))
            self.near1.append(near)
        new = self.mid1
        self.spans1 = self.ion_spans(new[0], 2, X - 2)
        k = self.spans1[0]
        self.face1 = Span(k.values[1:] + k.values[:-1], 2)
        self.inv1 = self.ion_inverse(self.spans1, self.face1, 3, X - 3)
        self.target1 = self.targets(1, new, 2, X - 2)
        sets = ((self.heat[0], self.heat[1]), ((self.face1, *self.spans1[1:]), self.inv1))
        self.first1, self.mid2 = [], []
        for f in range(2):
            faces, inv = sets[f]
            first = gathered(lambda a, b: self.sweep(new[f], self.target1[f], faces, a, b) * inv(a, b), 3, X - 3)
            self.first1.append(first)
            self.mid2.append(self.last(new[f], self.target1[f], first, faces, inv, 4, X - 4))
            near = []
            for x, inner, between, opened in ((2, 3, 2, 1), (X - 3, X - 4, X - 4, X - 3)):
                base = self.partial(new[f], self.target1[f], faces, x, inner, between)
                if f == 0:
                    near.append((base * inv(x, x + 1), faces[0](opened, opened + 1) * inv(x, x + 1)))
                else:
                    rest = [part(x, x + 1) for part in faces[1:]]
                    total = (1.0 + faces[0](between, between + 1)) + (rest[0] + rest[1]) + (rest[2] + rest[3])
                    near.append((base, total))
            self.near2.append(near)
            near = []
            for x, inner, between, opened in ((3, 4, 3, 2), (X - 4, X - 5, X - 5, X - 4)):
                scale = take_new * inv(x, x + 1)
                base = self.partial(first, self.target1[f], faces, x, inner, between)
                near.append((base * scale - keep_old * new[f](x, x + 1), faces[0](opened, opened + 1) * scale))
            self.near3.append(near)

    def after(self, trace):
        old = self.olds[0]
        news = []
        for f in range(2):
            faces, inv, k = self.sets0[f]
            ends, target = [], self.target0[f].values
            for side, x in ((0, 0), (1, X - 1)):
                given = 4.0 * k(x, x + 1) * trace(0, f, side)
                ends.append((self.total0[f](x, x + 1) + given) * inv(x, x + 1))
                target = (
                    jnp.concatenate([target[:1] + given, target[1:]], axis=0)
                    if side == 0
                    else jnp.concatenate([target[:-1], target[-1:] + given], axis=0)
                )
            first = Span(jnp.concatenate([ends[0], self.first0[f].values, ends[1]], axis=0), 0)
            target = Span(target, 0)
            (low, low_face), (high, high_face) = self.near1[f]
            low = Span(low + low_face * ends[0], 1)
            high = Span(high + high_face * ends[1], X - 2)
            lowest = self.last(old[f], target, first, faces, inv, 0, 1)
            highest = self.last(old[f], target, first, faces, inv, X - 1, X)
            news.append(joined(lowest, low, self.mid1[f], high, highest))
            yield
        low, high = self.ion_spans(news[0], 0, 2), self.ion_spans(news[0], X - 2, X)
        spans = [joined(a, b, c) for a, b, c in zip(low, self.spans1, high)]
        k = spans[0].values
        face = Span(
            jnp.concatenate([k[1:3] + k[0:2], self.face1.values, k[X - 2 :] + k[X - 3 : X - 1]], axis=0), 0
        )
        reached = [
            inverse(self.near2[1][side][1] + face(between, between + 1)) for side, between in ((0, 1), (1, X - 3))
        ]
        inv = joined(
            self.ion_inverse(spans, face, 0, 2),
            Span(reached[0], 2),
            self.inv1,
            Span(reached[1], X - 3),
            self.ion_inverse(spans, face, X - 2, X),
        )
        yield
        lows, highs = self.targets(1, news, 0, 2), self.targets(1, news, X - 2, X)
        ends = []
        for f, (faces, inv, k) in enumerate((self.heat, ((face, *spans[1:]), inv, spans[0]))):
            target = joined(lows[f], self.target1[f], highs[f]).values
            target = Span(
                jnp.concatenate(
                    [
                        target[:1] + 4.0 * k(0, 1) * trace(1, f, 0),
                        target[1:-1],
                        target[-1:] + 4.0 * k(X - 1, X) * trace(1, f, 1),
                    ],
                    axis=0,
                ),
                0,
            )
            part = lambda a, b: self.sweep(news[f], target, faces, a, b) * inv(a, b)
            at2 = []
            for side, x, beside, between in ((0, 2, 1, 1), (1, X - 3, X - 2, X - 3)):
                base, other = self.near2[f][side]
                given = news[f](beside, beside + 1)
                if f == 0:
                    at2.append(base + other * given)
                else:
                    at2.append((base + face(between, between + 1) * given) * inv(x, x + 1))
            first = joined(
                gathered(part, 0, 2), Span(at2[0], 2), self.first1[f], Span(at2[1], X - 3), gathered(part, X - 2, X)
            )
            (low, low_face), (high, high_face) = self.near3[f]
            at3 = [low + low_face * at2[0], high + high_face * at2[1]]
            ends.append(
                joined(
                    self.last(news[f], target, first, faces, inv, 0, 3),
                    Span(at3[0], 3),
                    self.mid2[f],
                    Span(at3[1], X - 4),
                    self.last(news[f], target, first, faces, inv, X - 3, X),
                )
            )
            yield
        self.states = news, ends


class Strips:
    def __init__(self, left_open, right_open):
        self.lane = lanes((1, 1, 1, 1, C))
        self.column = self.lane % 16
        row = lax.broadcasted_iota(jnp.int32, (1, 1, 1, 8, 1), 3)
        half_x = lax.broadcasted_iota(jnp.int32, (1, 1, 2, 1, 1), 2)
        half_z = lax.broadcasted_iota(jnp.int32, (1, 2, 1, 1, 1), 1)
        side = lax.broadcasted_iota(jnp.int32, (2, 1, 1, 1, 1), 0)
        self.low, self.high = row == 0, row == 7
        self.floor, self.top = self.lane < 16, self.lane >= 112
        self.edge4 = jnp.where(2 * row + half_x == 0, 4.0, 0.0) + jnp.where(2 * row + half_x == X - 1, 4.0, 0.0)
        opened = jnp.where(side == 0, left_open, right_open)
        self.between_up = jnp.where(self.column == 7, opened, 1.0)
        self.between_down = jnp.where(self.column == 8, opened, 1.0)
        self.decay = jnp.exp(-4.0 * (2 * (self.lane // 16) + half_z).astype(jnp.float32) / Z)

    def xp(self, v):
        return next_of(v, 2, lambda u: roll_rows(u, -1))

    def xm(self, v):
        return previous_of(v, 2, lambda u: roll_rows(u, 1))

    def yp(self, v):
        return roll_last(v, -1)

    def ym(self, v):
        return roll_last(v, 1)

    def zp(self, v):
        return next_of(v, 1, lambda u: roll_last(u, -16))

    def zm(self, v):
        return previous_of(v, 1, lambda u: roll_last(u, 16))

    def x_faces(self, k):
        return faces_of(k, 2, lambda u: roll_rows(u, -1), lambda u: roll_rows(u, 1), self.high, self.low)

    def y_faces(self, k):
        return (k + self.yp(k)) * self.between_up, (k + self.ym(k)) * self.between_down

    def layers(self, k):
        up, down = faces_of(k, 1, lambda u: roll_last(u, -16), lambda u: roll_last(u, 16), self.top, self.floor)
        return lambda v: up * self.zp(v) + down * self.zm(v), up + down

    def even_layers(self, k, diagonal):
        twice = 2.0 * k
        up = jnp.concatenate([twice, jnp.where(self.top, 0.0, twice)], axis=1)
        down = jnp.concatenate([jnp.where(self.floor, 0.0, twice), twice], axis=1)
        return lambda v: up * self.zp(v) + down * self.zm(v), inverse(diagonal + (up + down))


def kernel(
    n_gx,
    n_gy,
    f_hbm,
    ph_hbm,
    el_hbm,
    pl_hbm,
    of_ref,
    op_ref,
    f_in,
    f_32,
    ph_in,
    el_in,
    pl_in,
    own_b,
    send_b,
    send_g,
    recv_b,
    recv_g,
    recv_c,
    merge_ref,
    late_ref,
    send_sem,
    recv_sem,
):
    gx = lax.axis_index("gx")
    gy = lax.axis_index("gy")

    def exists(offset):
        found = []
        for place, move, count in ((gx, offset[0], n_gx), (gy, offset[1], n_gy)):
            if move < 0:
                found.append(place > 0)
            if move > 0:
                found.append(place < count - 1)
        return functools.reduce(jnp.logical_and, found)

    def at(offset):
        return (gx + offset[0], gy + offset[1])

    barrier = pltpu.get_barrier_semaphore()
    expected = jnp.int32(0)
    for offset in ALL:

        @pl.when(exists(offset))
        def _(offset=offset):
            pl.semaphore_signal(barrier, inc=1, device_id=at(offset), device_id_type=MESH)

        expected = expected + exists(offset).astype(jnp.int32)

    loads = [
        pltpu.make_async_copy(src, dst, send_sem.at[i])
        for i, (src, dst) in enumerate(((ph_hbm, ph_in), (el_hbm, el_in), (f_hbm, f_in), (pl_hbm, pl_in)))
    ]
    for load in loads:
        load.start()

    for i, offset in enumerate(SIDES_Y):

        @pl.when(jnp.logical_not(exists(offset)))
        def _(i=i):
            recv_b[i] = jnp.zeros(recv_b.shape[1:], jnp.float32)

    for i, offset in enumerate(SIDES_X):

        @pl.when(jnp.logical_not(exists(offset)))
        def _(i=i):
            recv_g[i] = jnp.zeros(recv_g.shape[1:], jnp.float32)

    for i, offset in enumerate(CORNERS):

        @pl.when(jnp.logical_not(exists(offset)))
        def _(i=i):
            recv_c[i] = jnp.zeros(recv_c.shape[1:], jnp.float32)

    for load in loads:
        load.wait()
    maps = [ph_in[...].astype(jnp.float32), el_in[0].astype(jnp.float32), el_in[1].astype(jnp.float32)]
    drop, on0, on1 = [periodic_columns(m) for m in maps]
    near = edge_columns(f_in[...].astype(jnp.float32))
    place = lanes((X, C)) % 8
    send_b[0, 0] = jnp.where(place >= 4, near[0], roll_last(drop, -4))
    send_b[0, 1] = jnp.where(place >= 4, near[1], jnp.where(place == 0, roll_last(on1, -4), roll_last(on0, -3)))
    send_b[1, 0] = jnp.where(place < 4, near[0], roll_last(drop, 4))
    send_b[1, 1] = jnp.where(place < 4, near[1], jnp.where(place == 7, roll_last(on1, 4), roll_last(on0, 3)))
    own_row = lax.broadcasted_iota(jnp.int32, (8, C), 0) == lanes((8, C)) // 16
    for side in range(2):
        near, far = ((0, 1), (3, 2))[side]
        for s in range(2):
            for f in range(2):
                first = (s * 2 + f) * Z
                a = pl_in[pl.ds(4 * first + near, Z, stride=4), :]
                b = pl_in[pl.ds(4 * first + far, Z, stride=4), :]
                send_g[side, first : first + Z, :] = a + 0.5 * (a - b)
    for side in range(2):
        for row in range(4):
            halves = rows_of(send_g, (side,), row * Z, 2)
            for h in range(2):
                spread = pltpu.roll(halves[h], 8, 1, stride=16, stride_axis=0)
                spread = jnp.sum(jnp.where(own_row, spread, 0.0), axis=0, keepdims=True)
                send_g[side, 64 + 2 * row + h : 65 + 2 * row + h, :] = spread

    pl.semaphore_wait(barrier, expected)

    def copy_of(i, offset):
        back = (-offset[0], -offset[1])
        if offset in CORNERS:
            src = send_g.at[(offset[0] + 1) // 2, pl.ds(64, 8)]
            dst = recv_c.at[CORNERS.index(back)]
        elif offset in SIDES_Y:
            src = send_b.at[(offset[1] + 1) // 2]
            dst = recv_b.at[SIDES_Y.index(back)]
        else:
            src = send_g.at[(offset[0] + 1) // 2]
            dst = recv_g.at[SIDES_X.index(back)]
        return pltpu.make_async_remote_copy(
            src_ref=src,
            dst_ref=dst,
            send_sem=send_sem.at[i],
            recv_sem=recv_sem.at[ALL.index(back)],
            device_id=at(offset),
            device_id_type=MESH,
        )

    for i, offset in enumerate(ALL):

        @pl.when(exists(offset))
        def _(i=i, offset=offset):
            copy_of(i, offset).start()

    for i in range(3):
        own_b[4 + i] = packed_map(maps[i])
    own_b[0:4] = packed_columns(f_in[...].astype(jnp.float32)).reshape(4, X, C)

    def wait_from(offset):
        back = (-offset[0], -offset[1])

        @pl.when(exists(offset))
        def _():
            copy_of(ALL.index(back), back).wait_recv()

    for f in range(2):
        layers = f_in[f].astype(jnp.float32)
        for z in range(Z):
            f_32[f, PITCH * z : PITCH * z + X, :] = layers[z]
    planes_x = lambda f: jnp.stack([rows_of(f_32, (f,), x, 2 * PITCH) for x in range(X)], axis=0)
    rows = lambda v: jnp.broadcast_to(v[:, None, None, :], (X, 1, 8, C))
    half = lax.broadcasted_iota(jnp.int32, (1, 2, 1, 1), 1)
    height = 2 * lax.broadcasted_iota(jnp.int32, (1, 1, 8, C), 2) + half
    decay = jnp.exp(-4.0 * height.astype(jnp.float32) / Z)
    columns = OwnColumns(rows(maps[0]), [rows(maps[1]), rows(maps[2])], planes_x(0), planes_x(1), decay)
    columns.before()
    for offset in SIDES_X + SIDES_Y:
        wait_from(offset)

    def trace_own(step, field, side):
        return rows_of(recv_g, (side,), (step * 2 + field) * Z, 2)[None]

    rest = columns.after(trace_own)
    next(rest)
    grid = Strips((gy > 0).astype(jnp.float32), (gy < n_gy - 1).astype(jnp.float32))
    inner = grid.column[0] < 8

    def strip(outer, own):
        return jnp.stack([jnp.where(inner, outer[0], own), jnp.where(inner, own, outer[1])], axis=0)

    def halo(side, field):
        v = rows_of(recv_b, (side, field), 0, 2)
        return jnp.stack([roll_last(v, 4), roll_last(v, -4)], axis=0)

    def own_strip(i):
        return rows_of(own_b, (i,), 0, 2)

    def map_strip(field, own, turns):
        outer = [roll_last(rows_of(recv_b, (side, field), 0, 2), turns[side])[None] for side in range(2)]
        return strip(outer, own_strip(own)[None])

    def trace_strip(step, field):
        row = (step * 2 + field) * 2
        halves = []
        for i in range(2):
            mid = recv_g[i, 64 + row : 66 + row, :]
            low = jnp.where(inner[0, 0], recv_c[2 * i, row : row + 2, :], mid)
            high = jnp.where(inner[0, 0], mid, recv_c[2 * i + 1, row : row + 2, :])
            halves.append(jnp.broadcast_to(jnp.stack([low, high], axis=0)[:, :, None, :], (2, 2, 8, C)))
        return jnp.stack(halves, axis=2)

    next(rest)
    fields = [
        strip([halo(side, f) for side in range(2)], jnp.stack([own_strip(2 * f), own_strip(2 * f + 1)], axis=0))
        for f in range(2)
    ]
    drop = map_strip(0, 4, (0, 0))
    on0 = map_strip(1, 5, (1, -1))
    on1 = map_strip(1, 6, (0, 0))
    work = steps_of(
        drop,
        [on0, on1],
        fields[0],
        fields[1],
        grid.decay,
        grid,
    )
    for _ in rest:
        next(work)
    early, late = columns.states
    for f in range(2):
        for h in range(2):
            for x in range(X):
                late_ref[f, pl.ds(PITCH * x + h, 8, stride=2), :] = late[f].values[x, h]
            for p, x in enumerate((0, 1, X - 2, X - 1)):
                op_ref[0, f, pl.ds(p + 4 * h, 8, stride=8), :] = early[f].values[x, h]
    for i, offset in enumerate(ALL):

        @pl.when(exists(offset))
        def _(i=i, offset=offset):
            copy_of(i, offset).wait_send()

    for offset in CORNERS:
        wait_from(offset)
    lane = lanes((X, C))
    edge = (lane < 4) | (lane >= C - 4)

    def both_sides(state):
        return jnp.where(inner, state[1], state[0])

    def merge(field, state):
        state = both_sides(state)
        for h in range(2):
            for i in range(2):
                merge_ref[field, h, pl.ds(i, 8, stride=2), :] = state[h, i]
        for h in range(2):
            state = merge_ref[field, h]
            for j in range(8):
                z = 2 * j + h
                rows = slice(X * z, X * z + X)
                own = late_ref[field, pl.ds(z, X, stride=PITCH), :]
                value = jnp.where(edge, roll_last(state, -(16 * j + 8)), own)
                of_ref[field, rows, :] = value
                op_ref[1, field, 4 * z : 4 * z + 4, :] = jnp.concatenate([value[0:2], value[X - 2 :]], axis=0)

    four = []
    for state in work.send(trace_strip):
        state = both_sides(state)
        four += [state[:, 0, 0:1], state[:, 1, 0:1], state[:, 0, 7:8], state[:, 1, 7:8]]
    four = jnp.concatenate(four, axis=1)
    temper = next(work)
    for j in range(8):
        back = roll_last(four, -(16 * j + 8))
        for h in range(2):
            for f in range(2):
                rows = slice(4 * (2 * j + h), 4 * (2 * j + h) + 4)
                op_ref[0, f, rows, :] = jnp.where(edge[:4], back[h, 4 * f : 4 * f + 4], op_ref[0, f, rows, :])
    merge(0, temper)
    merge(1, next(work))


def write_out(f_ref, p_ref, of_hbm, op_hbm, sem):
    copies = [
        pltpu.make_async_copy(f_ref, of_hbm, sem.at[0]),
        pltpu.make_async_copy(p_ref, op_hbm, sem.at[1]),
    ]
    for copy in copies:
        copy.start()
    for copy in copies:
        copy.wait()


def solution(mesh):
    n_gx = mesh.shape["gx"]
    n_gy = mesh.shape["gy"]

    def shards(fields, phase, electrode, planes):
        in_hbm = pl.BlockSpec(memory_space=pltpu.HBM)
        vmem = pl.BlockSpec(memory_space=pltpu.VMEM)
        made = pl.pallas_call(
            functools.partial(kernel, n_gx, n_gy),
            out_shape=(
                jax.ShapeDtypeStruct((2, Z * X, C), jnp.float32),
                jax.ShapeDtypeStruct((2, 2, Z * 4, C), jnp.float32),
            ),
            in_specs=[in_hbm] * 4,
            out_specs=(vmem, vmem),
            scratch_shapes=[
                pltpu.VMEM((2, Z, X, C), jnp.bfloat16),
                pltpu.VMEM((2, Z * PITCH, C), jnp.float32),
                pltpu.VMEM((X, C), jnp.int32),
                pltpu.VMEM((2, X, C), jnp.int32),
                pltpu.VMEM((2 * 2 * Z * 4, C), jnp.float32),
                pltpu.VMEM((7, X, C), jnp.float32),
                pltpu.VMEM((2, 2, X, C), jnp.float32),
                pltpu.VMEM((2, 72, C), jnp.float32),
                pltpu.VMEM((2, 2, X, C), jnp.float32),
                pltpu.VMEM((2, 72, C), jnp.float32),
                pltpu.VMEM((4, 8, C), jnp.float32),
                pltpu.VMEM((2, 2, X, C), jnp.float32),
                pltpu.VMEM((2, PITCH * X, C), jnp.float32),
                pltpu.SemaphoreType.DMA((8,)),
                pltpu.SemaphoreType.DMA((8,)),
            ],
            compiler_params=pltpu.CompilerParams(
                collective_id=0, has_side_effects=True, vmem_limit_bytes=32 * 1024 * 1024
            ),
        )(*[pltpu.with_memory_space_constraint(v, pltpu.HBM) for v in (fields, phase, electrode, planes.reshape(2 * 2 * Z * 4, C))])
        new_fields, new_planes = pl.pallas_call(
            write_out,
            out_shape=(
                pltpu.HBM((2, Z * X, C), jnp.float32),
                pltpu.HBM((2, 2, Z * 4, C), jnp.float32),
            ),
            in_specs=[vmem, vmem],
            out_specs=(in_hbm, in_hbm),
            scratch_shapes=[pltpu.SemaphoreType.DMA((2,))],
        )(*[pltpu.with_memory_space_constraint(v, pltpu.VMEM) for v in made])
        return new_fields.reshape(2, Z, X, C), new_planes.reshape(2, 2, Z, 4, C)

    placed = (
        P(None, None, "gx", "gy"),
        P("gx", "gy"),
        P(None, "gx", "gy"),
        P(None, None, None, "gx", "gy"),
    )
    return jax.shard_map(
        shards,
        mesh=mesh,
        in_specs=placed,
        out_specs=(P(None, None, "gx", "gy"), P(None, None, None, "gx", "gy")),
        check_vma=False,
    )
```

```python
import functools

import jax
import jax.numpy as jnp
from jax import lax
from jax.experimental import pallas as pl
from jax.experimental.pallas import tpu as pltpu
from jax.sharding import PartitionSpec as P

MESH = pl.DeviceIdType.MESH
cond_oil = 0.6
cond_drop = 2.0
diff_oil = 0.3
diff_drop = 1.0
thermal_slope = 0.3
cheb_radius = 0.95
cheb_ratio = 1.0 / cheb_radius
rho_first = 1.0 / cheb_ratio
rho_second = 1.0 / (2.0 * cheb_ratio - rho_first)
log2_e = 1.4426950408889634
keep_old = rho_second * rho_first
take_new = 2.0 * rho_second / cheb_radius

Z = 16
X = 16
C = 128
PITCH = 17
CORNERS = ((-1, -1), (-1, 1), (1, -1), (1, 1))
SIDES_Y = ((0, -1), (0, 1))
SIDES_X = ((-1, 0), (1, 0))
ALL = CORNERS + SIDES_Y + SIDES_X


def lanes(shape):
    return lax.broadcasted_iota(jnp.int32, shape, len(shape) - 1)


def roll_last(v, shift):
    return pltpu.roll(v, shift % C, v.ndim - 1)


def roll_rows(v, shift):
    return pltpu.roll(v, shift % 8, v.ndim - 2)


def rows_of(ref, index, start, step):
    at = lambda first: ref[(*index, pl.ds(first, 8, stride=step), slice(None))]
    return jnp.stack([at(start), at(start + step // 2)], axis=0)


def next_of(v, axis, turn):
    even, odd = lax.slice_in_dim(v, 0, 1, axis=axis), lax.slice_in_dim(v, 1, 2, axis=axis)
    return jnp.concatenate([odd, turn(even)], axis=axis)


def previous_of(v, axis, turn):
    even, odd = lax.slice_in_dim(v, 0, 1, axis=axis), lax.slice_in_dim(v, 1, 2, axis=axis)
    return jnp.concatenate([turn(odd), even], axis=axis)


def faces_of(k, axis, forth, back, last, first):
    even, odd = lax.slice_in_dim(k, 0, 1, axis=axis), lax.slice_in_dim(k, 1, 2, axis=axis)
    inner = even + odd
    up = jnp.where(last, 0.0, odd + forth(even))
    down = jnp.where(first, 0.0, even + back(odd))
    return jnp.concatenate([inner, up], axis=axis), jnp.concatenate([down, inner], axis=axis)


def packed_columns(v):
    head = v.shape[:-3]
    v = v.reshape(head + (8, 2, X, C))
    lane = lanes(head + (2, X, C))
    out = None
    for j in range(8):
        moved = roll_last(v[..., j, :, :, :], 16 * j + 8)
        out = moved if out is None else jnp.where(lane >= 16 * j, moved, out)
    return out


def packed_map(v):
    base = jnp.where(lanes(v.shape) < 16, roll_last(v, 8), 0.0)
    base = base + roll_last(base, 16)
    base = base + roll_last(base, 32)
    return base + roll_last(base, 64)


def periodic_columns(v):
    base = jnp.where(lanes(v.shape) < 8, roll_last(v, 4), 0.0)
    for shift in (8, 16, 32, 64):
        base = base + roll_last(base, shift)
    return base


def edge_columns(v):
    lane = lanes(v.shape[:-3] + (X, C))
    out = None
    for z in range(Z):
        moved = roll_last(v[..., z, :, :], 8 * z + 4)
        out = moved if out is None else jnp.where(lane >= 8 * z, moved, out)
    return out


def inverse(v):
    guess = pl.reciprocal(v, approx=True)
    return guess * (2.0 - v * guess)


def steps_of(droplet, active, old_t, old_n, decay, grid):
    def sweep(v, target, faces):
        px, mx, py, my, z_part = faces
        along = px * grid.xp(v) + mx * grid.xm(v)
        across = py * grid.yp(v) + my * grid.ym(v)
        return (target + along) + (across + z_part(v))

    def sides(k):
        return (*grid.x_faces(k), *grid.y_faces(k))

    def coefficients(k):
        px, mx, py, my = sides(k)
        z_part, z_total = grid.layers(k)
        robin = k * grid.edge4
        diagonal = (1.0 + robin) + (px + mx) + (py + my) + z_total
        return (px, mx, py, my, z_part), robin, inverse(diagonal)

    def heat_coefficients(k):
        px, mx, py, my = sides(k)
        robin = k * grid.edge4
        diagonal = (1.0 + robin) + (px + mx) + (py + my)
        z_part, inv = grid.even_layers(k, diagonal)
        return (px, mx, py, my, z_part), robin, inv

    ion_base = diff_oil + (diff_drop - diff_oil) * droplet
    heat_faces, heat_robin, heat_inv = heat_coefficients(cond_oil + (cond_drop - cond_oil) * droplet)
    heating = [(0.5 * (e * droplet)) * decay for e in active]

    def open_step(step, old_t, old_n):
        ions = ion_base * jnp.exp2((thermal_slope * log2_e) * old_t)
        target_t = old_t + heating[step] * (2.0 + old_n * old_n)
        ion_faces, ion_robin, ion_inv = coefficients(ions)
        if step == 0:
            yield
        return (
            (old_t, target_t, sweep(old_t, target_t, heat_faces), heat_faces, heat_robin, heat_inv),
            (old_n, old_n, sweep(old_n, old_n, ion_faces), ion_faces, ion_robin, ion_inv),
        )

    def close_field(parts, step, field, trace):
        old, target, total, faces, robin, inv = parts[field]
        given = robin * trace(step, field)
        first = (total + given) * inv
        return sweep(first, target + given, faces) * (take_new * inv) - keep_old * old

    yield
    parts = yield from open_step(0, old_t, old_n)
    trace = yield
    early = [close_field(parts, 0, field, trace) for field in range(2)]
    yield early
    parts = yield from open_step(1, *early)
    for field in range(2):
        yield close_field(parts, 1, field, trace)


class Span:
    def __init__(self, values, start):
        self.values, self.start = values, start

    def __call__(self, lo, hi):
        return self.values[lo - self.start : hi - self.start]


def gathered(function, lo, hi, size=4):
    return Span(jnp.concatenate([function(a, min(a + size, hi)) for a in range(lo, hi, size)], axis=0), lo)


def joined(*spans):
    return Span(jnp.concatenate([span.values for span in spans], axis=0), spans[0].start)


def x_sum(face, v, lo, hi):
    top, low = min(hi, X - 1), max(lo - 1, 0)
    up = face(lo, top)
    down = face(low, hi - 1)
    if v is not None:
        up = up * v(lo + 1, top + 1)
        down = down * v(low, hi - 1)
    first, last = max(lo, 1), top
    parts = [up[:1]] if lo == 0 else []
    if last > first:
        parts.append(up[first - lo : last - lo] + down[first - low - 1 : last - low - 1])
    if hi == X:
        parts.append(down[-1:])
    return jnp.concatenate(parts, axis=0)


class OwnColumns:
    def __init__(self, droplet, active, temper, ions, decay):
        self.olds = [[Span(temper, 0), Span(ions, 0)]]
        both = lambda v: jnp.concatenate([v, v], axis=1)
        heat = cond_oil + (cond_drop - cond_oil) * droplet
        self.ion_base = both(diff_oil + (diff_drop - diff_oil) * droplet)
        self.heating = [Span(both(0.5 * (e * droplet)) * decay, 0) for e in active]
        face = Span(heat[1:] + heat[:-1], 0)
        py = heat + roll_last(heat, -1)
        my = roll_last(py, 1)
        edge = jnp.concatenate([heat[:1], jnp.zeros_like(heat[1:-1]), heat[-1:]], axis=0)
        base = (1.0 + 4.0 * edge) + x_sum(face, None, 0, X) + (py + my)
        row = lax.broadcasted_iota(jnp.int32, (1, 1, 8, 1), 2)
        self.high, self.low = row == 7, row == 0
        pz = jnp.concatenate([2.0 * heat, jnp.where(self.high, 0.0, 2.0 * heat)], axis=1)
        mz = jnp.concatenate([jnp.where(self.low, 0.0, 2.0 * heat), 2.0 * heat], axis=1)
        heat_faces = (Span(both(face.values), 0), Span(both(py), 0), Span(both(my), 0), Span(pz, 0), Span(mz, 0))
        self.heat = (heat_faces, Span(inverse(both(base) + (pz + mz)), 0), Span(both(heat), 0))
        self.states = []

    def ion_parts(self, temper, lo, hi):
        k = self.ion_base[lo:hi] * jnp.exp2((thermal_slope * log2_e) * temper(lo, hi))
        pz, mz = faces_of(k, 1, lambda u: roll_rows(u, -1), lambda u: roll_rows(u, 1), self.high, self.low)
        return k, k + roll_last(k, -1), k + roll_last(k, 1), pz, mz

    def ion_spans(self, temper, lo, hi):
        parts = [self.ion_parts(temper, a, min(a + 4, hi)) for a in range(lo, hi, 4)]
        return [Span(jnp.concatenate(p, axis=0), lo) for p in zip(*parts)]

    def ion_inverse(self, spans, face, lo, hi):
        def part(a, b):
            k, py, my, pz, mz = [v(a, b) for v in spans]
            total = (1.0 + x_sum(face, None, a, b)) + (py + my) + (pz + mz)
            if a == 0:
                total = jnp.concatenate([total[:1] + 4.0 * k[:1], total[1:]], axis=0)
            if b == X:
                total = jnp.concatenate([total[:-1], total[-1:] + 4.0 * k[-1:]], axis=0)
            return inverse(total)

        return gathered(part, lo, hi)

    def sweep(self, v, target, faces, a, b):
        face, py, my, pz, mz = faces
        mid = v(a, b)
        across = py(a, b) * roll_last(mid, -1) + my(a, b) * roll_last(mid, 1)
        above = next_of(mid, 1, lambda u: roll_rows(u, -1))
        below = previous_of(mid, 1, lambda u: roll_rows(u, 1))
        upright = pz(a, b) * above + mz(a, b) * below
        return (target(a, b) + x_sum(face, v, a, b)) + (across + upright)

    def targets(self, step, old, lo, hi):
        heated = lambda a, b: old[0](a, b) + self.heating[step](a, b) * (2.0 + old[1](a, b) * old[1](a, b))
        return [gathered(heated, lo, hi), Span(old[1](lo, hi), lo)]

    def last(self, old, target, first, faces, inv, lo, hi):
        def part(a, b):
            return self.sweep(first, target, faces, a, b) * (take_new * inv(a, b)) - keep_old * old(a, b)

        return gathered(part, lo, hi)

    def partial(self, v, target, faces, x, inner, between):
        face, py, my, pz, mz = faces
        mid = v(x, x + 1)
        across = py(x, x + 1) * roll_last(mid, -1) + my(x, x + 1) * roll_last(mid, 1)
        above = next_of(mid, 1, lambda u: roll_rows(u, -1))
        below = previous_of(mid, 1, lambda u: roll_rows(u, 1))
        upright = pz(x, x + 1) * above + mz(x, x + 1) * below
        return (target(x, x + 1) + face(between, between + 1) * v(inner, inner + 1)) + (across + upright)

    def before(self):
        old = self.olds[0]
        self.near1, self.near2, self.near3 = [], [], []
        spans = self.ion_spans(old[0], 0, X)
        face = Span(spans[0].values[1:] + spans[0].values[:-1], 0)
        ion = ((face, *spans[1:]), self.ion_inverse(spans, face, 0, X), spans[0])
        self.sets0 = (self.heat, ion)
        self.target0 = self.targets(0, old, 0, X)
        self.total0, self.first0, self.mid1 = [], [], []
        for f in range(2):
            faces, inv, k = self.sets0[f]
            total = gathered(lambda a, b: self.sweep(old[f], self.target0[f], faces, a, b), 0, X)
            first = gathered(lambda a, b: total(a, b) * inv(a, b), 1, X - 1)
            self.total0.append(total)
            self.first0.append(first)
            self.mid1.append(self.last(old[f], self.target0[f], first, faces, inv, 2, X - 2))
            near = []
            for x, inner, between, opened in ((1, 2, 1, 0), (X - 2, X - 3, X - 3, X - 2)):
                scale = take_new * inv(x, x + 1)
                base = self.partial(first, self.target0[f], faces, x, inner, between)
                near.append((base * scale - keep_old * old[f](x, x + 1), faces[0](opened, opened + 1) * scale))
            self.near1.append(near)
        new = self.mid1
        self.spans1 = self.ion_spans(new[0], 2, X - 2)
        k = self.spans1[0]
        self.face1 = Span(k.values[1:] + k.values[:-1], 2)
        self.inv1 = self.ion_inverse(self.spans1, self.face1, 3, X - 3)
        self.target1 = self.targets(1, new, 2, X - 2)
        sets = ((self.heat[0], self.heat[1]), ((self.face1, *self.spans1[1:]), self.inv1))
        self.first1, self.mid2 = [], []
        for f in range(2):
            faces, inv = sets[f]
            first = gathered(lambda a, b: self.sweep(new[f], self.target1[f], faces, a, b) * inv(a, b), 3, X - 3)
            self.first1.append(first)
            self.mid2.append(self.last(new[f], self.target1[f], first, faces, inv, 4, X - 4))
            near = []
            for x, inner, between, opened in ((2, 3, 2, 1), (X - 3, X - 4, X - 4, X - 3)):
                base = self.partial(new[f], self.target1[f], faces, x, inner, between)
                if f == 0:
                    near.append((base * inv(x, x + 1), faces[0](opened, opened + 1) * inv(x, x + 1)))
                else:
                    rest = [part(x, x + 1) for part in faces[1:]]
                    total = (1.0 + faces[0](between, between + 1)) + (rest[0] + rest[1]) + (rest[2] + rest[3])
                    near.append((base, total))
            self.near2.append(near)
            near = []
            for x, inner, between, opened in ((3, 4, 3, 2), (X - 4, X - 5, X - 5, X - 4)):
                scale = take_new * inv(x, x + 1)
                base = self.partial(first, self.target1[f], faces, x, inner, between)
                near.append((base * scale - keep_old * new[f](x, x + 1), faces[0](opened, opened + 1) * scale))
            self.near3.append(near)

    def after(self, trace):
        old = self.olds[0]
        news = []
        for f in range(2):
            faces, inv, k = self.sets0[f]
            ends, target = [], self.target0[f].values
            for side, x in ((0, 0), (1, X - 1)):
                given = 4.0 * k(x, x + 1) * trace(0, f, side)
                ends.append((self.total0[f](x, x + 1) + given) * inv(x, x + 1))
                target = (
                    jnp.concatenate([target[:1] + given, target[1:]], axis=0)
                    if side == 0
                    else jnp.concatenate([target[:-1], target[-1:] + given], axis=0)
                )
            first = Span(jnp.concatenate([ends[0], self.first0[f].values, ends[1]], axis=0), 0)
            target = Span(target, 0)
            (low, low_face), (high, high_face) = self.near1[f]
            low = Span(low + low_face * ends[0], 1)
            high = Span(high + high_face * ends[1], X - 2)
            lowest = self.last(old[f], target, first, faces, inv, 0, 1)
            highest = self.last(old[f], target, first, faces, inv, X - 1, X)
            news.append(joined(lowest, low, self.mid1[f], high, highest))
            yield
        low, high = self.ion_spans(news[0], 0, 2), self.ion_spans(news[0], X - 2, X)
        spans = [joined(a, b, c) for a, b, c in zip(low, self.spans1, high)]
        k = spans[0].values
        face = Span(
            jnp.concatenate([k[1:3] + k[0:2], self.face1.values, k[X - 2 :] + k[X - 3 : X - 1]], axis=0), 0
        )
        reached = [
            inverse(self.near2[1][side][1] + face(between, between + 1)) for side, between in ((0, 1), (1, X - 3))
        ]
        inv = joined(
            self.ion_inverse(spans, face, 0, 2),
            Span(reached[0], 2),
            self.inv1,
            Span(reached[1], X - 3),
            self.ion_inverse(spans, face, X - 2, X),
        )
        yield
        lows, highs = self.targets(1, news, 0, 2), self.targets(1, news, X - 2, X)
        ends = []
        for f, (faces, inv, k) in enumerate((self.heat, ((face, *spans[1:]), inv, spans[0]))):
            target = joined(lows[f], self.target1[f], highs[f]).values
            target = Span(
                jnp.concatenate(
                    [
                        target[:1] + 4.0 * k(0, 1) * trace(1, f, 0),
                        target[1:-1],
                        target[-1:] + 4.0 * k(X - 1, X) * trace(1, f, 1),
                    ],
                    axis=0,
                ),
                0,
            )
            part = lambda a, b: self.sweep(news[f], target, faces, a, b) * inv(a, b)
            at2 = []
            for side, x, beside, between in ((0, 2, 1, 1), (1, X - 3, X - 2, X - 3)):
                base, other = self.near2[f][side]
                given = news[f](beside, beside + 1)
                if f == 0:
                    at2.append(base + other * given)
                else:
                    at2.append((base + face(between, between + 1) * given) * inv(x, x + 1))
            first = joined(
                gathered(part, 0, 2), Span(at2[0], 2), self.first1[f], Span(at2[1], X - 3), gathered(part, X - 2, X)
            )
            (low, low_face), (high, high_face) = self.near3[f]
            at3 = [low + low_face * at2[0], high + high_face * at2[1]]
            ends.append(
                joined(
                    self.last(news[f], target, first, faces, inv, 0, 3),
                    Span(at3[0], 3),
                    self.mid2[f],
                    Span(at3[1], X - 4),
                    self.last(news[f], target, first, faces, inv, X - 3, X),
                )
            )
            yield
        self.states = news, ends


class Strips:
    def __init__(self, left_open, right_open):
        self.lane = lanes((1, 1, 1, 1, C))
        self.column = self.lane % 16
        row = lax.broadcasted_iota(jnp.int32, (1, 1, 1, 8, 1), 3)
        half_x = lax.broadcasted_iota(jnp.int32, (1, 1, 2, 1, 1), 2)
        half_z = lax.broadcasted_iota(jnp.int32, (1, 2, 1, 1, 1), 1)
        side = lax.broadcasted_iota(jnp.int32, (2, 1, 1, 1, 1), 0)
        self.low, self.high = row == 0, row == 7
        self.floor, self.top = self.lane < 16, self.lane >= 112
        self.edge4 = jnp.where(2 * row + half_x == 0, 4.0, 0.0) + jnp.where(2 * row + half_x == X - 1, 4.0, 0.0)
        opened = jnp.where(side == 0, left_open, right_open)
        self.between_up = jnp.where(self.column == 7, opened, 1.0)
        self.between_down = jnp.where(self.column == 8, opened, 1.0)
        self.decay = jnp.exp(-4.0 * (2 * (self.lane // 16) + half_z).astype(jnp.float32) / Z)

    def xp(self, v):
        return next_of(v, 2, lambda u: roll_rows(u, -1))

    def xm(self, v):
        return previous_of(v, 2, lambda u: roll_rows(u, 1))

    def yp(self, v):
        return roll_last(v, -1)

    def ym(self, v):
        return roll_last(v, 1)

    def zp(self, v):
        return next_of(v, 1, lambda u: roll_last(u, -16))

    def zm(self, v):
        return previous_of(v, 1, lambda u: roll_last(u, 16))

    def x_faces(self, k):
        return faces_of(k, 2, lambda u: roll_rows(u, -1), lambda u: roll_rows(u, 1), self.high, self.low)

    def y_faces(self, k):
        return (k + self.yp(k)) * self.between_up, (k + self.ym(k)) * self.between_down

    def layers(self, k):
        up, down = faces_of(k, 1, lambda u: roll_last(u, -16), lambda u: roll_last(u, 16), self.top, self.floor)
        return lambda v: up * self.zp(v) + down * self.zm(v), up + down

    def even_layers(self, k, diagonal):
        twice = 2.0 * k
        up = jnp.concatenate([twice, jnp.where(self.top, 0.0, twice)], axis=1)
        down = jnp.concatenate([jnp.where(self.floor, 0.0, twice), twice], axis=1)
        return lambda v: up * self.zp(v) + down * self.zm(v), inverse(diagonal + (up + down))


def kernel(
    n_gx,
    n_gy,
    f_hbm,
    ph_hbm,
    el_hbm,
    pl_hbm,
    of_ref,
    op_ref,
    f_in,
    f_32,
    ph_in,
    el_in,
    pl_in,
    own_b,
    send_b,
    send_g,
    recv_b,
    recv_g,
    recv_c,
    merge_ref,
    late_ref,
    send_sem,
    recv_sem,
):
    gx = lax.axis_index("gx")
    gy = lax.axis_index("gy")

    def exists(offset):
        found = []
        for place, move, count in ((gx, offset[0], n_gx), (gy, offset[1], n_gy)):
            if move < 0:
                found.append(place > 0)
            if move > 0:
                found.append(place < count - 1)
        return functools.reduce(jnp.logical_and, found)

    def at(offset):
        return (gx + offset[0], gy + offset[1])

    barrier = pltpu.get_barrier_semaphore()
    expected = jnp.int32(0)
    for offset in SIDES_Y + CORNERS + SIDES_X:

        @pl.when(exists(offset))
        def _(offset=offset):
            pl.semaphore_signal(barrier, inc=1, device_id=at(offset), device_id_type=MESH)

        expected = expected + exists(offset).astype(jnp.int32)

    loads = [
        pltpu.make_async_copy(src, dst, send_sem.at[i])
        for i, (src, dst) in enumerate(((ph_hbm, ph_in), (el_hbm, el_in), (f_hbm, f_in), (pl_hbm, pl_in)))
    ]
    for load in loads:
        load.start()

    for i, offset in enumerate(SIDES_Y):

        @pl.when(jnp.logical_not(exists(offset)))
        def _(i=i):
            recv_b[i] = jnp.zeros(recv_b.shape[1:], jnp.float32)

    for i, offset in enumerate(SIDES_X):

        @pl.when(jnp.logical_not(exists(offset)))
        def _(i=i):
            recv_g[i] = jnp.zeros(recv_g.shape[1:], jnp.float32)

    for i, offset in enumerate(CORNERS):

        @pl.when(jnp.logical_not(exists(offset)))
        def _(i=i):
            recv_c[i] = jnp.zeros(recv_c.shape[1:], jnp.float32)

    for load in loads:
        load.wait()
    maps = [ph_in[...].astype(jnp.float32), el_in[0].astype(jnp.float32), el_in[1].astype(jnp.float32)]
    drop, on0, on1 = [periodic_columns(m) for m in maps]
    near = edge_columns(f_in[...].astype(jnp.float32))
    place = lanes((X, C)) % 8
    send_b[0, 0] = jnp.where(place >= 4, near[0], roll_last(drop, -4))
    send_b[0, 1] = jnp.where(place >= 4, near[1], jnp.where(place == 0, roll_last(on1, -4), roll_last(on0, -3)))
    send_b[1, 0] = jnp.where(place < 4, near[0], roll_last(drop, 4))
    send_b[1, 1] = jnp.where(place < 4, near[1], jnp.where(place == 7, roll_last(on1, 4), roll_last(on0, 3)))
    own_row = lax.broadcasted_iota(jnp.int32, (8, C), 0) == lanes((8, C)) // 16
    for side in range(2):
        near, far = ((0, 1), (3, 2))[side]
        for s in range(2):
            for f in range(2):
                first = (s * 2 + f) * Z
                a = pl_in[pl.ds(4 * first + near, Z, stride=4), :]
                b = pl_in[pl.ds(4 * first + far, Z, stride=4), :]
                send_g[side, first : first + Z, :] = a + 0.5 * (a - b)
    for side in range(2):
        for row in range(4):
            halves = rows_of(send_g, (side,), row * Z, 2)
            for h in range(2):
                spread = pltpu.roll(halves[h], 8, 1, stride=16, stride_axis=0)
                spread = jnp.sum(jnp.where(own_row, spread, 0.0), axis=0, keepdims=True)
                send_g[side, 64 + 2 * row + h : 65 + 2 * row + h, :] = spread

    pl.semaphore_wait(barrier, expected)

    def copy_of(i, offset):
        back = (-offset[0], -offset[1])
        if offset in CORNERS:
            src = send_g.at[(offset[0] + 1) // 2, pl.ds(64, 8)]
            dst = recv_c.at[CORNERS.index(back)]
        elif offset in SIDES_Y:
            src = send_b.at[(offset[1] + 1) // 2]
            dst = recv_b.at[SIDES_Y.index(back)]
        else:
            src = send_g.at[(offset[0] + 1) // 2]
            dst = recv_g.at[SIDES_X.index(back)]
        return pltpu.make_async_remote_copy(
            src_ref=src,
            dst_ref=dst,
            send_sem=send_sem.at[i],
            recv_sem=recv_sem.at[ALL.index(back)],
            device_id=at(offset),
            device_id_type=MESH,
        )

    for i, offset in enumerate(ALL):

        @pl.when(exists(offset))
        def _(i=i, offset=offset):
            copy_of(i, offset).start()

    for i in range(3):
        own_b[4 + i] = packed_map(maps[i])
    own_b[0:4] = packed_columns(f_in[...].astype(jnp.float32)).reshape(4, X, C)

    def wait_from(offset):
        back = (-offset[0], -offset[1])

        @pl.when(exists(offset))
        def _():
            copy_of(ALL.index(back), back).wait_recv()

    for f in range(2):
        layers = f_in[f].astype(jnp.float32)
        for z in range(Z):
            f_32[f, PITCH * z : PITCH * z + X, :] = layers[z]
    planes_x = lambda f: jnp.stack([rows_of(f_32, (f,), x, 2 * PITCH) for x in range(X)], axis=0)
    rows = lambda v: jnp.broadcast_to(v[:, None, None, :], (X, 1, 8, C))
    half = lax.broadcasted_iota(jnp.int32, (1, 2, 1, 1), 1)
    height = 2 * lax.broadcasted_iota(jnp.int32, (1, 1, 8, C), 2) + half
    decay = jnp.exp(-4.0 * height.astype(jnp.float32) / Z)
    columns = OwnColumns(rows(maps[0]), [rows(maps[1]), rows(maps[2])], planes_x(0), planes_x(1), decay)
    columns.before()
    for offset in SIDES_X + SIDES_Y:
        wait_from(offset)

    def trace_own(step, field, side):
        return rows_of(recv_g, (side,), (step * 2 + field) * Z, 2)[None]

    rest = columns.after(trace_own)
    next(rest)
    grid = Strips((gy > 0).astype(jnp.float32), (gy < n_gy - 1).astype(jnp.float32))
    inner = grid.column[0] < 8

    def strip(outer, own):
        return jnp.stack([jnp.where(inner, outer[0], own), jnp.where(inner, own, outer[1])], axis=0)

    def halo(side, field):
        v = rows_of(recv_b, (side, field), 0, 2)
        return jnp.stack([roll_last(v, 4), roll_last(v, -4)], axis=0)

    def own_strip(i):
        return rows_of(own_b, (i,), 0, 2)

    def map_strip(field, own, turns):
        outer = [roll_last(rows_of(recv_b, (side, field), 0, 2), turns[side])[None] for side in range(2)]
        return strip(outer, own_strip(own)[None])

    def trace_strip(step, field):
        row = (step * 2 + field) * 2
        halves = []
        for i in range(2):
            mid = recv_g[i, 64 + row : 66 + row, :]
            low = jnp.where(inner[0, 0], recv_c[2 * i, row : row + 2, :], mid)
            high = jnp.where(inner[0, 0], mid, recv_c[2 * i + 1, row : row + 2, :])
            halves.append(jnp.broadcast_to(jnp.stack([low, high], axis=0)[:, :, None, :], (2, 2, 8, C)))
        return jnp.stack(halves, axis=2)

    next(rest)
    fields = [
        strip([halo(side, f) for side in range(2)], jnp.stack([own_strip(2 * f), own_strip(2 * f + 1)], axis=0))
        for f in range(2)
    ]
    drop = map_strip(0, 4, (0, 0))
    on0 = map_strip(1, 5, (1, -1))
    on1 = map_strip(1, 6, (0, 0))
    work = steps_of(
        drop,
        [on0, on1],
        fields[0],
        fields[1],
        grid.decay,
        grid,
    )
    for _ in rest:
        next(work)
    early, late = columns.states
    for f in range(2):
        for h in range(2):
            for x in range(X):
                late_ref[f, pl.ds(PITCH * x + h, 8, stride=2), :] = late[f].values[x, h]
            for p, x in enumerate((0, 1, X - 2, X - 1)):
                op_ref[0, f, pl.ds(p + 4 * h, 8, stride=8), :] = early[f].values[x, h]
    for i, offset in enumerate(ALL):

        @pl.when(exists(offset))
        def _(i=i, offset=offset):
            copy_of(i, offset).wait_send()

    for offset in CORNERS:
        wait_from(offset)
    lane = lanes((X, C))
    edge = (lane < 4) | (lane >= C - 4)

    def both_sides(state):
        return jnp.where(inner, state[1], state[0])

    def merge(field, state):
        state = both_sides(state)
        for h in range(2):
            for i in range(2):
                merge_ref[field, h, pl.ds(i, 8, stride=2), :] = state[h, i]
        for h in range(2):
            state = merge_ref[field, h]
            for j in range(8):
                z = 2 * j + h
                rows = slice(X * z, X * z + X)
                own = late_ref[field, pl.ds(z, X, stride=PITCH), :]
                value = jnp.where(edge, roll_last(state, -(16 * j + 8)), own)
                of_ref[field, rows, :] = value
                op_ref[1, field, 4 * z : 4 * z + 4, :] = jnp.concatenate([value[0:2], value[X - 2 :]], axis=0)

    four = []
    for state in work.send(trace_strip):
        state = both_sides(state)
        four += [state[:, 0, 0:1], state[:, 1, 0:1], state[:, 0, 7:8], state[:, 1, 7:8]]
    four = jnp.concatenate(four, axis=1)
    temper = next(work)
    for j in range(8):
        back = roll_last(four, -(16 * j + 8))
        for h in range(2):
            for f in range(2):
                rows = slice(4 * (2 * j + h), 4 * (2 * j + h) + 4)
                op_ref[0, f, rows, :] = jnp.where(edge[:4], back[h, 4 * f : 4 * f + 4], op_ref[0, f, rows, :])
    merge(0, temper)
    merge(1, next(work))


def write_out(f_ref, p_ref, of_hbm, op_hbm, sem):
    copies = [
        pltpu.make_async_copy(f_ref, of_hbm, sem.at[0]),
        pltpu.make_async_copy(p_ref, op_hbm, sem.at[1]),
    ]
    for copy in copies:
        copy.start()
    for copy in copies:
        copy.wait()


def solution(mesh):
    n_gx = mesh.shape["gx"]
    n_gy = mesh.shape["gy"]

    def shards(fields, phase, electrode, planes):
        in_hbm = pl.BlockSpec(memory_space=pltpu.HBM)
        vmem = pl.BlockSpec(memory_space=pltpu.VMEM)
        made = pl.pallas_call(
            functools.partial(kernel, n_gx, n_gy),
            out_shape=(
                jax.ShapeDtypeStruct((2, Z * X, C), jnp.float32),
                jax.ShapeDtypeStruct((2, 2, Z * 4, C), jnp.float32),
            ),
            in_specs=[in_hbm] * 4,
            out_specs=(vmem, vmem),
            scratch_shapes=[
                pltpu.VMEM((2, Z, X, C), jnp.bfloat16),
                pltpu.VMEM((2, Z * PITCH, C), jnp.float32),
                pltpu.VMEM((X, C), jnp.int32),
                pltpu.VMEM((2, X, C), jnp.int32),
                pltpu.VMEM((2 * 2 * Z * 4, C), jnp.float32),
                pltpu.VMEM((7, X, C), jnp.float32),
                pltpu.VMEM((2, 2, X, C), jnp.float32),
                pltpu.VMEM((2, 72, C), jnp.float32),
                pltpu.VMEM((2, 2, X, C), jnp.float32),
                pltpu.VMEM((2, 72, C), jnp.float32),
                pltpu.VMEM((4, 8, C), jnp.float32),
                pltpu.VMEM((2, 2, X, C), jnp.float32),
                pltpu.VMEM((2, PITCH * X, C), jnp.float32),
                pltpu.SemaphoreType.DMA((8,)),
                pltpu.SemaphoreType.DMA((8,)),
            ],
            compiler_params=pltpu.CompilerParams(
                collective_id=0, has_side_effects=True, vmem_limit_bytes=32 * 1024 * 1024
            ),
        )(*[pltpu.with_memory_space_constraint(v, pltpu.HBM) for v in (fields, phase, electrode, planes.reshape(2 * 2 * Z * 4, C))])
        new_fields, new_planes = pl.pallas_call(
            write_out,
            out_shape=(
                pltpu.HBM((2, Z * X, C), jnp.float32),
                pltpu.HBM((2, 2, Z * 4, C), jnp.float32),
            ),
            in_specs=[vmem, vmem],
            out_specs=(in_hbm, in_hbm),
            scratch_shapes=[pltpu.SemaphoreType.DMA((2,))],
        )(*[pltpu.with_memory_space_constraint(v, pltpu.VMEM) for v in made])
        return new_fields.reshape(2, Z, X, C), new_planes.reshape(2, 2, Z, 4, C)

    placed = (
        P(None, None, "gx", "gy"),
        P("gx", "gy"),
        P(None, "gx", "gy"),
        P(None, None, None, "gx", "gy"),
    )
    return jax.shard_map(
        shards,
        mesh=mesh,
        in_specs=placed,
        out_specs=(P(None, None, "gx", "gy"), P(None, None, None, "gx", "gy")),
        check_vma=False,
    )
```

```python
import functools

import jax
import jax.numpy as jnp
from jax import lax
from jax.experimental import pallas as pl
from jax.experimental.pallas import tpu as pltpu
from jax.sharding import PartitionSpec as P

MESH = pl.DeviceIdType.MESH
cond_oil = 0.6
cond_drop = 2.0
diff_oil = 0.3
diff_drop = 1.0
thermal_slope = 0.3
cheb_radius = 0.95
cheb_ratio = 1.0 / cheb_radius
rho_first = 1.0 / cheb_ratio
rho_second = 1.0 / (2.0 * cheb_ratio - rho_first)
log2_e = 1.4426950408889634
keep_old = rho_second * rho_first
take_new = 2.0 * rho_second / cheb_radius

Z = 16
X = 16
C = 128
PITCH = 17
CORNERS = ((-1, -1), (-1, 1), (1, -1), (1, 1))
SIDES_Y = ((0, -1), (0, 1))
SIDES_X = ((-1, 0), (1, 0))
ALL = CORNERS + SIDES_Y + SIDES_X


def lanes(shape):
    return lax.broadcasted_iota(jnp.int32, shape, len(shape) - 1)


def roll_last(v, shift):
    return pltpu.roll(v, shift % C, v.ndim - 1)


def roll_rows(v, shift):
    return pltpu.roll(v, shift % 8, v.ndim - 2)


def rows_of(ref, index, start, step):
    at = lambda first: ref[(*index, pl.ds(first, 8, stride=step), slice(None))]
    return jnp.stack([at(start), at(start + step // 2)], axis=0)


def next_of(v, axis, turn):
    even, odd = lax.slice_in_dim(v, 0, 1, axis=axis), lax.slice_in_dim(v, 1, 2, axis=axis)
    return jnp.concatenate([odd, turn(even)], axis=axis)


def previous_of(v, axis, turn):
    even, odd = lax.slice_in_dim(v, 0, 1, axis=axis), lax.slice_in_dim(v, 1, 2, axis=axis)
    return jnp.concatenate([turn(odd), even], axis=axis)


def faces_of(k, axis, forth, back, last, first):
    even, odd = lax.slice_in_dim(k, 0, 1, axis=axis), lax.slice_in_dim(k, 1, 2, axis=axis)
    inner = even + odd
    up = jnp.where(last, 0.0, odd + forth(even))
    down = jnp.where(first, 0.0, even + back(odd))
    return jnp.concatenate([inner, up], axis=axis), jnp.concatenate([down, inner], axis=axis)


def packed_columns(v):
    head = v.shape[:-3]
    v = v.reshape(head + (8, 2, X, C))
    lane = lanes(head + (2, X, C))
    out = None
    for j in range(8):
        moved = roll_last(v[..., j, :, :, :], 16 * j + 8)
        out = moved if out is None else jnp.where(lane >= 16 * j, moved, out)
    return out


def packed_map(v):
    base = jnp.where(lanes(v.shape) < 16, roll_last(v, 8), 0.0)
    base = base + roll_last(base, 16)
    base = base + roll_last(base, 32)
    return base + roll_last(base, 64)


def periodic_columns(v):
    base = jnp.where(lanes(v.shape) < 8, roll_last(v, 4), 0.0)
    for shift in (8, 16, 32, 64):
        base = base + roll_last(base, shift)
    return base


def edge_columns(v):
    lane = lanes(v.shape[:-3] + (X, C))
    out = None
    for z in range(Z):
        moved = roll_last(v[..., z, :, :], 8 * z + 4)
        out = moved if out is None else jnp.where(lane >= 8 * z, moved, out)
    return out


def inverse(v):
    guess = pl.reciprocal(v, approx=True)
    return guess * (2.0 - v * guess)


def steps_of(droplet, active, old_t, old_n, decay, grid):
    def sweep(v, target, faces):
        px, mx, py, my, z_part = faces
        along = px * grid.xp(v) + mx * grid.xm(v)
        across = py * grid.yp(v) + my * grid.ym(v)
        return (target + along) + (across + z_part(v))

    def sides(k):
        return (*grid.x_faces(k), *grid.y_faces(k))

    def coefficients(k):
        px, mx, py, my = sides(k)
        z_part, z_total = grid.layers(k)
        robin = k * grid.edge4
        diagonal = (1.0 + robin) + (px + mx) + (py + my) + z_total
        return (px, mx, py, my, z_part), robin, inverse(diagonal)

    def heat_coefficients(k):
        px, mx, py, my = sides(k)
        robin = k * grid.edge4
        diagonal = (1.0 + robin) + (px + mx) + (py + my)
        z_part, inv = grid.even_layers(k, diagonal)
        return (px, mx, py, my, z_part), robin, inv

    ion_base = diff_oil + (diff_drop - diff_oil) * droplet
    heat_faces, heat_robin, heat_inv = heat_coefficients(cond_oil + (cond_drop - cond_oil) * droplet)
    heating = [(0.5 * (e * droplet)) * decay for e in active]

    def open_step(step, old_t, old_n):
        ions = ion_base * jnp.exp2((thermal_slope * log2_e) * old_t)
        target_t = old_t + heating[step] * (2.0 + old_n * old_n)
        ion_faces, ion_robin, ion_inv = coefficients(ions)
        if step == 0:
            yield
        return (
            (old_t, target_t, sweep(old_t, target_t, heat_faces), heat_faces, heat_robin, heat_inv),
            (old_n, old_n, sweep(old_n, old_n, ion_faces), ion_faces, ion_robin, ion_inv),
        )

    def close_field(parts, step, field, trace):
        old, target, total, faces, robin, inv = parts[field]
        given = robin * trace(step, field)
        first = (total + given) * inv
        return sweep(first, target + given, faces) * (take_new * inv) - keep_old * old

    yield
    parts = yield from open_step(0, old_t, old_n)
    trace = yield
    early = [close_field(parts, 0, field, trace) for field in range(2)]
    yield early
    parts = yield from open_step(1, *early)
    for field in range(2):
        yield close_field(parts, 1, field, trace)


class Span:
    def __init__(self, values, start):
        self.values, self.start = values, start

    def __call__(self, lo, hi):
        return self.values[lo - self.start : hi - self.start]


def gathered(function, lo, hi, size=4):
    return Span(jnp.concatenate([function(a, min(a + size, hi)) for a in range(lo, hi, size)], axis=0), lo)


def joined(*spans):
    return Span(jnp.concatenate([span.values for span in spans], axis=0), spans[0].start)


def x_sum(face, v, lo, hi):
    top, low = min(hi, X - 1), max(lo - 1, 0)
    up = face(lo, top)
    down = face(low, hi - 1)
    if v is not None:
        up = up * v(lo + 1, top + 1)
        down = down * v(low, hi - 1)
    first, last = max(lo, 1), top
    parts = [up[:1]] if lo == 0 else []
    if last > first:
        parts.append(up[first - lo : last - lo] + down[first - low - 1 : last - low - 1])
    if hi == X:
        parts.append(down[-1:])
    return jnp.concatenate(parts, axis=0)


class OwnColumns:
    def __init__(self, droplet, active, temper, ions, decay):
        self.olds = [[Span(temper, 0), Span(ions, 0)]]
        both = lambda v: jnp.concatenate([v, v], axis=1)
        heat = cond_oil + (cond_drop - cond_oil) * droplet
        self.ion_base = both(diff_oil + (diff_drop - diff_oil) * droplet)
        self.heating = [Span(both(0.5 * (e * droplet)) * decay, 0) for e in active]
        face = Span(heat[1:] + heat[:-1], 0)
        py = heat + roll_last(heat, -1)
        my = roll_last(py, 1)
        edge = jnp.concatenate([heat[:1], jnp.zeros_like(heat[1:-1]), heat[-1:]], axis=0)
        base = (1.0 + 4.0 * edge) + x_sum(face, None, 0, X) + (py + my)
        row = lax.broadcasted_iota(jnp.int32, (1, 1, 8, 1), 2)
        self.high, self.low = row == 7, row == 0
        pz = jnp.concatenate([2.0 * heat, jnp.where(self.high, 0.0, 2.0 * heat)], axis=1)
        mz = jnp.concatenate([jnp.where(self.low, 0.0, 2.0 * heat), 2.0 * heat], axis=1)
        heat_faces = (Span(both(face.values), 0), Span(both(py), 0), Span(both(my), 0), Span(pz, 0), Span(mz, 0))
        self.heat = (heat_faces, Span(inverse(both(base) + (pz + mz)), 0), Span(both(heat), 0))
        self.states = []

    def ion_parts(self, temper, lo, hi):
        k = self.ion_base[lo:hi] * jnp.exp2((thermal_slope * log2_e) * temper(lo, hi))
        pz, mz = faces_of(k, 1, lambda u: roll_rows(u, -1), lambda u: roll_rows(u, 1), self.high, self.low)
        return k, k + roll_last(k, -1), k + roll_last(k, 1), pz, mz

    def ion_spans(self, temper, lo, hi):
        parts = [self.ion_parts(temper, a, min(a + 4, hi)) for a in range(lo, hi, 4)]
        return [Span(jnp.concatenate(p, axis=0), lo) for p in zip(*parts)]

    def ion_inverse(self, spans, face, lo, hi):
        def part(a, b):
            k, py, my, pz, mz = [v(a, b) for v in spans]
            total = (1.0 + x_sum(face, None, a, b)) + (py + my) + (pz + mz)
            if a == 0:
                total = jnp.concatenate([total[:1] + 4.0 * k[:1], total[1:]], axis=0)
            if b == X:
                total = jnp.concatenate([total[:-1], total[-1:] + 4.0 * k[-1:]], axis=0)
            return inverse(total)

        return gathered(part, lo, hi)

    def sweep(self, v, target, faces, a, b):
        face, py, my, pz, mz = faces
        mid = v(a, b)
        across = py(a, b) * roll_last(mid, -1) + my(a, b) * roll_last(mid, 1)
        above = next_of(mid, 1, lambda u: roll_rows(u, -1))
        below = previous_of(mid, 1, lambda u: roll_rows(u, 1))
        upright = pz(a, b) * above + mz(a, b) * below
        return (target(a, b) + x_sum(face, v, a, b)) + (across + upright)

    def targets(self, step, old, lo, hi):
        heated = lambda a, b: old[0](a, b) + self.heating[step](a, b) * (2.0 + old[1](a, b) * old[1](a, b))
        return [gathered(heated, lo, hi), Span(old[1](lo, hi), lo)]

    def last(self, old, target, first, faces, inv, lo, hi):
        def part(a, b):
            return self.sweep(first, target, faces, a, b) * (take_new * inv(a, b)) - keep_old * old(a, b)

        return gathered(part, lo, hi)

    def before(self):
        old = self.olds[0]
        spans = self.ion_spans(old[0], 0, X)
        face = Span(spans[0].values[1:] + spans[0].values[:-1], 0)
        ion = ((face, *spans[1:]), self.ion_inverse(spans, face, 0, X), spans[0])
        self.sets0 = (self.heat, ion)
        self.target0 = self.targets(0, old, 0, X)
        self.total0, self.first0, self.mid1 = [], [], []
        for f in range(2):
            faces, inv, k = self.sets0[f]
            total = gathered(lambda a, b: self.sweep(old[f], self.target0[f], faces, a, b), 0, X)
            first = gathered(lambda a, b: total(a, b) * inv(a, b), 1, X - 1)
            self.total0.append(total)
            self.first0.append(first)
            self.mid1.append(self.last(old[f], self.target0[f], first, faces, inv, 2, X - 2))
        new = self.mid1
        self.spans1 = self.ion_spans(new[0], 2, X - 2)
        k = self.spans1[0]
        self.face1 = Span(k.values[1:] + k.values[:-1], 2)
        self.inv1 = self.ion_inverse(self.spans1, self.face1, 3, X - 3)
        self.target1 = self.targets(1, new, 2, X - 2)
        sets = ((self.heat[0], self.heat[1]), ((self.face1, *self.spans1[1:]), self.inv1))
        self.first1, self.mid2 = [], []
        for f in range(2):
            faces, inv = sets[f]
            first = gathered(lambda a, b: self.sweep(new[f], self.target1[f], faces, a, b) * inv(a, b), 3, X - 3)
            self.first1.append(first)
            self.mid2.append(self.last(new[f], self.target1[f], first, faces, inv, 4, X - 4))

    def after(self, trace):
        old = self.olds[0]
        news = []
        for f in range(2):
            faces, inv, k = self.sets0[f]
            ends, target = [], self.target0[f].values
            for side, x in ((0, 0), (1, X - 1)):
                given = 4.0 * k(x, x + 1) * trace(0, f, side)
                ends.append((self.total0[f](x, x + 1) + given) * inv(x, x + 1))
                target = (
                    jnp.concatenate([target[:1] + given, target[1:]], axis=0)
                    if side == 0
                    else jnp.concatenate([target[:-1], target[-1:] + given], axis=0)
                )
            first = Span(jnp.concatenate([ends[0], self.first0[f].values, ends[1]], axis=0), 0)
            target = Span(target, 0)
            low = self.last(old[f], target, first, faces, inv, 0, 2)
            high = self.last(old[f], target, first, faces, inv, X - 2, X)
            news.append(joined(low, self.mid1[f], high))
            yield
        low, high = self.ion_spans(news[0], 0, 2), self.ion_spans(news[0], X - 2, X)
        spans = [joined(a, b, c) for a, b, c in zip(low, self.spans1, high)]
        k = spans[0].values
        face = Span(
            jnp.concatenate([k[1:3] + k[0:2], self.face1.values, k[X - 2 :] + k[X - 3 : X - 1]], axis=0), 0
        )
        inv = joined(self.ion_inverse(spans, face, 0, 3), self.inv1, self.ion_inverse(spans, face, X - 3, X))
        yield
        low, high = self.targets(1, news, 0, 2), self.targets(1, news, X - 2, X)
        ends = []
        for f, (faces, inv, k) in enumerate((self.heat, ((face, *spans[1:]), inv, spans[0]))):
            target = joined(low[f], self.target1[f], high[f]).values
            target = Span(
                jnp.concatenate(
                    [
                        target[:1] + 4.0 * k(0, 1) * trace(1, f, 0),
                        target[1:-1],
                        target[-1:] + 4.0 * k(X - 1, X) * trace(1, f, 1),
                    ],
                    axis=0,
                ),
                0,
            )
            part = lambda a, b: self.sweep(news[f], target, faces, a, b) * inv(a, b)
            first = joined(gathered(part, 0, 3), self.first1[f], gathered(part, X - 3, X))
            ends.append(
                joined(
                    self.last(news[f], target, first, faces, inv, 0, 4),
                    self.mid2[f],
                    self.last(news[f], target, first, faces, inv, X - 4, X),
                )
            )
            yield
        self.states = news, ends


class Strips:
    def __init__(self, left_open, right_open):
        self.lane = lanes((1, 1, 1, 1, C))
        self.column = self.lane % 16
        row = lax.broadcasted_iota(jnp.int32, (1, 1, 1, 8, 1), 3)
        half_x = lax.broadcasted_iota(jnp.int32, (1, 1, 2, 1, 1), 2)
        half_z = lax.broadcasted_iota(jnp.int32, (1, 2, 1, 1, 1), 1)
        side = lax.broadcasted_iota(jnp.int32, (2, 1, 1, 1, 1), 0)
        self.low, self.high = row == 0, row == 7
        self.floor, self.top = self.lane < 16, self.lane >= 112
        self.edge4 = jnp.where(2 * row + half_x == 0, 4.0, 0.0) + jnp.where(2 * row + half_x == X - 1, 4.0, 0.0)
        opened = jnp.where(side == 0, left_open, right_open)
        self.between_up = jnp.where(self.column == 7, opened, 1.0)
        self.between_down = jnp.where(self.column == 8, opened, 1.0)
        self.decay = jnp.exp(-4.0 * (2 * (self.lane // 16) + half_z).astype(jnp.float32) / Z)

    def xp(self, v):
        return next_of(v, 2, lambda u: roll_rows(u, -1))

    def xm(self, v):
        return previous_of(v, 2, lambda u: roll_rows(u, 1))

    def yp(self, v):
        return roll_last(v, -1)

    def ym(self, v):
        return roll_last(v, 1)

    def zp(self, v):
        return next_of(v, 1, lambda u: roll_last(u, -16))

    def zm(self, v):
        return previous_of(v, 1, lambda u: roll_last(u, 16))

    def x_faces(self, k):
        return faces_of(k, 2, lambda u: roll_rows(u, -1), lambda u: roll_rows(u, 1), self.high, self.low)

    def y_faces(self, k):
        return (k + self.yp(k)) * self.between_up, (k + self.ym(k)) * self.between_down

    def layers(self, k):
        up, down = faces_of(k, 1, lambda u: roll_last(u, -16), lambda u: roll_last(u, 16), self.top, self.floor)
        return lambda v: up * self.zp(v) + down * self.zm(v), up + down

    def even_layers(self, k, diagonal):
        twice = 2.0 * k
        up = jnp.concatenate([twice, jnp.where(self.top, 0.0, twice)], axis=1)
        down = jnp.concatenate([jnp.where(self.floor, 0.0, twice), twice], axis=1)
        return lambda v: up * self.zp(v) + down * self.zm(v), inverse(diagonal + (up + down))


def kernel(
    n_gx,
    n_gy,
    f_hbm,
    ph_hbm,
    el_hbm,
    pl_hbm,
    of_ref,
    op_ref,
    f_in,
    f_32,
    ph_in,
    el_in,
    pl_in,
    own_b,
    send_b,
    send_g,
    recv_b,
    recv_g,
    recv_c,
    merge_ref,
    late_ref,
    send_sem,
    recv_sem,
):
    gx = lax.axis_index("gx")
    gy = lax.axis_index("gy")

    def exists(offset):
        found = []
        for place, move, count in ((gx, offset[0], n_gx), (gy, offset[1], n_gy)):
            if move < 0:
                found.append(place > 0)
            if move > 0:
                found.append(place < count - 1)
        return functools.reduce(jnp.logical_and, found)

    def at(offset):
        return (gx + offset[0], gy + offset[1])

    barrier = pltpu.get_barrier_semaphore()
    expected = jnp.int32(0)
    for offset in ALL:

        @pl.when(exists(offset))
        def _(offset=offset):
            pl.semaphore_signal(barrier, inc=1, device_id=at(offset), device_id_type=MESH)

        expected = expected + exists(offset).astype(jnp.int32)

    loads = [
        pltpu.make_async_copy(src, dst, send_sem.at[i])
        for i, (src, dst) in enumerate(((ph_hbm, ph_in), (el_hbm, el_in), (f_hbm, f_in), (pl_hbm, pl_in)))
    ]
    for load in loads:
        load.start()

    for i, offset in enumerate(SIDES_Y):

        @pl.when(jnp.logical_not(exists(offset)))
        def _(i=i):
            recv_b[i] = jnp.zeros(recv_b.shape[1:], jnp.float32)

    for i, offset in enumerate(SIDES_X):

        @pl.when(jnp.logical_not(exists(offset)))
        def _(i=i):
            recv_g[i] = jnp.zeros(recv_g.shape[1:], jnp.float32)

    for i, offset in enumerate(CORNERS):

        @pl.when(jnp.logical_not(exists(offset)))
        def _(i=i):
            recv_c[i] = jnp.zeros(recv_c.shape[1:], jnp.float32)

    for load in loads:
        load.wait()
    maps = [ph_in[...].astype(jnp.float32), el_in[0].astype(jnp.float32), el_in[1].astype(jnp.float32)]
    drop, on0, on1 = [periodic_columns(m) for m in maps]
    near = edge_columns(f_in[...].astype(jnp.float32))
    place = lanes((X, C)) % 8
    send_b[0, 0] = jnp.where(place >= 4, near[0], roll_last(drop, -4))
    send_b[0, 1] = jnp.where(place >= 4, near[1], jnp.where(place == 0, roll_last(on1, -4), roll_last(on0, -3)))
    send_b[1, 0] = jnp.where(place < 4, near[0], roll_last(drop, 4))
    send_b[1, 1] = jnp.where(place < 4, near[1], jnp.where(place == 7, roll_last(on1, 4), roll_last(on0, 3)))
    own_row = lax.broadcasted_iota(jnp.int32, (8, C), 0) == lanes((8, C)) // 16
    for side in range(2):
        near, far = ((0, 1), (3, 2))[side]
        for s in range(2):
            for f in range(2):
                first = (s * 2 + f) * Z
                a = pl_in[pl.ds(4 * first + near, Z, stride=4), :]
                b = pl_in[pl.ds(4 * first + far, Z, stride=4), :]
                send_g[side, first : first + Z, :] = a + 0.5 * (a - b)
    for side in range(2):
        for row in range(4):
            halves = rows_of(send_g, (side,), row * Z, 2)
            for h in range(2):
                spread = pltpu.roll(halves[h], 8, 1, stride=16, stride_axis=0)
                spread = jnp.sum(jnp.where(own_row, spread, 0.0), axis=0, keepdims=True)
                send_g[side, 64 + 2 * row + h : 65 + 2 * row + h, :] = spread

    pl.semaphore_wait(barrier, expected)

    def copy_of(i, offset):
        back = (-offset[0], -offset[1])
        if offset in CORNERS:
            src = send_g.at[(offset[0] + 1) // 2, pl.ds(64, 8)]
            dst = recv_c.at[CORNERS.index(back)]
        elif offset in SIDES_Y:
            src = send_b.at[(offset[1] + 1) // 2]
            dst = recv_b.at[SIDES_Y.index(back)]
        else:
            src = send_g.at[(offset[0] + 1) // 2]
            dst = recv_g.at[SIDES_X.index(back)]
        return pltpu.make_async_remote_copy(
            src_ref=src,
            dst_ref=dst,
            send_sem=send_sem.at[i],
            recv_sem=recv_sem.at[ALL.index(back)],
            device_id=at(offset),
            device_id_type=MESH,
        )

    for i, offset in enumerate(ALL):

        @pl.when(exists(offset))
        def _(i=i, offset=offset):
            copy_of(i, offset).start()

    for i in range(3):
        own_b[4 + i] = packed_map(maps[i])
    own_b[0:4] = packed_columns(f_in[...].astype(jnp.float32)).reshape(4, X, C)

    def wait_from(offset):
        back = (-offset[0], -offset[1])

        @pl.when(exists(offset))
        def _():
            copy_of(ALL.index(back), back).wait_recv()

    for f in range(2):
        layers = f_in[f].astype(jnp.float32)
        for z in range(Z):
            f_32[f, PITCH * z : PITCH * z + X, :] = layers[z]
    planes_x = lambda f: jnp.stack([rows_of(f_32, (f,), x, 2 * PITCH) for x in range(X)], axis=0)
    rows = lambda v: jnp.broadcast_to(v[:, None, None, :], (X, 1, 8, C))
    half = lax.broadcasted_iota(jnp.int32, (1, 2, 1, 1), 1)
    height = 2 * lax.broadcasted_iota(jnp.int32, (1, 1, 8, C), 2) + half
    decay = jnp.exp(-4.0 * height.astype(jnp.float32) / Z)
    columns = OwnColumns(rows(maps[0]), [rows(maps[1]), rows(maps[2])], planes_x(0), planes_x(1), decay)
    columns.before()
    for offset in SIDES_X + SIDES_Y:
        wait_from(offset)

    def trace_own(step, field, side):
        return rows_of(recv_g, (side,), (step * 2 + field) * Z, 2)[None]

    rest = columns.after(trace_own)
    next(rest)
    grid = Strips((gy > 0).astype(jnp.float32), (gy < n_gy - 1).astype(jnp.float32))
    inner = grid.column[0] < 8

    def strip(outer, own):
        return jnp.stack([jnp.where(inner, outer[0], own), jnp.where(inner, own, outer[1])], axis=0)

    def halo(side, field):
        v = rows_of(recv_b, (side, field), 0, 2)
        return jnp.stack([roll_last(v, 4), roll_last(v, -4)], axis=0)

    def own_strip(i):
        return rows_of(own_b, (i,), 0, 2)

    def map_strip(field, own, turns):
        outer = [roll_last(rows_of(recv_b, (side, field), 0, 2), turns[side])[None] for side in range(2)]
        return strip(outer, own_strip(own)[None])

    def trace_strip(step, field):
        row = (step * 2 + field) * 2
        halves = []
        for i in range(2):
            mid = recv_g[i, 64 + row : 66 + row, :]
            low = jnp.where(inner[0, 0], recv_c[2 * i, row : row + 2, :], mid)
            high = jnp.where(inner[0, 0], mid, recv_c[2 * i + 1, row : row + 2, :])
            halves.append(jnp.broadcast_to(jnp.stack([low, high], axis=0)[:, :, None, :], (2, 2, 8, C)))
        return jnp.stack(halves, axis=2)

    next(rest)
    fields = [
        strip([halo(side, f) for side in range(2)], jnp.stack([own_strip(2 * f), own_strip(2 * f + 1)], axis=0))
        for f in range(2)
    ]
    drop = map_strip(0, 4, (0, 0))
    on0 = map_strip(1, 5, (1, -1))
    on1 = map_strip(1, 6, (0, 0))
    work = steps_of(
        drop,
        [on0, on1],
        fields[0],
        fields[1],
        grid.decay,
        grid,
    )
    for _ in rest:
        next(work)
    early, late = columns.states
    for f in range(2):
        for h in range(2):
            for x in range(X):
                late_ref[f, pl.ds(PITCH * x + h, 8, stride=2), :] = late[f].values[x, h]
            for p, x in enumerate((0, 1, X - 2, X - 1)):
                op_ref[0, f, pl.ds(p + 4 * h, 8, stride=8), :] = early[f].values[x, h]
    for i, offset in enumerate(ALL):

        @pl.when(exists(offset))
        def _(i=i, offset=offset):
            copy_of(i, offset).wait_send()

    for offset in CORNERS:
        wait_from(offset)
    lane = lanes((X, C))
    edge = (lane < 4) | (lane >= C - 4)

    def both_sides(state):
        return jnp.where(inner, state[1], state[0])

    def merge(field, state):
        state = both_sides(state)
        for h in range(2):
            for i in range(2):
                merge_ref[field, h, pl.ds(i, 8, stride=2), :] = state[h, i]
        for h in range(2):
            state = merge_ref[field, h]
            for j in range(8):
                z = 2 * j + h
                rows = slice(X * z, X * z + X)
                own = late_ref[field, pl.ds(z, X, stride=PITCH), :]
                value = jnp.where(edge, roll_last(state, -(16 * j + 8)), own)
                of_ref[field, rows, :] = value
                op_ref[1, field, 4 * z : 4 * z + 4, :] = jnp.concatenate([value[0:2], value[X - 2 :]], axis=0)

    four = []
    for state in work.send(trace_strip):
        state = both_sides(state)
        four += [state[:, 0, 0:1], state[:, 1, 0:1], state[:, 0, 7:8], state[:, 1, 7:8]]
    four = jnp.concatenate(four, axis=1)
    temper = next(work)
    for j in range(8):
        back = roll_last(four, -(16 * j + 8))
        for h in range(2):
            for f in range(2):
                rows = slice(4 * (2 * j + h), 4 * (2 * j + h) + 4)
                op_ref[0, f, rows, :] = jnp.where(edge[:4], back[h, 4 * f : 4 * f + 4], op_ref[0, f, rows, :])
    merge(0, temper)
    merge(1, next(work))


def write_out(f_ref, p_ref, of_hbm, op_hbm, sem):
    copies = [
        pltpu.make_async_copy(f_ref, of_hbm, sem.at[0]),
        pltpu.make_async_copy(p_ref, op_hbm, sem.at[1]),
    ]
    copies[0].start(priority=0)
    copies[1].start(priority=1)
    for copy in copies:
        copy.wait()


def solution(mesh):
    n_gx = mesh.shape["gx"]
    n_gy = mesh.shape["gy"]

    def shards(fields, phase, electrode, planes):
        in_hbm = pl.BlockSpec(memory_space=pltpu.HBM)
        vmem = pl.BlockSpec(memory_space=pltpu.VMEM)
        made = pl.pallas_call(
            functools.partial(kernel, n_gx, n_gy),
            out_shape=(
                jax.ShapeDtypeStruct((2, Z * X, C), jnp.float32),
                jax.ShapeDtypeStruct((2, 2, Z * 4, C), jnp.float32),
            ),
            in_specs=[in_hbm] * 4,
            out_specs=(vmem, vmem),
            scratch_shapes=[
                pltpu.VMEM((2, Z, X, C), jnp.bfloat16),
                pltpu.VMEM((2, Z * PITCH, C), jnp.float32),
                pltpu.VMEM((X, C), jnp.int32),
                pltpu.VMEM((2, X, C), jnp.int32),
                pltpu.VMEM((2 * 2 * Z * 4, C), jnp.float32),
                pltpu.VMEM((7, X, C), jnp.float32),
                pltpu.VMEM((2, 2, X, C), jnp.float32),
                pltpu.VMEM((2, 72, C), jnp.float32),
                pltpu.VMEM((2, 2, X, C), jnp.float32),
                pltpu.VMEM((2, 72, C), jnp.float32),
                pltpu.VMEM((4, 8, C), jnp.float32),
                pltpu.VMEM((2, 2, X, C), jnp.float32),
                pltpu.VMEM((2, PITCH * X, C), jnp.float32),
                pltpu.SemaphoreType.DMA((8,)),
                pltpu.SemaphoreType.DMA((8,)),
            ],
            compiler_params=pltpu.CompilerParams(
                collective_id=0, has_side_effects=True, vmem_limit_bytes=32 * 1024 * 1024
            ),
        )(*[pltpu.with_memory_space_constraint(v, pltpu.HBM) for v in (fields, phase, electrode, planes.reshape(2 * 2 * Z * 4, C))])
        new_fields, new_planes = pl.pallas_call(
            write_out,
            out_shape=(
                pltpu.HBM((2, Z * X, C), jnp.float32),
                pltpu.HBM((2, 2, Z * 4, C), jnp.float32),
            ),
            in_specs=[vmem, vmem],
            out_specs=(in_hbm, in_hbm),
            scratch_shapes=[pltpu.SemaphoreType.DMA((2,))],
        )(*[pltpu.with_memory_space_constraint(v, pltpu.VMEM) for v in made])
        return new_fields.reshape(2, Z, X, C), new_planes.reshape(2, 2, Z, 4, C)

    placed = (
        P(None, None, "gx", "gy"),
        P("gx", "gy"),
        P(None, "gx", "gy"),
        P(None, None, None, "gx", "gy"),
    )
    return jax.shard_map(
        shards,
        mesh=mesh,
        in_specs=placed,
        out_specs=(P(None, None, "gx", "gy"), P(None, None, None, "gx", "gy")),
        check_vma=False,
    )
```

```python
import functools

import jax
import jax.numpy as jnp
from jax import lax
from jax.experimental import pallas as pl
from jax.experimental.pallas import tpu as pltpu
from jax.sharding import PartitionSpec as P

MESH = pl.DeviceIdType.MESH
cond_oil = 0.6
cond_drop = 2.0
diff_oil = 0.3
diff_drop = 1.0
thermal_slope = 0.3
cheb_radius = 0.95
cheb_ratio = 1.0 / cheb_radius
rho_first = 1.0 / cheb_ratio
rho_second = 1.0 / (2.0 * cheb_ratio - rho_first)
log2_e = 1.4426950408889634
keep_old = rho_second * rho_first
take_new = 2.0 * rho_second / cheb_radius

Z = 16
X = 16
C = 128
PITCH = 17
CORNERS = ((-1, -1), (-1, 1), (1, -1), (1, 1))
SIDES_Y = ((0, -1), (0, 1))
SIDES_X = ((-1, 0), (1, 0))
ALL = CORNERS + SIDES_Y + SIDES_X


def lanes(shape):
    return lax.broadcasted_iota(jnp.int32, shape, len(shape) - 1)


def roll_last(v, shift):
    return pltpu.roll(v, shift % C, v.ndim - 1)


def roll_rows(v, shift):
    return pltpu.roll(v, shift % 8, v.ndim - 2)


def rows_of(ref, index, start, step):
    at = lambda first: ref[(*index, pl.ds(first, 8, stride=step), slice(None))]
    return jnp.stack([at(start), at(start + step // 2)], axis=0)


def next_of(v, axis, turn):
    even, odd = lax.slice_in_dim(v, 0, 1, axis=axis), lax.slice_in_dim(v, 1, 2, axis=axis)
    return jnp.concatenate([odd, turn(even)], axis=axis)


def previous_of(v, axis, turn):
    even, odd = lax.slice_in_dim(v, 0, 1, axis=axis), lax.slice_in_dim(v, 1, 2, axis=axis)
    return jnp.concatenate([turn(odd), even], axis=axis)


def faces_of(k, axis, forth, back, last, first):
    even, odd = lax.slice_in_dim(k, 0, 1, axis=axis), lax.slice_in_dim(k, 1, 2, axis=axis)
    inner = even + odd
    up = jnp.where(last, 0.0, odd + forth(even))
    down = jnp.where(first, 0.0, even + back(odd))
    return jnp.concatenate([inner, up], axis=axis), jnp.concatenate([down, inner], axis=axis)


def packed_columns(v):
    head = v.shape[:-3]
    v = v.reshape(head + (8, 2, X, C))
    lane = lanes(head + (2, X, C))
    out = None
    for j in range(8):
        moved = roll_last(v[..., j, :, :, :], 16 * j + 8)
        out = moved if out is None else jnp.where(lane >= 16 * j, moved, out)
    return out


def packed_map(v):
    base = jnp.where(lanes(v.shape) < 16, roll_last(v, 8), 0.0)
    base = base + roll_last(base, 16)
    base = base + roll_last(base, 32)
    return base + roll_last(base, 64)


def periodic_columns(v):
    base = jnp.where(lanes(v.shape) < 8, roll_last(v, 4), 0.0)
    for shift in (8, 16, 32, 64):
        base = base + roll_last(base, shift)
    return base


def edge_columns(v):
    lane = lanes(v.shape[:-3] + (X, C))
    out = None
    for z in range(Z):
        moved = roll_last(v[..., z, :, :], 8 * z + 4)
        out = moved if out is None else jnp.where(lane >= 8 * z, moved, out)
    return out


def inverse(v):
    guess = pl.reciprocal(v, approx=True)
    return guess * (2.0 - v * guess)


def steps_of(droplet, active, old_t, old_n, decay, grid):
    def sweep(v, target, faces):
        px, mx, py, my, z_part = faces
        along = px * grid.xp(v) + mx * grid.xm(v)
        across = py * grid.yp(v) + my * grid.ym(v)
        return (target + along) + (across + z_part(v))

    def sides(k):
        return (*grid.x_faces(k), *grid.y_faces(k))

    def coefficients(k):
        px, mx, py, my = sides(k)
        z_part, z_total = grid.layers(k)
        robin = k * grid.edge4
        diagonal = (1.0 + robin) + (px + mx) + (py + my) + z_total
        return (px, mx, py, my, z_part), robin, inverse(diagonal)

    def heat_coefficients(k):
        px, mx, py, my = sides(k)
        robin = k * grid.edge4
        diagonal = (1.0 + robin) + (px + mx) + (py + my)
        z_part, inv = grid.even_layers(k, diagonal)
        return (px, mx, py, my, z_part), robin, inv

    ion_base = diff_oil + (diff_drop - diff_oil) * droplet
    heat_faces, heat_robin, heat_inv = heat_coefficients(cond_oil + (cond_drop - cond_oil) * droplet)
    heating = [(0.5 * (e * droplet)) * decay for e in active]

    def open_step(step, old_t, old_n):
        ions = ion_base * jnp.exp2((thermal_slope * log2_e) * old_t)
        target_t = old_t + heating[step] * (2.0 + old_n * old_n)
        ion_faces, ion_robin, ion_inv = coefficients(ions)
        if step == 0:
            yield
        return (
            (old_t, target_t, sweep(old_t, target_t, heat_faces), heat_faces, heat_robin, heat_inv),
            (old_n, old_n, sweep(old_n, old_n, ion_faces), ion_faces, ion_robin, ion_inv),
        )

    def close_field(parts, step, field, trace):
        old, target, total, faces, robin, inv = parts[field]
        given = robin * trace(step, field)
        first = (total + given) * inv
        return sweep(first, target + given, faces) * (take_new * inv) - keep_old * old

    yield
    parts = yield from open_step(0, old_t, old_n)
    trace = yield
    early = [close_field(parts, 0, field, trace) for field in range(2)]
    yield early
    parts = yield from open_step(1, *early)
    for field in range(2):
        yield close_field(parts, 1, field, trace)


class Span:
    def __init__(self, values, start):
        self.values, self.start = values, start

    def __call__(self, lo, hi):
        return self.values[lo - self.start : hi - self.start]


def gathered(function, lo, hi, size=4):
    return Span(jnp.concatenate([function(a, min(a + size, hi)) for a in range(lo, hi, size)], axis=0), lo)


def joined(*spans):
    return Span(jnp.concatenate([span.values for span in spans], axis=0), spans[0].start)


def x_sum(face, v, lo, hi):
    top, low = min(hi, X - 1), max(lo - 1, 0)
    up = face(lo, top)
    down = face(low, hi - 1)
    if v is not None:
        up = up * v(lo + 1, top + 1)
        down = down * v(low, hi - 1)
    first, last = max(lo, 1), top
    parts = [up[:1]] if lo == 0 else []
    if last > first:
        parts.append(up[first - lo : last - lo] + down[first - low - 1 : last - low - 1])
    if hi == X:
        parts.append(down[-1:])
    return jnp.concatenate(parts, axis=0)


class OwnColumns:
    def __init__(self, droplet, active, temper, ions, decay):
        self.olds = [[Span(temper, 0), Span(ions, 0)]]
        both = lambda v: jnp.concatenate([v, v], axis=1)
        heat = cond_oil + (cond_drop - cond_oil) * droplet
        self.ion_base = both(diff_oil + (diff_drop - diff_oil) * droplet)
        self.heating = [Span(both(0.5 * (e * droplet)) * decay, 0) for e in active]
        face = Span(heat[1:] + heat[:-1], 0)
        py = heat + roll_last(heat, -1)
        my = roll_last(py, 1)
        edge = jnp.concatenate([heat[:1], jnp.zeros_like(heat[1:-1]), heat[-1:]], axis=0)
        base = (1.0 + 4.0 * edge) + x_sum(face, None, 0, X) + (py + my)
        row = lax.broadcasted_iota(jnp.int32, (1, 1, 8, 1), 2)
        self.high, self.low = row == 7, row == 0
        pz = jnp.concatenate([2.0 * heat, jnp.where(self.high, 0.0, 2.0 * heat)], axis=1)
        mz = jnp.concatenate([jnp.where(self.low, 0.0, 2.0 * heat), 2.0 * heat], axis=1)
        heat_faces = (Span(both(face.values), 0), Span(both(py), 0), Span(both(my), 0), Span(pz, 0), Span(mz, 0))
        self.heat = (heat_faces, Span(inverse(both(base) + (pz + mz)), 0), Span(both(heat), 0))
        self.states = []

    def ion_parts(self, temper, lo, hi):
        k = self.ion_base[lo:hi] * jnp.exp2((thermal_slope * log2_e) * temper(lo, hi))
        pz, mz = faces_of(k, 1, lambda u: roll_rows(u, -1), lambda u: roll_rows(u, 1), self.high, self.low)
        return k, k + roll_last(k, -1), k + roll_last(k, 1), pz, mz

    def ion_spans(self, temper, lo, hi):
        parts = [self.ion_parts(temper, a, min(a + 4, hi)) for a in range(lo, hi, 4)]
        return [Span(jnp.concatenate(p, axis=0), lo) for p in zip(*parts)]

    def ion_inverse(self, spans, face, lo, hi):
        def part(a, b):
            k, py, my, pz, mz = [v(a, b) for v in spans]
            total = (1.0 + x_sum(face, None, a, b)) + (py + my) + (pz + mz)
            if a == 0:
                total = jnp.concatenate([total[:1] + 4.0 * k[:1], total[1:]], axis=0)
            if b == X:
                total = jnp.concatenate([total[:-1], total[-1:] + 4.0 * k[-1:]], axis=0)
            return inverse(total)

        return gathered(part, lo, hi)

    def sweep(self, v, target, faces, a, b):
        face, py, my, pz, mz = faces
        mid = v(a, b)
        across = py(a, b) * roll_last(mid, -1) + my(a, b) * roll_last(mid, 1)
        above = next_of(mid, 1, lambda u: roll_rows(u, -1))
        below = previous_of(mid, 1, lambda u: roll_rows(u, 1))
        upright = pz(a, b) * above + mz(a, b) * below
        return (target(a, b) + x_sum(face, v, a, b)) + (across + upright)

    def targets(self, step, old, lo, hi):
        heated = lambda a, b: old[0](a, b) + self.heating[step](a, b) * (2.0 + old[1](a, b) * old[1](a, b))
        return [gathered(heated, lo, hi), Span(old[1](lo, hi), lo)]

    def last(self, old, target, first, faces, inv, lo, hi):
        def part(a, b):
            return self.sweep(first, target, faces, a, b) * (take_new * inv(a, b)) - keep_old * old(a, b)

        return gathered(part, lo, hi)

    def before(self):
        old = self.olds[0]
        spans = self.ion_spans(old[0], 0, X)
        face = Span(spans[0].values[1:] + spans[0].values[:-1], 0)
        ion = ((face, *spans[1:]), self.ion_inverse(spans, face, 0, X), spans[0])
        self.sets0 = (self.heat, ion)
        self.target0 = self.targets(0, old, 0, X)
        self.total0, self.first0, self.mid1 = [], [], []
        for f in range(2):
            faces, inv, k = self.sets0[f]
            total = gathered(lambda a, b: self.sweep(old[f], self.target0[f], faces, a, b), 0, X)
            first = gathered(lambda a, b: total(a, b) * inv(a, b), 1, X - 1)
            self.total0.append(total)
            self.first0.append(first)
            self.mid1.append(self.last(old[f], self.target0[f], first, faces, inv, 2, X - 2))
        new = self.mid1
        self.spans1 = self.ion_spans(new[0], 2, X - 2)
        k = self.spans1[0]
        self.face1 = Span(k.values[1:] + k.values[:-1], 2)
        self.inv1 = self.ion_inverse(self.spans1, self.face1, 3, X - 3)
        self.target1 = self.targets(1, new, 2, X - 2)
        sets = ((self.heat[0], self.heat[1]), ((self.face1, *self.spans1[1:]), self.inv1))
        self.first1, self.mid2 = [], []
        for f in range(2):
            faces, inv = sets[f]
            first = gathered(lambda a, b: self.sweep(new[f], self.target1[f], faces, a, b) * inv(a, b), 3, X - 3)
            self.first1.append(first)
            self.mid2.append(self.last(new[f], self.target1[f], first, faces, inv, 4, X - 4))

    def after(self, trace):
        old = self.olds[0]
        news = []
        for f in range(2):
            faces, inv, k = self.sets0[f]
            ends, target = [], self.target0[f].values
            for side, x in ((0, 0), (1, X - 1)):
                given = 4.0 * k(x, x + 1) * trace(0, f, side)
                ends.append((self.total0[f](x, x + 1) + given) * inv(x, x + 1))
                target = (
                    jnp.concatenate([target[:1] + given, target[1:]], axis=0)
                    if side == 0
                    else jnp.concatenate([target[:-1], target[-1:] + given], axis=0)
                )
            first = Span(jnp.concatenate([ends[0], self.first0[f].values, ends[1]], axis=0), 0)
            target = Span(target, 0)
            low = self.last(old[f], target, first, faces, inv, 0, 2)
            high = self.last(old[f], target, first, faces, inv, X - 2, X)
            news.append(joined(low, self.mid1[f], high))
            yield
        low, high = self.ion_spans(news[0], 0, 2), self.ion_spans(news[0], X - 2, X)
        spans = [joined(a, b, c) for a, b, c in zip(low, self.spans1, high)]
        k = spans[0].values
        face = Span(
            jnp.concatenate([k[1:3] + k[0:2], self.face1.values, k[X - 2 :] + k[X - 3 : X - 1]], axis=0), 0
        )
        inv = joined(self.ion_inverse(spans, face, 0, 3), self.inv1, self.ion_inverse(spans, face, X - 3, X))
        yield
        low, high = self.targets(1, news, 0, 2), self.targets(1, news, X - 2, X)
        ends = []
        for f, (faces, inv, k) in enumerate((self.heat, ((face, *spans[1:]), inv, spans[0]))):
            target = joined(low[f], self.target1[f], high[f]).values
            target = Span(
                jnp.concatenate(
                    [
                        target[:1] + 4.0 * k(0, 1) * trace(1, f, 0),
                        target[1:-1],
                        target[-1:] + 4.0 * k(X - 1, X) * trace(1, f, 1),
                    ],
                    axis=0,
                ),
                0,
            )
            part = lambda a, b: self.sweep(news[f], target, faces, a, b) * inv(a, b)
            first = joined(gathered(part, 0, 3), self.first1[f], gathered(part, X - 3, X))
            ends.append(
                joined(
                    self.last(news[f], target, first, faces, inv, 0, 4),
                    self.mid2[f],
                    self.last(news[f], target, first, faces, inv, X - 4, X),
                )
            )
            yield
        self.states = news, ends


class Strips:
    def __init__(self, left_open, right_open):
        self.lane = lanes((1, 1, 1, 1, C))
        self.column = self.lane % 16
        row = lax.broadcasted_iota(jnp.int32, (1, 1, 1, 8, 1), 3)
        half_x = lax.broadcasted_iota(jnp.int32, (1, 1, 2, 1, 1), 2)
        half_z = lax.broadcasted_iota(jnp.int32, (1, 2, 1, 1, 1), 1)
        side = lax.broadcasted_iota(jnp.int32, (2, 1, 1, 1, 1), 0)
        self.low, self.high = row == 0, row == 7
        self.floor, self.top = self.lane < 16, self.lane >= 112
        self.edge4 = jnp.where(2 * row + half_x == 0, 4.0, 0.0) + jnp.where(2 * row + half_x == X - 1, 4.0, 0.0)
        opened = jnp.where(side == 0, left_open, right_open)
        self.between_up = jnp.where(self.column == 7, opened, 1.0)
        self.between_down = jnp.where(self.column == 8, opened, 1.0)
        self.decay = jnp.exp(-4.0 * (2 * (self.lane // 16) + half_z).astype(jnp.float32) / Z)

    def xp(self, v):
        return next_of(v, 2, lambda u: roll_rows(u, -1))

    def xm(self, v):
        return previous_of(v, 2, lambda u: roll_rows(u, 1))

    def yp(self, v):
        return roll_last(v, -1)

    def ym(self, v):
        return roll_last(v, 1)

    def zp(self, v):
        return next_of(v, 1, lambda u: roll_last(u, -16))

    def zm(self, v):
        return previous_of(v, 1, lambda u: roll_last(u, 16))

    def x_faces(self, k):
        return faces_of(k, 2, lambda u: roll_rows(u, -1), lambda u: roll_rows(u, 1), self.high, self.low)

    def y_faces(self, k):
        return (k + self.yp(k)) * self.between_up, (k + self.ym(k)) * self.between_down

    def layers(self, k):
        up, down = faces_of(k, 1, lambda u: roll_last(u, -16), lambda u: roll_last(u, 16), self.top, self.floor)
        return lambda v: up * self.zp(v) + down * self.zm(v), up + down

    def even_layers(self, k, diagonal):
        twice = 2.0 * k
        up = jnp.concatenate([twice, jnp.where(self.top, 0.0, twice)], axis=1)
        down = jnp.concatenate([jnp.where(self.floor, 0.0, twice), twice], axis=1)
        return lambda v: up * self.zp(v) + down * self.zm(v), inverse(diagonal + (up + down))


def kernel(
    n_gx,
    n_gy,
    f_hbm,
    ph_hbm,
    el_hbm,
    pl_hbm,
    of_ref,
    op_ref,
    f_in,
    f_32,
    ph_in,
    el_in,
    pl_in,
    own_b,
    send_b,
    send_g,
    recv_b,
    recv_g,
    recv_c,
    merge_ref,
    late_ref,
    send_sem,
    recv_sem,
):
    gx = lax.axis_index("gx")
    gy = lax.axis_index("gy")

    def exists(offset):
        found = []
        for place, move, count in ((gx, offset[0], n_gx), (gy, offset[1], n_gy)):
            if move < 0:
                found.append(place > 0)
            if move > 0:
                found.append(place < count - 1)
        return functools.reduce(jnp.logical_and, found)

    def at(offset):
        return (gx + offset[0], gy + offset[1])

    barrier = pltpu.get_barrier_semaphore()
    expected = jnp.int32(0)
    for offset in SIDES_Y + CORNERS + SIDES_X:

        @pl.when(exists(offset))
        def _(offset=offset):
            pl.semaphore_signal(barrier, inc=1, device_id=at(offset), device_id_type=MESH)

        expected = expected + exists(offset).astype(jnp.int32)

    loads = [
        pltpu.make_async_copy(src, dst, send_sem.at[i])
        for i, (src, dst) in enumerate(((ph_hbm, ph_in), (el_hbm, el_in), (f_hbm, f_in), (pl_hbm, pl_in)))
    ]
    for load in loads:
        load.start()

    for i, offset in enumerate(SIDES_Y):

        @pl.when(jnp.logical_not(exists(offset)))
        def _(i=i):
            recv_b[i] = jnp.zeros(recv_b.shape[1:], jnp.float32)

    for i, offset in enumerate(SIDES_X):

        @pl.when(jnp.logical_not(exists(offset)))
        def _(i=i):
            recv_g[i] = jnp.zeros(recv_g.shape[1:], jnp.float32)

    for i, offset in enumerate(CORNERS):

        @pl.when(jnp.logical_not(exists(offset)))
        def _(i=i):
            recv_c[i] = jnp.zeros(recv_c.shape[1:], jnp.float32)

    for load in loads:
        load.wait()
    maps = [ph_in[...].astype(jnp.float32), el_in[0].astype(jnp.float32), el_in[1].astype(jnp.float32)]
    drop, on0, on1 = [periodic_columns(m) for m in maps]
    near = edge_columns(f_in[...].astype(jnp.float32))
    place = lanes((X, C)) % 8
    send_b[0, 0] = jnp.where(place >= 4, near[0], roll_last(drop, -4))
    send_b[0, 1] = jnp.where(place >= 4, near[1], jnp.where(place == 0, roll_last(on1, -4), roll_last(on0, -3)))
    send_b[1, 0] = jnp.where(place < 4, near[0], roll_last(drop, 4))
    send_b[1, 1] = jnp.where(place < 4, near[1], jnp.where(place == 7, roll_last(on1, 4), roll_last(on0, 3)))
    own_row = lax.broadcasted_iota(jnp.int32, (8, C), 0) == lanes((8, C)) // 16
    for side in range(2):
        near, far = ((0, 1), (3, 2))[side]
        for s in range(2):
            for f in range(2):
                first = (s * 2 + f) * Z
                a = pl_in[pl.ds(4 * first + near, Z, stride=4), :]
                b = pl_in[pl.ds(4 * first + far, Z, stride=4), :]
                send_g[side, first : first + Z, :] = a + 0.5 * (a - b)
    for side in range(2):
        for row in range(4):
            halves = rows_of(send_g, (side,), row * Z, 2)
            for h in range(2):
                spread = pltpu.roll(halves[h], 8, 1, stride=16, stride_axis=0)
                spread = jnp.sum(jnp.where(own_row, spread, 0.0), axis=0, keepdims=True)
                send_g[side, 64 + 2 * row + h : 65 + 2 * row + h, :] = spread

    pl.semaphore_wait(barrier, expected)

    def copy_of(i, offset):
        back = (-offset[0], -offset[1])
        if offset in CORNERS:
            src = send_g.at[(offset[0] + 1) // 2, pl.ds(64, 8)]
            dst = recv_c.at[CORNERS.index(back)]
        elif offset in SIDES_Y:
            src = send_b.at[(offset[1] + 1) // 2]
            dst = recv_b.at[SIDES_Y.index(back)]
        else:
            src = send_g.at[(offset[0] + 1) // 2]
            dst = recv_g.at[SIDES_X.index(back)]
        return pltpu.make_async_remote_copy(
            src_ref=src,
            dst_ref=dst,
            send_sem=send_sem.at[i],
            recv_sem=recv_sem.at[ALL.index(back)],
            device_id=at(offset),
            device_id_type=MESH,
        )

    for i, offset in enumerate(ALL):

        @pl.when(exists(offset))
        def _(i=i, offset=offset):
            copy_of(i, offset).start()

    for i in range(3):
        own_b[4 + i] = packed_map(maps[i])
    own_b[0:4] = packed_columns(f_in[...].astype(jnp.float32)).reshape(4, X, C)

    def wait_from(offset):
        back = (-offset[0], -offset[1])

        @pl.when(exists(offset))
        def _():
            copy_of(ALL.index(back), back).wait_recv()

    for f in range(2):
        layers = f_in[f].astype(jnp.float32)
        for z in range(Z):
            f_32[f, PITCH * z : PITCH * z + X, :] = layers[z]
    planes_x = lambda f: jnp.stack([rows_of(f_32, (f,), x, 2 * PITCH) for x in range(X)], axis=0)
    rows = lambda v: jnp.broadcast_to(v[:, None, None, :], (X, 1, 8, C))
    half = lax.broadcasted_iota(jnp.int32, (1, 2, 1, 1), 1)
    height = 2 * lax.broadcasted_iota(jnp.int32, (1, 1, 8, C), 2) + half
    decay = jnp.exp(-4.0 * height.astype(jnp.float32) / Z)
    columns = OwnColumns(rows(maps[0]), [rows(maps[1]), rows(maps[2])], planes_x(0), planes_x(1), decay)
    columns.before()
    for offset in SIDES_X + SIDES_Y:
        wait_from(offset)

    def trace_own(step, field, side):
        return rows_of(recv_g, (side,), (step * 2 + field) * Z, 2)[None]

    rest = columns.after(trace_own)
    next(rest)
    grid = Strips((gy > 0).astype(jnp.float32), (gy < n_gy - 1).astype(jnp.float32))
    inner = grid.column[0] < 8

    def strip(outer, own):
        return jnp.stack([jnp.where(inner, outer[0], own), jnp.where(inner, own, outer[1])], axis=0)

    def halo(side, field):
        v = rows_of(recv_b, (side, field), 0, 2)
        return jnp.stack([roll_last(v, 4), roll_last(v, -4)], axis=0)

    def own_strip(i):
        return rows_of(own_b, (i,), 0, 2)

    def map_strip(field, own, turns):
        outer = [roll_last(rows_of(recv_b, (side, field), 0, 2), turns[side])[None] for side in range(2)]
        return strip(outer, own_strip(own)[None])

    def trace_strip(step, field):
        row = (step * 2 + field) * 2
        halves = []
        for i in range(2):
            mid = recv_g[i, 64 + row : 66 + row, :]
            low = jnp.where(inner[0, 0], recv_c[2 * i, row : row + 2, :], mid)
            high = jnp.where(inner[0, 0], mid, recv_c[2 * i + 1, row : row + 2, :])
            halves.append(jnp.broadcast_to(jnp.stack([low, high], axis=0)[:, :, None, :], (2, 2, 8, C)))
        return jnp.stack(halves, axis=2)

    next(rest)
    fields = [
        strip([halo(side, f) for side in range(2)], jnp.stack([own_strip(2 * f), own_strip(2 * f + 1)], axis=0))
        for f in range(2)
    ]
    drop = map_strip(0, 4, (0, 0))
    on0 = map_strip(1, 5, (1, -1))
    on1 = map_strip(1, 6, (0, 0))
    work = steps_of(
        drop,
        [on0, on1],
        fields[0],
        fields[1],
        grid.decay,
        grid,
    )
    for _ in rest:
        next(work)
    early, late = columns.states
    for f in range(2):
        for h in range(2):
            for x in range(X):
                late_ref[f, pl.ds(PITCH * x + h, 8, stride=2), :] = late[f].values[x, h]
            for p, x in enumerate((0, 1, X - 2, X - 1)):
                op_ref[0, f, pl.ds(p + 4 * h, 8, stride=8), :] = early[f].values[x, h]
    for i, offset in enumerate(ALL):

        @pl.when(exists(offset))
        def _(i=i, offset=offset):
            copy_of(i, offset).wait_send()

    for offset in CORNERS:
        wait_from(offset)
    lane = lanes((X, C))
    edge = (lane < 4) | (lane >= C - 4)

    def both_sides(state):
        return jnp.where(inner, state[1], state[0])

    def merge(field, state):
        state = both_sides(state)
        for h in range(2):
            for i in range(2):
                merge_ref[field, h, pl.ds(i, 8, stride=2), :] = state[h, i]
        for h in range(2):
            state = merge_ref[field, h]
            for j in range(8):
                z = 2 * j + h
                rows = slice(X * z, X * z + X)
                own = late_ref[field, pl.ds(z, X, stride=PITCH), :]
                value = jnp.where(edge, roll_last(state, -(16 * j + 8)), own)
                of_ref[field, rows, :] = value
                op_ref[1, field, 4 * z : 4 * z + 4, :] = jnp.concatenate([value[0:2], value[X - 2 :]], axis=0)

    four = []
    for state in work.send(trace_strip):
        state = both_sides(state)
        four += [state[:, 0, 0:1], state[:, 1, 0:1], state[:, 0, 7:8], state[:, 1, 7:8]]
    four = jnp.concatenate(four, axis=1)
    temper = next(work)
    for j in range(8):
        back = roll_last(four, -(16 * j + 8))
        for h in range(2):
            for f in range(2):
                rows = slice(4 * (2 * j + h), 4 * (2 * j + h) + 4)
                op_ref[0, f, rows, :] = jnp.where(edge[:4], back[h, 4 * f : 4 * f + 4], op_ref[0, f, rows, :])
    merge(0, temper)
    merge(1, next(work))


def write_out(f_ref, p_ref, of_hbm, op_hbm, sem):
    copies = [
        pltpu.make_async_copy(f_ref, of_hbm, sem.at[0]),
        pltpu.make_async_copy(p_ref, op_hbm, sem.at[1]),
    ]
    for copy in copies:
        copy.start()
    for copy in copies:
        copy.wait()


def solution(mesh):
    n_gx = mesh.shape["gx"]
    n_gy = mesh.shape["gy"]

    def shards(fields, phase, electrode, planes):
        in_hbm = pl.BlockSpec(memory_space=pltpu.HBM)
        vmem = pl.BlockSpec(memory_space=pltpu.VMEM)
        made = pl.pallas_call(
            functools.partial(kernel, n_gx, n_gy),
            out_shape=(
                jax.ShapeDtypeStruct((2, Z * X, C), jnp.float32),
                jax.ShapeDtypeStruct((2, 2, Z * 4, C), jnp.float32),
            ),
            in_specs=[in_hbm] * 4,
            out_specs=(vmem, vmem),
            scratch_shapes=[
                pltpu.VMEM((2, Z, X, C), jnp.bfloat16),
                pltpu.VMEM((2, Z * PITCH, C), jnp.float32),
                pltpu.VMEM((X, C), jnp.int32),
                pltpu.VMEM((2, X, C), jnp.int32),
                pltpu.VMEM((2 * 2 * Z * 4, C), jnp.float32),
                pltpu.VMEM((7, X, C), jnp.float32),
                pltpu.VMEM((2, 2, X, C), jnp.float32),
                pltpu.VMEM((2, 72, C), jnp.float32),
                pltpu.VMEM((2, 2, X, C), jnp.float32),
                pltpu.VMEM((2, 72, C), jnp.float32),
                pltpu.VMEM((4, 8, C), jnp.float32),
                pltpu.VMEM((2, 2, X, C), jnp.float32),
                pltpu.VMEM((2, PITCH * X, C), jnp.float32),
                pltpu.SemaphoreType.DMA((8,)),
                pltpu.SemaphoreType.DMA((8,)),
            ],
            compiler_params=pltpu.CompilerParams(
                collective_id=0, has_side_effects=True, vmem_limit_bytes=32 * 1024 * 1024
            ),
        )(*[pltpu.with_memory_space_constraint(v, pltpu.HBM) for v in (fields, phase, electrode, planes.reshape(2 * 2 * Z * 4, C))])
        new_fields, new_planes = pl.pallas_call(
            write_out,
            out_shape=(
                pltpu.HBM((2, Z * X, C), jnp.float32),
                pltpu.HBM((2, 2, Z * 4, C), jnp.float32),
            ),
            in_specs=[vmem, vmem],
            out_specs=(in_hbm, in_hbm),
            scratch_shapes=[pltpu.SemaphoreType.DMA((2,))],
        )(*[pltpu.with_memory_space_constraint(v, pltpu.VMEM) for v in made])
        return new_fields.reshape(2, Z, X, C), new_planes.reshape(2, 2, Z, 4, C)

    placed = (
        P(None, None, "gx", "gy"),
        P("gx", "gy"),
        P(None, "gx", "gy"),
        P(None, None, None, "gx", "gy"),
    )
    return jax.shard_map(
        shards,
        mesh=mesh,
        in_specs=placed,
        out_specs=(P(None, None, "gx", "gy"), P(None, None, None, "gx", "gy")),
        check_vma=False,
    )
```
